32 devices in a mesh: pix: 16 (over z, y, x), mode: 2 (over core).
Axes of the slice: x: 2, y: 2, z: 4, core: 2. Of those that a mesh axis runs over, the one named last changes fastest.
Arguments:
- frames: bfloat16 [4, 8192, 2048], P(None, 'pix', 'mode'), may hold values from 0 to 4
- ref_pixels: int32 [64], replicated, may hold values from 0 to 8191
Outputs:
- gram_band: float32 [2, 2048, 1024], P(None, 'mode', 'pix')
- gram_diag: float32 [2, 2048, 1024], P(None, 'mode', 'pix')
The draws below stay inside these ranges and needn't reach their ends.
Inputs may be any that keep to these rules, and one draw needn't show every extreme that they name: `ref_pixels`: indices of reference pixels; an index may appear more than once.
All inputs are finite; a program needn't handle non-finite values.
Results may differ from the reference program's by a relative error of at most 0.0088.
Values may be sent and summed in bfloat16 or wider, within the bound.
A program may use at most 128 MiB of HBM per device.

```python
import math
import jax
import jax.numpy as jnp
from jax import lax

MODES = 2048
NREF = 64
PIXELS = 8192
N_MODE = 2


def plant(values, rng, least, largest):
    longest = values.shape.index(max(values.shape))
    spots = []
    for shift in (0, 1):
        where = [jax.random.randint(jax.random.fold_in(rng, axis), (), 0, length) for axis, length in enumerate(values.shape)]
        where[longest] = (where[longest] + shift) % values.shape[longest]
        spots.append(tuple(where))
    return values.at[spots[0]].set(least).at[spots[1]].set(largest)


def block_scale(stream_key, shape, shards, smallest, largest):
    gain, own = 1.0, jax.random.fold_in(stream_key, 6)
    for axis_at, parts in shards:
        heights = jnp.exp(jax.random.uniform(jax.random.fold_in(own, axis_at), (parts,), jnp.float32, smallest / len(shards), largest / len(shards)))
        gain = gain * jnp.repeat(heights, shape[axis_at] // parts).reshape([-1 if axis == axis_at else 1 for axis in range(len(shape))])
    return gain


def setup_inputs(seed: int = 0) -> dict:
    streams_of = jax.random.split(jax.random.key(seed), 3)
    frames = jnp.clip(4.0 * jax.random.uniform(streams_of[0], (4, PIXELS, MODES), jnp.float32) ** block_scale(streams_of[0], (4, PIXELS, MODES), ((1, 16), (2, 2)), -0.2, 0.2), 0.0, 4.0).astype(jnp.bfloat16)
    ref_pixels = plant(jax.random.randint(streams_of[1], (NREF,), 0, PIXELS), jax.random.fold_in(streams_of[1], 1), 0, PIXELS - 1).astype(jnp.int32)
    return dict(frames=frames, ref_pixels=ref_pixels)


def reference(frames, ref_pixels):
    frame_float = frames.astype(jnp.float32)
    real_part = (frame_float[0] - frame_float[2]).astype(jnp.bfloat16)
    imag_part = (frame_float[3] - frame_float[1]).astype(jnp.bfloat16)
    ref_real = lax.optimization_barrier(jnp.sum(jnp.take(real_part, ref_pixels, axis=0).astype(jnp.float32), axis=0))
    ref_imag = lax.optimization_barrier(jnp.sum(jnp.take(imag_part, ref_pixels, axis=0).astype(jnp.float32), axis=0))
    magnitude = jnp.maximum(jnp.sqrt(ref_real * ref_real + ref_imag * ref_imag), 1.0)
    phase_real = ref_real / magnitude
    phase_imag = ref_imag / magnitude
    stacked = jnp.concatenate([real_part, imag_part], axis=0)
    turned = jnp.concatenate([imag_part, -real_part], axis=0)
    block_width = MODES // N_MODE
    full_width = (N_MODE // 2 + 1) * block_width
    stacked_twice = jnp.concatenate([stacked, stacked], axis=1)
    turned_twice = jnp.concatenate([turned, turned], axis=1)
    twice_real = jnp.concatenate([phase_real, phase_real], axis=0)
    twice_imag = jnp.concatenate([phase_imag, phase_imag], axis=0)
    pixel_scale = 1.0 / math.sqrt(PIXELS)

    def one_block(block_index):
        offset = (block_index * block_width).astype(jnp.int32)
        row_fields = lax.dynamic_slice_in_dim(stacked, offset, block_width, 1)
        col_fields = lax.dynamic_slice_in_dim(stacked_twice, offset, full_width, 1)
        turned_cols = lax.dynamic_slice_in_dim(turned_twice, offset, full_width, 1)
        gram_real = jnp.dot(row_fields.T, col_fields, preferred_element_type=jnp.float32)
        gram_imag = jnp.dot(row_fields.T, turned_cols, preferred_element_type=jnp.float32)
        row_real = lax.dynamic_slice_in_dim(phase_real, offset, block_width, 0)[:, None]
        row_imag = lax.dynamic_slice_in_dim(phase_imag, offset, block_width, 0)[:, None]
        col_real = lax.dynamic_slice_in_dim(twice_real, offset, full_width, 0)[None, :]
        col_imag = lax.dynamic_slice_in_dim(twice_imag, offset, full_width, 0)[None, :]
        unit_real = row_real * col_real + row_imag * col_imag
        unit_imag = row_imag * col_real - row_real * col_imag
        return jnp.stack([(unit_real * gram_real - unit_imag * gram_imag) * pixel_scale, (unit_real * gram_imag + unit_imag * gram_real) * pixel_scale])
    full_tiles = lax.map(one_block, jnp.arange(N_MODE, dtype=jnp.int32))
    full_rows = jnp.transpose(full_tiles, (1, 0, 2, 3)).reshape(2, MODES, full_width)
    return (full_rows[:, :, block_width:], full_rows[:, :, :block_width])
```

```python
import math

import jax
import jax.numpy as jnp
from jax import lax
from jax.experimental import pallas as pl
from jax.experimental.pallas import tpu as pltpu
from jax.sharding import PartitionSpec as P


def unit_phase(sums):
    magnitude = jnp.maximum(jnp.sqrt(sums[0] * sums[0] + sums[1] * sums[1]), 1.0)
    return sums / magnitude[None, :]


def rotate(gram_real, gram_imag, phase_rows, phase_cols, pixel_scale):
    row_real = phase_rows[0][:, None]
    row_imag = phase_rows[1][:, None]
    col_real = phase_cols[0][None, :]
    col_imag = phase_cols[1][None, :]
    unit_real = row_real * col_real + row_imag * col_imag
    unit_imag = row_imag * col_real - row_real * col_imag
    return jnp.stack(
        [
            (unit_real * gram_real - unit_imag * gram_imag) * pixel_scale,
            (unit_real * gram_imag + unit_imag * gram_real) * pixel_scale,
        ]
    )


def shards(frames, ref_pixels):
    pix_count = lax.axis_size("pix")
    mode_count = lax.axis_size("mode")
    pix_index = lax.axis_index("pix")
    mode_index = lax.axis_index("mode")
    pixel_rows = frames.shape[1]
    block_width = frames.shape[2]
    full_tiles = mode_count // 2 + 1
    full_width = full_tiles * block_width
    frame_float = frames.astype(jnp.float32)
    real_part = (frame_float[0] - frame_float[2]).astype(jnp.bfloat16)
    imag_part = (frame_float[3] - frame_float[1]).astype(jnp.bfloat16)
    fields = jnp.stack([real_part, imag_part])
    positions = pix_index * pixel_rows + lax.iota(jnp.int32, pixel_rows)
    counts = jnp.sum(
        (ref_pixels[:, None] == positions[None, :]).astype(jnp.float32), axis=0
    ).astype(jnp.bfloat16)
    local_ref = jnp.einsum("p,cpm->cm", counts, fields, preferred_element_type=jnp.float32)
    own_ref = lax.psum(local_ref, "pix")
    phase_all = lax.all_gather(unit_phase(own_ref), "mode", axis=1, tiled=True)
    phase_own = lax.dynamic_slice_in_dim(phase_all, mode_index * block_width, block_width, 1)
    phase_twice = jnp.concatenate([phase_all, phase_all], axis=1)
    phase_full = lax.dynamic_slice_in_dim(phase_twice, mode_index * block_width, full_width, 1)
    whole_fields = lax.all_gather(fields, "mode", axis=2, tiled=True)
    tiled = whole_fields.reshape(2, pixel_rows, mode_count, block_width)
    picked = (mode_index + lax.iota(jnp.int32, full_tiles)) % mode_count
    band_fields = jnp.take(tiled, picked, axis=2).reshape(2, pixel_rows, full_width)
    contract = (((0,), (0,)), ((), ()))
    own_real = fields[0]
    own_imag = fields[1]
    band_real = band_fields[0]
    band_imag = band_fields[1]
    gram_real = lax.dot_general(
        own_real, band_real, contract, preferred_element_type=jnp.float32
    ) + lax.dot_general(own_imag, band_imag, contract, preferred_element_type=jnp.float32)
    gram_imag = lax.dot_general(
        own_real, band_imag, contract, preferred_element_type=jnp.float32
    ) - lax.dot_general(own_imag, band_real, contract, preferred_element_type=jnp.float32)
    pixel_scale = 1.0 / math.sqrt(pix_count * pixel_rows)
    raw_terms = jnp.stack([gram_real, gram_imag])
    raw_diag, raw_band = (
        lax.psum_scatter(raw_terms[:, :, :block_width], "pix", scatter_dimension=2, tiled=True),
        lax.psum_scatter(raw_terms[:, :, block_width:], "pix", scatter_dimension=2, tiled=True),
    )
    diag_slice = block_width // pix_count
    band_slice = (full_width - block_width) // pix_count
    diag_cols = lax.dynamic_slice_in_dim(phase_full, pix_index * diag_slice, diag_slice, 1)
    band_cols = lax.dynamic_slice_in_dim(
        phase_full, block_width + pix_index * band_slice, band_slice, 1
    )
    diag_out = rotate(raw_diag[0], raw_diag[1], phase_own, diag_cols, pixel_scale)
    band_out = rotate(raw_band[0], raw_band[1], phase_own, band_cols, pixel_scale)
    return (band_out, diag_out)


MESH = pl.DeviceIdType.MESH
GROUP = 64
NEAR = 9
FAR = 7


def gram_kernel(
    frames_ref, weight_ref, gram_ref, sums_ref,
    own, other, part, first_in, second_in, outer_in, inner_in, end_in,
    ref_out, ref_in, total, cross_out, cross_in, turn_out, turn_in,
    field_send, field_recv, first_send, first_recv, second_send, second_recv,
    line_send, outer_recv, inner_recv, end_recv, ref_send, ref_recv,
    cross_send, cross_recv, turn_send, turn_recv,
):
    pix = lax.axis_index("pix")
    mode = lax.axis_index("mode")
    x, y, z = pix % 2, (pix // 2) % 2, pix // 4
    upper = z >= 2
    is_end = (z == 0) | (z == 3)
    is_mid = (z == 1) | (z == 2)
    x_peer = pix + 1 - 2 * x
    y_peer = pix + 2 - 4 * y
    inner_peer = jnp.where(upper, pix - 4, pix + 4)
    outer_peer = jnp.where(upper, pix + 4, pix - 4)
    z_even_peer = pix + 4 - 8 * (z % 2)
    z_far_peer = pix + 8 - 16 * (z // 2)
    pixel_rows = frames_ref.shape[1]
    width = frames_ref.shape[2]
    rows = NEAR * GROUP
    half = rows // 2
    chunk = 4 * GROUP

    barrier = pltpu.get_barrier_semaphore()
    for step in range(1, 16):
        pl.semaphore_signal(
            barrier, inc=1, device_id=((pix + step) % 16, mode), device_id_type=MESH
        )
    pl.semaphore_signal(barrier, inc=1, device_id=(pix, 1 - mode), device_id_type=MESH)

    def send(src, dst, send_sem, recv_sem, to_pix, to_mode):
        copy = pltpu.make_async_remote_copy(
            src_ref=src, dst_ref=dst, send_sem=send_sem, recv_sem=recv_sem,
            device_id=(to_pix, to_mode), device_id_type=MESH,
        )
        return copy

    def chunk_z(k):
        return jnp.where(upper, k, 3 - k)

    def field_chunk(k, carry):
        at = pl.multiple_of(chunk_z(k) * chunk, chunk)
        cols = pl.ds(at, chunk)
        real = frames_ref[0, :, cols].astype(jnp.float32) - frames_ref[2, :, cols].astype(jnp.float32)
        imag = frames_ref[3, :, cols].astype(jnp.float32) - frames_ref[1, :, cols].astype(jnp.float32)
        own[cols, 0:pixel_rows] = real.astype(jnp.bfloat16).T
        own[cols, pixel_rows:2 * pixel_rows] = imag.astype(jnp.bfloat16).T
        return carry

    lax.fori_loop(0, 4, field_chunk, 0)
    own[pl.ds(width, 8 * GROUP), :] = own[pl.ds(0, 8 * GROUP), :]
    pl.semaphore_wait(barrier, 16)

    def field_copy(k):
        cols = pl.ds(pl.multiple_of(chunk_z(k) * chunk, chunk), chunk)
        return send(own.at[cols], other.at[cols], field_send.at[k], field_recv.at[k], pix, 1 - mode)

    field_copies = [field_copy(k) for k in range(4)]
    for copy in field_copies:
        copy.start()

    ref_peers = [x_peer, y_peer, z_even_peer, z_far_peer, pix]

    def ref_copy(step):
        return send(
            ref_out.at[step], ref_in.at[step], ref_send.at[step], ref_recv.at[step],
            ref_peers[step], mode if step < 4 else 1 - mode,
        )

    ref_copies = [ref_copy(step) for step in range(5)]

    def ref_next(step):
        ref_copies[step].wait_recv()
        ref_out[step + 1] = ref_out[step] + ref_in[step]
        ref_copies[step + 1].start()

    contract = (((1,), (1,)), ((), ()))

    def turned(block):
        return jnp.concatenate([block[:, pixel_rows:], -block[:, :pixel_rows]], axis=1)

    def multiply(k):
        zc = chunk_z(k)
        field_copies[k].wait_recv()

        def one(t, carry):
            yy = jnp.where(t % 2 == 0, 1 - y, y)
            xx = jnp.where(t < 2, 1 - x, x)
            owner = zc * 4 + yy * 2 + xx
            at = pl.multiple_of(owner * GROUP, GROUP)
            own_cols = own[pl.ds(at, GROUP), :]
            other_cols = other[pl.ds(at, GROUP), :]
            cols = jnp.concatenate(
                [own_cols, turned(own_cols), other_cols, turned(other_cols)], axis=0
            )
            left = own[pl.ds(at, rows), :]
            out = lax.dot_general(left, cols, contract, preferred_element_type=jnp.float32)
            part[owner] = out.astype(jnp.bfloat16)
            return carry

        lax.fori_loop(0, 4, one, 0)

    spans = [pl.ds(0, half), pl.ds(half, half)]

    def owner_of(k, yy, xx):
        return chunk_z(k) * 4 + yy * 2 + xx

    def first_copy(axis, k, j):
        if axis == 0:
            owner = owner_of(k, 1 - y if j == 0 else y, 1 - x)
        else:
            owner = owner_of(k, 1 - y, 1 - x if j == 0 else x)
        return send(
            part.at[owner, spans[axis]], first_in.at[axis, k, j],
            first_send.at[axis, k, j], first_recv.at[axis, k, j],
            x_peer if axis == 0 else y_peer, mode,
        )

    def second_owner(axis, k):
        return owner_of(k, 1 - y, x) if axis == 0 else owner_of(k, y, 1 - x)

    def second_copy(axis, k):
        return send(
            part.at[second_owner(axis, k), spans[axis]], second_in.at[axis, k],
            second_send.at[axis, k], second_recv.at[axis, k],
            y_peer if axis == 0 else x_peer, mode,
        )

    firsts = {(a, k, j): first_copy(a, k, j) for a in range(2) for k in range(4) for j in range(2)}
    seconds = {(a, k): second_copy(a, k) for a in range(2) for k in range(4)}

    def f32(value):
        return value.astype(jnp.float32)

    def begin(k):
        multiply(k)
        for j in range(2):
            for a in range(2):
                firsts[a, k, j].start()

    def forward(k):
        for a in range(2):
            firsts[a, k, 0].wait_recv()
            owner = second_owner(a, k)
            part[owner, spans[a]] = (
                f32(part[owner, spans[a]]) + f32(first_in[a, k, 0])
            ).astype(jnp.bfloat16)
            seconds[a, k].start()

    def line_copy(k, to):
        owner = owner_of(k, y, x)
        if to == "outer":
            dst, sem = outer_in.at[k], outer_recv.at[k]
        elif to == "inner":
            dst, sem = inner_in.at[k], inner_recv.at[k]
        else:
            dst, sem = end_in, end_recv
        return send(
            part.at[owner], dst, line_send.at[k], sem,
            outer_peer if to == "end" else inner_peer, mode,
        )

    def keep(k):
        owner = owner_of(k, y, x)
        for a in range(2):
            firsts[a, k, 1].wait_recv()
            seconds[a, k].wait_recv()
            value = (
                f32(part[owner, spans[a]]) + f32(first_in[a, k, 1]) + f32(second_in[a, k])
            )
            if k >= 2:
                @pl.when(is_mid if k == 2 else is_end)
                def _():
                    total[spans[a], :] = value
            part[owner, spans[a]] = value.astype(jnp.bfloat16)
        if k < 3:
            @pl.when(is_end)
            def _():
                line_copy(k, "outer").start()

    def pass_on(k):
        owner = owner_of(k, y, x)

        @pl.when(is_mid)
        def _():
            if k < 2:
                line_copy(k, "outer").wait_recv()
                arrived = outer_in[k]
            else:
                line_copy(0, "inner").wait_recv()
                arrived = inner_in[0]
            part[owner] = (f32(part[owner]) + f32(arrived)).astype(jnp.bfloat16)
            line_copy(k, "inner" if k < 2 else "end").start()

    begin(0)
    begin(1)
    ref_out[0] = lax.dot_general(
        weight_ref[...], own[pl.ds(0, width), :], contract, preferred_element_type=jnp.float32
    )[0:8]
    ref_copies[0].start()
    forward(0)
    begin(2)
    ref_next(0)
    forward(1)
    keep(0)
    begin(3)
    ref_next(1)
    forward(2)
    keep(1)
    pass_on(0)
    ref_next(2)
    forward(3)
    keep(2)
    pass_on(1)
    ref_next(3)
    keep(3)
    pass_on(3)

    @pl.when(is_mid)
    def _():
        line_copy(2, "outer").wait_recv()
        line_copy(1, "inner").wait_recv()
        total[...] = total[...] + f32(outer_in[2]) + f32(inner_in[1])

    @pl.when(is_end)
    def _():
        line_copy(3, "end").wait_recv()
        total[...] = total[...] + f32(end_in[...])

    cross_out[...] = total[GROUP:8 * GROUP, 128:256].astype(jnp.bfloat16)
    cross = send(cross_out, cross_in, cross_send, cross_recv, pix, 1 - mode)
    cross.start()

    lane = lax.broadcasted_iota(jnp.int32, (GROUP, 128), 1)
    low = lane < GROUP

    def group_rows(step):
        return pl.ds(pl.multiple_of(((pix + step) % 16) * GROUP, GROUP), GROUP)

    for d in range(NEAR):
        here = total[d * GROUP:(d + 1) * GROUP, 0:128]
        there = total[d * GROUP:(d + 1) * GROUP, 128:256]
        gram_ref[0, group_rows(d), :] = jnp.where(low, here, pltpu.roll(there, GROUP, 1))
        gram_ref[1, group_rows(d), :] = jnp.where(low, pltpu.roll(here, GROUP, 1), there)

    cross.wait_recv()
    turns = []
    for d in range(1, FAR + 1):
        stacked = jnp.concatenate(
            [
                total[d * GROUP:(d + 1) * GROUP, 0:128].astype(jnp.bfloat16),
                cross_in[(d - 1) * GROUP:d * GROUP, :],
            ],
            axis=0,
        )
        turn_out[d - 1] = stacked.T
        turn = send(
            turn_out.at[d - 1], turn_in.at[d - 1], turn_send.at[d - 1], turn_recv.at[d - 1],
            (pix + d) % 16, mode,
        )
        turn.start()
        turns.append(turn)
    ref_copies[4].wait_recv()
    sums_ref[0] = ref_out[4]
    sums_ref[1] = ref_in[4]
    for d in range(1, FAR + 1):
        turns[d - 1].wait_recv()
        arrived = f32(turn_in[d - 1])
        gram_ref[0, group_rows(16 - d), :] = arrived[0:GROUP]
        gram_ref[1, group_rows(16 - d), :] = -arrived[GROUP:]

    for copy in field_copies + ref_copies + list(firsts.values()) + list(seconds.values()):
        copy.wait_send()
    for copy in turns + [cross]:
        copy.wait_send()
    for k in range(3):
        @pl.when(is_end | (k < 2))
        def _():
            line_copy(k, "outer").wait_send()

    @pl.when(is_mid)
    def _():
        line_copy(3, "end").wait_send()


def paired_shards(frames, ref_pixels):
    pix_index = lax.axis_index("pix")
    pixel_rows = frames.shape[1]
    width = frames.shape[2]
    positions = pix_index * pixel_rows + lax.iota(jnp.int32, pixel_rows)
    counts = jnp.sum(
        (ref_pixels[:, None] == positions[None, :]).astype(jnp.float32), axis=0
    ).astype(jnp.bfloat16)
    weight = (
        jnp.zeros((16, 2 * pixel_rows), jnp.bfloat16)
        .at[0, :pixel_rows].set(counts)
        .at[1, pixel_rows:].set(counts)
    )
    rows = NEAR * GROUP
    half = rows // 2
    b16 = jnp.bfloat16
    dma = pltpu.SemaphoreType.DMA
    gram, sums = pl.pallas_call(
        gram_kernel,
        out_shape=(
            jax.ShapeDtypeStruct((2, width, 128), jnp.float32),
            jax.ShapeDtypeStruct((2, 8, width), jnp.float32),
        ),
        in_specs=[pl.BlockSpec(memory_space=pltpu.VMEM)] * 2,
        out_specs=(pl.BlockSpec(memory_space=pltpu.VMEM),) * 2,
        scratch_shapes=[
            pltpu.VMEM((width + 8 * GROUP, 2 * pixel_rows), b16),
            pltpu.VMEM((width, 2 * pixel_rows), b16),
            pltpu.VMEM((16, rows, 256), b16),
            pltpu.VMEM((2, 4, 2, half, 256), b16),
            pltpu.VMEM((2, 4, half, 256), b16),
            pltpu.VMEM((3, rows, 256), b16),
            pltpu.VMEM((2, rows, 256), b16),
            pltpu.VMEM((rows, 256), b16),
            pltpu.VMEM((5, 8, width), jnp.float32),
            pltpu.VMEM((5, 8, width), jnp.float32),
            pltpu.VMEM((rows, 256), jnp.float32),
            pltpu.VMEM((FAR * GROUP, 128), b16),
            pltpu.VMEM((FAR * GROUP, 128), b16),
            pltpu.VMEM((FAR, 128, 128), b16),
            pltpu.VMEM((FAR, 128, 128), b16),
            dma((4,)), dma((4,)),
            dma((2, 4, 2)), dma((2, 4, 2)),
            dma((2, 4)), dma((2, 4)),
            dma((4,)), dma((3,)), dma((2,)), dma,
            dma((5,)), dma((5,)),
            dma, dma,
            dma((FAR,)), dma((FAR,)),
        ],
        compiler_params=pltpu.CompilerParams(
            collective_id=0, has_side_effects=True, vmem_limit_bytes=48 * 1024 * 1024
        ),
    )(frames, weight)
    phase_own = unit_phase(sums[0, :2])
    phase_other = unit_phase(sums[1, :2])
    start = pix_index * GROUP
    cols = jnp.concatenate(
        [
            lax.dynamic_slice_in_dim(phase_own, start, GROUP, 1),
            lax.dynamic_slice_in_dim(phase_other, start, GROUP, 1),
        ],
        axis=1,
    )
    pixel_scale = 1.0 / math.sqrt(lax.axis_size("pix") * pixel_rows)
    turned = rotate(gram[0], gram[1], phase_own, cols, pixel_scale)
    return (turned[:, :, GROUP:], turned[:, :, :GROUP])


def solution(mesh):
    placed = (P(None, "pix", "mode"), P())
    paired = mesh.shape["pix"] == 16 and mesh.shape["mode"] == 2

    def body(frames, ref_pixels):
        if paired and frames.shape[2] == 16 * GROUP:
            return paired_shards(frames, ref_pixels)
        return shards(frames, ref_pixels)

    return jax.shard_map(
        body,
        mesh=mesh,
        in_specs=placed,
        out_specs=(P(None, "mode", "pix"), P(None, "mode", "pix")),
        check_vma=False,
    )
```

```python
import functools
import math

import jax
import jax.numpy as jnp
from jax import lax
from jax.experimental import pallas as pl
from jax.experimental.pallas import tpu as pltpu
from jax.sharding import PartitionSpec as P


def unit_phase(sums):
    magnitude = jnp.maximum(jnp.sqrt(sums[0] * sums[0] + sums[1] * sums[1]), 1.0)
    return sums / magnitude[None, :]


def rotate(gram_real, gram_imag, phase_rows, phase_cols, pixel_scale):
    row_real = phase_rows[0][:, None]
    row_imag = phase_rows[1][:, None]
    col_real = phase_cols[0][None, :]
    col_imag = phase_cols[1][None, :]
    unit_real = row_real * col_real + row_imag * col_imag
    unit_imag = row_imag * col_real - row_real * col_imag
    return jnp.stack(
        [
            (unit_real * gram_real - unit_imag * gram_imag) * pixel_scale,
            (unit_real * gram_imag + unit_imag * gram_real) * pixel_scale,
        ]
    )


def shards(frames, ref_pixels):
    pix_count = lax.axis_size("pix")
    mode_count = lax.axis_size("mode")
    pix_index = lax.axis_index("pix")
    mode_index = lax.axis_index("mode")
    pixel_rows = frames.shape[1]
    block_width = frames.shape[2]
    full_tiles = mode_count // 2 + 1
    full_width = full_tiles * block_width
    frame_float = frames.astype(jnp.float32)
    real_part = (frame_float[0] - frame_float[2]).astype(jnp.bfloat16)
    imag_part = (frame_float[3] - frame_float[1]).astype(jnp.bfloat16)
    fields = jnp.stack([real_part, imag_part])
    positions = pix_index * pixel_rows + lax.iota(jnp.int32, pixel_rows)
    counts = jnp.sum(
        (ref_pixels[:, None] == positions[None, :]).astype(jnp.float32), axis=0
    ).astype(jnp.bfloat16)
    local_ref = jnp.einsum("p,cpm->cm", counts, fields, preferred_element_type=jnp.float32)
    own_ref = lax.psum(local_ref, "pix")
    phase_all = lax.all_gather(unit_phase(own_ref), "mode", axis=1, tiled=True)
    phase_own = lax.dynamic_slice_in_dim(phase_all, mode_index * block_width, block_width, 1)
    phase_twice = jnp.concatenate([phase_all, phase_all], axis=1)
    phase_full = lax.dynamic_slice_in_dim(phase_twice, mode_index * block_width, full_width, 1)
    whole_fields = lax.all_gather(fields, "mode", axis=2, tiled=True)
    tiled = whole_fields.reshape(2, pixel_rows, mode_count, block_width)
    picked = (mode_index + lax.iota(jnp.int32, full_tiles)) % mode_count
    band_fields = jnp.take(tiled, picked, axis=2).reshape(2, pixel_rows, full_width)
    contract = (((0,), (0,)), ((), ()))
    own_real = fields[0]
    own_imag = fields[1]
    band_real = band_fields[0]
    band_imag = band_fields[1]
    gram_real = lax.dot_general(
        own_real, band_real, contract, preferred_element_type=jnp.float32
    ) + lax.dot_general(own_imag, band_imag, contract, preferred_element_type=jnp.float32)
    gram_imag = lax.dot_general(
        own_real, band_imag, contract, preferred_element_type=jnp.float32
    ) - lax.dot_general(own_imag, band_real, contract, preferred_element_type=jnp.float32)
    pixel_scale = 1.0 / math.sqrt(pix_count * pixel_rows)
    raw_terms = jnp.stack([gram_real, gram_imag])
    raw_diag, raw_band = (
        lax.psum_scatter(raw_terms[:, :, :block_width], "pix", scatter_dimension=2, tiled=True),
        lax.psum_scatter(raw_terms[:, :, block_width:], "pix", scatter_dimension=2, tiled=True),
    )
    diag_slice = block_width // pix_count
    band_slice = (full_width - block_width) // pix_count
    diag_cols = lax.dynamic_slice_in_dim(phase_full, pix_index * diag_slice, diag_slice, 1)
    band_cols = lax.dynamic_slice_in_dim(
        phase_full, block_width + pix_index * band_slice, band_slice, 1
    )
    diag_out = rotate(raw_diag[0], raw_diag[1], phase_own, diag_cols, pixel_scale)
    band_out = rotate(raw_band[0], raw_band[1], phase_own, band_cols, pixel_scale)
    return (band_out, diag_out)


MESH = pl.DeviceIdType.MESH
GROUP = 64
NEAR = 9
FAR = 7


def gram_kernel(
    frames_hbm, pixels_ref, gram_ref, sums_ref,
    frames_ref, own, other, part, first_in, second_in, outer_in, inner_in, end_in,
    ref_out, ref_in, total, cross_out, cross_in, turn_out, turn_in,
    frame_sem, field_send, field_recv, first_send, first_recv, second_send, second_recv,
    line_send, outer_recv, inner_recv, end_recv, ref_send, ref_recv,
    cross_send, cross_recv, turn_send, turn_recv,
):
    pix = lax.axis_index("pix")
    mode = lax.axis_index("mode")
    x, y, z = pix % 2, (pix // 2) % 2, pix // 4
    upper = z >= 2
    is_end = (z == 0) | (z == 3)
    is_mid = (z == 1) | (z == 2)
    x_peer = pix + 1 - 2 * x
    y_peer = pix + 2 - 4 * y
    inner_peer = jnp.where(upper, pix - 4, pix + 4)
    outer_peer = jnp.where(upper, pix + 4, pix - 4)
    z_even_peer = pix + 4 - 8 * (z % 2)
    z_far_peer = pix + 8 - 16 * (z // 2)
    pixel_rows = frames_hbm.shape[1]
    width = frames_hbm.shape[2]
    rows = NEAR * GROUP
    half = rows // 2
    chunk = 4 * GROUP

    def chunk_z(k):
        return jnp.where(upper, k, 3 - k)

    def chunk_modes(k):
        return pl.ds(pl.multiple_of(chunk_z(k) * chunk, chunk), chunk)

    loads = [
        pltpu.make_async_copy(
            frames_hbm.at[:, :, chunk_modes(k)], frames_ref.at[k], frame_sem.at[k]
        )
        for k in range(4)
    ]
    for load in loads:
        load.start()
    barrier = pltpu.get_barrier_semaphore()
    for step in range(1, 16):
        pl.semaphore_signal(
            barrier, inc=1, device_id=((pix + step) % 16, mode), device_id_type=MESH
        )
    pl.semaphore_signal(barrier, inc=1, device_id=(pix, 1 - mode), device_id_type=MESH)

    def send(src, dst, send_sem, recv_sem, to_pix, to_mode):
        copy = pltpu.make_async_remote_copy(
            src_ref=src, dst_ref=dst, send_sem=send_sem, recv_sem=recv_sem,
            device_id=(to_pix, to_mode), device_id_type=MESH,
        )
        return copy

    for k in range(4):
        loads[k].wait()
        frame = [frames_ref[k, step].astype(jnp.float32) for step in range(4)]
        modes = chunk_modes(k)
        own[modes, 0:pixel_rows] = (frame[0] - frame[2]).astype(jnp.bfloat16).T
        own[modes, pixel_rows:2 * pixel_rows] = (frame[3] - frame[1]).astype(jnp.bfloat16).T
    own[pl.ds(width, 8 * GROUP), :] = own[pl.ds(0, 8 * GROUP), :]
    pl.semaphore_wait(barrier, 16)

    def field_copy(k):
        modes = chunk_modes(k)
        return send(own.at[modes], other.at[modes], field_send.at[k], field_recv.at[k], pix, 1 - mode)

    field_copies = [field_copy(k) for k in range(4)]
    for copy in field_copies:
        copy.start()

    ref_peers = [x_peer, y_peer, z_even_peer, z_far_peer, pix]

    def ref_copy(step):
        return send(
            ref_out.at[step], ref_in.at[step], ref_send.at[step], ref_recv.at[step],
            ref_peers[step], mode if step < 4 else 1 - mode,
        )

    ref_copies = [ref_copy(step) for step in range(5)]

    def ref_next(step):
        ref_copies[step].wait_recv()
        ref_out[step + 1] = ref_out[step] + ref_in[step]
        ref_copies[step + 1].start()

    contract = (((1,), (1,)), ((), ()))

    def turned(block):
        return jnp.concatenate([block[:, pixel_rows:], -block[:, :pixel_rows]], axis=1)

    def multiply(k):
        zc = chunk_z(k)
        field_copies[k].wait_recv()

        def one(t, carry):
            yy = jnp.where(t % 2 == 0, 1 - y, y)
            xx = jnp.where(t < 2, 1 - x, x)
            owner = zc * 4 + yy * 2 + xx
            at = pl.multiple_of(owner * GROUP, GROUP)
            own_cols = own[pl.ds(at, GROUP), :]
            other_cols = other[pl.ds(at, GROUP), :]
            cols = jnp.concatenate(
                [own_cols, turned(own_cols), other_cols, turned(other_cols)], axis=0
            )
            left = own[pl.ds(at, rows), :]
            out = lax.dot_general(left, cols, contract, preferred_element_type=jnp.float32)
            part[owner] = out.astype(jnp.bfloat16)
            return carry

        lax.fori_loop(0, 4, one, 0)

    spans = [pl.ds(0, half), pl.ds(half, half)]

    def owner_of(k, yy, xx):
        return chunk_z(k) * 4 + yy * 2 + xx

    def first_copy(axis, k, j):
        if axis == 0:
            owner = owner_of(k, 1 - y if j == 0 else y, 1 - x)
        else:
            owner = owner_of(k, 1 - y, 1 - x if j == 0 else x)
        return send(
            part.at[owner, spans[axis]], first_in.at[axis, k, j],
            first_send.at[axis, k, j], first_recv.at[axis, k, j],
            x_peer if axis == 0 else y_peer, mode,
        )

    def second_owner(axis, k):
        return owner_of(k, 1 - y, x) if axis == 0 else owner_of(k, y, 1 - x)

    def second_copy(axis, k):
        return send(
            part.at[second_owner(axis, k), spans[axis]], second_in.at[axis, k],
            second_send.at[axis, k], second_recv.at[axis, k],
            y_peer if axis == 0 else x_peer, mode,
        )

    firsts = {(a, k, j): first_copy(a, k, j) for a in range(2) for k in range(4) for j in range(2)}
    seconds = {(a, k): second_copy(a, k) for a in range(2) for k in range(4)}

    def f32(value):
        return value.astype(jnp.float32)

    def begin(k):
        multiply(k)
        for j in range(2):
            for a in range(2):
                firsts[a, k, j].start()

    def forward(k):
        for a in range(2):
            firsts[a, k, 0].wait_recv()
            owner = second_owner(a, k)
            part[owner, spans[a]] = (
                f32(part[owner, spans[a]]) + f32(first_in[a, k, 0])
            ).astype(jnp.bfloat16)
            seconds[a, k].start()

    def line_copy(k, to):
        owner = owner_of(k, y, x)
        if to == "outer":
            dst, sem = outer_in.at[k], outer_recv.at[k]
        elif to == "inner":
            dst, sem = inner_in.at[k], inner_recv.at[k]
        else:
            dst, sem = end_in, end_recv
        return send(
            part.at[owner], dst, line_send.at[k], sem,
            outer_peer if to == "end" else inner_peer, mode,
        )

    def keep(k):
        owner = owner_of(k, y, x)
        for a in range(2):
            firsts[a, k, 1].wait_recv()
            seconds[a, k].wait_recv()
            value = (
                f32(part[owner, spans[a]]) + f32(first_in[a, k, 1]) + f32(second_in[a, k])
            )
            if k >= 2:
                @pl.when(is_mid if k == 2 else is_end)
                def _():
                    total[spans[a], :] = value
            part[owner, spans[a]] = value.astype(jnp.bfloat16)
        if k < 3:
            @pl.when(is_end)
            def _():
                line_copy(k, "outer").start()

    def pass_on(k):
        owner = owner_of(k, y, x)

        @pl.when(is_mid)
        def _():
            if k < 2:
                line_copy(k, "outer").wait_recv()
                arrived = outer_in[k]
            else:
                line_copy(0, "inner").wait_recv()
                arrived = inner_in[0]
            part[owner] = (f32(part[owner]) + f32(arrived)).astype(jnp.bfloat16)
            line_copy(k, "inner" if k < 2 else "end").start()

    begin(0)
    begin(1)
    positions = pix * pixel_rows + lax.broadcasted_iota(
        jnp.int32, (pixels_ref.shape[0], pixel_rows), 1
    )
    counts = jnp.sum(
        jnp.where(pixels_ref[...] == positions, 1.0, 0.0), axis=0, keepdims=True
    )
    nothing = jnp.zeros_like(counts)
    row = lax.broadcasted_iota(jnp.int32, (16, 2 * pixel_rows), 0)
    real_weight = jnp.concatenate([counts, nothing], axis=1)
    imag_weight = jnp.concatenate([nothing, counts], axis=1)
    weight = jnp.where(row == 0, real_weight, jnp.where(row == 1, imag_weight, 0.0))
    ref_out[0] = lax.dot_general(
        weight.astype(jnp.bfloat16), own[pl.ds(0, width), :], contract, preferred_element_type=jnp.float32
    )[0:8]
    ref_copies[0].start()
    forward(0)
    begin(2)
    ref_next(0)
    forward(1)
    keep(0)
    begin(3)
    ref_next(1)
    forward(2)
    keep(1)
    pass_on(0)
    ref_next(2)
    forward(3)
    keep(2)
    pass_on(1)
    ref_next(3)
    keep(3)
    pass_on(3)

    @pl.when(is_mid)
    def _():
        line_copy(2, "outer").wait_recv()
        line_copy(1, "inner").wait_recv()
        total[...] = total[...] + f32(outer_in[2]) + f32(inner_in[1])

    @pl.when(is_end)
    def _():
        line_copy(3, "end").wait_recv()
        total[...] = total[...] + f32(end_in[...])

    cross_out[...] = total[GROUP:8 * GROUP, 128:256].astype(jnp.bfloat16)
    cross = send(cross_out, cross_in, cross_send, cross_recv, pix, 1 - mode)
    cross.start()

    lane = lax.broadcasted_iota(jnp.int32, (GROUP, 128), 1)
    low = lane < GROUP

    def group_rows(step):
        return pl.ds(pl.multiple_of(((pix + step) % 16) * GROUP, GROUP), GROUP)

    for d in range(NEAR):
        here = total[d * GROUP:(d + 1) * GROUP, 0:128]
        there = total[d * GROUP:(d + 1) * GROUP, 128:256]
        gram_ref[0, group_rows(d), :] = jnp.where(low, here, pltpu.roll(there, GROUP, 1))
        gram_ref[1, group_rows(d), :] = jnp.where(low, pltpu.roll(here, GROUP, 1), there)

    cross.wait_recv()
    turns = []
    for d in range(1, FAR + 1):
        stacked = jnp.concatenate(
            [
                total[d * GROUP:(d + 1) * GROUP, 0:128].astype(jnp.bfloat16),
                cross_in[(d - 1) * GROUP:d * GROUP, :],
            ],
            axis=0,
        )
        turn_out[d - 1] = stacked.T
        turn = send(
            turn_out.at[d - 1], turn_in.at[d - 1], turn_send.at[d - 1], turn_recv.at[d - 1],
            (pix + d) % 16, mode,
        )
        turn.start()
        turns.append(turn)
    ref_copies[4].wait_recv()
    sums_ref[0] = ref_out[4]
    sums_ref[1] = ref_in[4]
    for d in range(1, FAR + 1):
        turns[d - 1].wait_recv()
        arrived = f32(turn_in[d - 1])
        gram_ref[0, group_rows(16 - d), :] = arrived[0:GROUP]
        gram_ref[1, group_rows(16 - d), :] = -arrived[GROUP:]

    for copy in field_copies + ref_copies + list(firsts.values()) + list(seconds.values()):
        copy.wait_send()
    for copy in turns + [cross]:
        copy.wait_send()
    for k in range(3):
        @pl.when(is_end | (k < 2))
        def _():
            line_copy(k, "outer").wait_send()

    @pl.when(is_mid)
    def _():
        line_copy(3, "end").wait_send()


def finish_kernel(pixel_scale, gram_ref, sums_ref, band_ref, diag_ref):
    pix = lax.axis_index("pix")
    odd = pix % 2 == 1
    at = pl.multiple_of((pix // 2) * 128, 128)
    own = sums_ref[0, :, pl.ds(at, 128)]
    other = sums_ref[1, :, pl.ds(at, 128)]
    low = lax.broadcasted_iota(jnp.int32, own.shape, 1) < GROUP
    own = jnp.where(odd, pltpu.roll(own, GROUP, 1), own)
    other = jnp.where(odd, other, pltpu.roll(other, GROUP, 1))
    cols = jnp.where(low, own, other).T

    def unit(real, imag):
        magnitude = jnp.maximum(jnp.sqrt(real * real + imag * imag), 1.0)
        return real / magnitude, imag / magnitude

    col_real, col_imag = unit(cols[:, 0:1], cols[:, 1:2])
    row_real, row_imag = unit(sums_ref[0, 0:1, :], sums_ref[0, 1:2, :])
    unit_real = row_real * col_real + row_imag * col_imag
    unit_imag = row_imag * col_real - row_real * col_imag
    gram_real = gram_ref[0].T
    gram_imag = gram_ref[1].T
    real = (unit_real * gram_real - unit_imag * gram_imag) * pixel_scale
    imag = (unit_real * gram_imag + unit_imag * gram_real) * pixel_scale
    diag_ref[0] = real[:GROUP]
    diag_ref[1] = imag[:GROUP]
    band_ref[0] = real[GROUP:]
    band_ref[1] = imag[GROUP:]


def paired_shards(frames, ref_pixels):
    pixel_rows = frames.shape[1]
    width = frames.shape[2]
    rows = NEAR * GROUP
    half = rows // 2
    b16 = jnp.bfloat16
    dma = pltpu.SemaphoreType.DMA
    gram, sums = pl.pallas_call(
        gram_kernel,
        out_shape=(
            jax.ShapeDtypeStruct((2, width, 128), jnp.float32),
            jax.ShapeDtypeStruct((2, 8, width), jnp.float32),
        ),
        in_specs=[
            pl.BlockSpec(memory_space=pltpu.HBM),
            pl.BlockSpec(memory_space=pltpu.VMEM),
        ],
        out_specs=(pl.BlockSpec(memory_space=pltpu.VMEM),) * 2,
        scratch_shapes=[
            pltpu.VMEM((4, 4, pixel_rows, 4 * GROUP), b16),
            pltpu.VMEM((width + 8 * GROUP, 2 * pixel_rows), b16),
            pltpu.VMEM((width, 2 * pixel_rows), b16),
            pltpu.VMEM((16, rows, 256), b16),
            pltpu.VMEM((2, 4, 2, half, 256), b16),
            pltpu.VMEM((2, 4, half, 256), b16),
            pltpu.VMEM((3, rows, 256), b16),
            pltpu.VMEM((2, rows, 256), b16),
            pltpu.VMEM((rows, 256), b16),
            pltpu.VMEM((5, 8, width), jnp.float32),
            pltpu.VMEM((5, 8, width), jnp.float32),
            pltpu.VMEM((rows, 256), jnp.float32),
            pltpu.VMEM((FAR * GROUP, 128), b16),
            pltpu.VMEM((FAR * GROUP, 128), b16),
            pltpu.VMEM((FAR, 128, 128), b16),
            pltpu.VMEM((FAR, 128, 128), b16),
            dma((4,)), dma((4,)), dma((4,)),
            dma((2, 4, 2)), dma((2, 4, 2)),
            dma((2, 4)), dma((2, 4)),
            dma((4,)), dma((3,)), dma((2,)), dma,
            dma((5,)), dma((5,)),
            dma, dma,
            dma((FAR,)), dma((FAR,)),
        ],
        compiler_params=pltpu.CompilerParams(
            collective_id=0, has_side_effects=True, vmem_limit_bytes=61 * 1024 * 1024
        ),
    )(frames, ref_pixels.reshape(-1, 1))
    pixel_scale = 1.0 / math.sqrt(lax.axis_size("pix") * pixel_rows)
    band, diag = pl.pallas_call(
        functools.partial(finish_kernel, pixel_scale),
        out_shape=(jax.ShapeDtypeStruct((2, GROUP, width), jnp.float32),) * 2,
        in_specs=[pl.BlockSpec(memory_space=pltpu.VMEM)] * 2,
        out_specs=(pl.BlockSpec(memory_space=pltpu.VMEM),) * 2,
    )(gram, sums)
    return (jnp.swapaxes(band, 1, 2), jnp.swapaxes(diag, 1, 2))


def solution(mesh):
    placed = (P(None, "pix", "mode"), P())
    paired = mesh.shape["pix"] == 16 and mesh.shape["mode"] == 2

    def body(frames, ref_pixels):
        if paired and frames.shape[2] == 16 * GROUP:
            return paired_shards(frames, ref_pixels)
        return shards(frames, ref_pixels)

    return jax.shard_map(
        body,
        mesh=mesh,
        in_specs=placed,
        out_specs=(P(None, "mode", "pix"), P(None, "mode", "pix")),
        check_vma=False,
    )
```

```python
import functools
import math

import jax
import jax.numpy as jnp
from jax import lax
from jax.experimental import pallas as pl
from jax.experimental.pallas import tpu as pltpu
from jax.sharding import PartitionSpec as P


def unit_phase(sums):
    magnitude = jnp.maximum(jnp.sqrt(sums[0] * sums[0] + sums[1] * sums[1]), 1.0)
    return sums / magnitude[None, :]


def rotate(gram_real, gram_imag, phase_rows, phase_cols, pixel_scale):
    row_real = phase_rows[0][:, None]
    row_imag = phase_rows[1][:, None]
    col_real = phase_cols[0][None, :]
    col_imag = phase_cols[1][None, :]
    unit_real = row_real * col_real + row_imag * col_imag
    unit_imag = row_imag * col_real - row_real * col_imag
    return jnp.stack(
        [
            (unit_real * gram_real - unit_imag * gram_imag) * pixel_scale,
            (unit_real * gram_imag + unit_imag * gram_real) * pixel_scale,
        ]
    )


def shards(frames, ref_pixels):
    pix_count = lax.axis_size("pix")
    mode_count = lax.axis_size("mode")
    pix_index = lax.axis_index("pix")
    mode_index = lax.axis_index("mode")
    pixel_rows = frames.shape[1]
    block_width = frames.shape[2]
    full_tiles = mode_count // 2 + 1
    full_width = full_tiles * block_width
    frame_float = frames.astype(jnp.float32)
    real_part = (frame_float[0] - frame_float[2]).astype(jnp.bfloat16)
    imag_part = (frame_float[3] - frame_float[1]).astype(jnp.bfloat16)
    fields = jnp.stack([real_part, imag_part])
    positions = pix_index * pixel_rows + lax.iota(jnp.int32, pixel_rows)
    counts = jnp.sum(
        (ref_pixels[:, None] == positions[None, :]).astype(jnp.float32), axis=0
    ).astype(jnp.bfloat16)
    local_ref = jnp.einsum("p,cpm->cm", counts, fields, preferred_element_type=jnp.float32)
    own_ref = lax.psum(local_ref, "pix")
    phase_all = lax.all_gather(unit_phase(own_ref), "mode", axis=1, tiled=True)
    phase_own = lax.dynamic_slice_in_dim(phase_all, mode_index * block_width, block_width, 1)
    phase_twice = jnp.concatenate([phase_all, phase_all], axis=1)
    phase_full = lax.dynamic_slice_in_dim(phase_twice, mode_index * block_width, full_width, 1)
    whole_fields = lax.all_gather(fields, "mode", axis=2, tiled=True)
    tiled = whole_fields.reshape(2, pixel_rows, mode_count, block_width)
    picked = (mode_index + lax.iota(jnp.int32, full_tiles)) % mode_count
    band_fields = jnp.take(tiled, picked, axis=2).reshape(2, pixel_rows, full_width)
    contract = (((0,), (0,)), ((), ()))
    own_real = fields[0]
    own_imag = fields[1]
    band_real = band_fields[0]
    band_imag = band_fields[1]
    gram_real = lax.dot_general(
        own_real, band_real, contract, preferred_element_type=jnp.float32
    ) + lax.dot_general(own_imag, band_imag, contract, preferred_element_type=jnp.float32)
    gram_imag = lax.dot_general(
        own_real, band_imag, contract, preferred_element_type=jnp.float32
    ) - lax.dot_general(own_imag, band_real, contract, preferred_element_type=jnp.float32)
    pixel_scale = 1.0 / math.sqrt(pix_count * pixel_rows)
    raw_terms = jnp.stack([gram_real, gram_imag])
    raw_diag, raw_band = (
        lax.psum_scatter(raw_terms[:, :, :block_width], "pix", scatter_dimension=2, tiled=True),
        lax.psum_scatter(raw_terms[:, :, block_width:], "pix", scatter_dimension=2, tiled=True),
    )
    diag_slice = block_width // pix_count
    band_slice = (full_width - block_width) // pix_count
    diag_cols = lax.dynamic_slice_in_dim(phase_full, pix_index * diag_slice, diag_slice, 1)
    band_cols = lax.dynamic_slice_in_dim(
        phase_full, block_width + pix_index * band_slice, band_slice, 1
    )
    diag_out = rotate(raw_diag[0], raw_diag[1], phase_own, diag_cols, pixel_scale)
    band_out = rotate(raw_band[0], raw_band[1], phase_own, band_cols, pixel_scale)
    return (band_out, diag_out)


MESH = pl.DeviceIdType.MESH
GROUP = 64
NEAR = 9
SIDE = 224
LAST = 128
FAR = 7


def gram_kernel(
    frames_hbm, pixels_ref, gram_ref, sums_ref,
    frames_ref, own, other, part, first_in, second_in, outer_in, inner_in, end_in,
    last_outer_in, last_inner_in, last_end_in, last_first_in, last_second_in,
    ref_out, ref_in, total, cross_out, cross_in, turn_out, turn_in,
    frame_sem, field_send, field_recv, first_send, first_recv, second_send, second_recv,
    line_send, outer_recv, inner_recv, end_recv,
    last_send, last_outer_recv, last_inner_recv, last_end_recv,
    last_first_send, last_first_recv, last_second_send, last_second_recv, ref_send, ref_recv,
    cross_send, cross_recv, turn_send, turn_recv,
):
    pix = lax.axis_index("pix")
    mode = lax.axis_index("mode")
    x, y, z = pix % 2, (pix // 2) % 2, pix // 4
    upper = z >= 2
    is_end = (z == 0) | (z == 3)
    is_mid = (z == 1) | (z == 2)
    x_peer = pix + 1 - 2 * x
    y_peer = pix + 2 - 4 * y
    inner_peer = jnp.where(upper, pix - 4, pix + 4)
    outer_peer = jnp.where(upper, pix + 4, pix - 4)
    z_even_peer = pix + 4 - 8 * (z % 2)
    z_far_peer = pix + 8 - 16 * (z // 2)
    pixel_rows = frames_hbm.shape[1]
    width = frames_hbm.shape[2]
    rows = NEAR * GROUP
    chunk = 4 * GROUP

    def chunk_z(k):
        return jnp.where(upper, k, 3 - k)

    def chunk_modes(k):
        return pl.ds(pl.multiple_of(chunk_z(k) * chunk, chunk), chunk)

    loads = [
        pltpu.make_async_copy(
            frames_hbm.at[:, :, chunk_modes(k)], frames_ref.at[k], frame_sem.at[k]
        )
        for k in range(4)
    ]
    for load in loads:
        load.start()
    barrier = pltpu.get_barrier_semaphore()
    for step in range(1, 16):
        pl.semaphore_signal(
            barrier, inc=1, device_id=((pix + step) % 16, mode), device_id_type=MESH
        )
    pl.semaphore_signal(barrier, inc=1, device_id=(pix, 1 - mode), device_id_type=MESH)

    def send(src, dst, send_sem, recv_sem, to_pix, to_mode):
        copy = pltpu.make_async_remote_copy(
            src_ref=src, dst_ref=dst, send_sem=send_sem, recv_sem=recv_sem,
            device_id=(to_pix, to_mode), device_id_type=MESH,
        )
        return copy

    for k in range(4):
        loads[k].wait()
        frame = [frames_ref[k, step].astype(jnp.float32) for step in range(4)]
        modes = chunk_modes(k)
        own[modes, 0:pixel_rows] = (frame[0] - frame[2]).astype(jnp.bfloat16).T
        own[modes, pixel_rows:2 * pixel_rows] = (frame[3] - frame[1]).astype(jnp.bfloat16).T
    own[pl.ds(width, 8 * GROUP), :] = own[pl.ds(0, 8 * GROUP), :]
    pl.semaphore_wait(barrier, 16)

    def field_copy(k):
        modes = chunk_modes(k)
        return send(own.at[modes], other.at[modes], field_send.at[k], field_recv.at[k], pix, 1 - mode)

    field_copies = [field_copy(k) for k in range(4)]
    for copy in field_copies:
        copy.start()

    ref_peers = [x_peer, y_peer, z_even_peer, z_far_peer, pix]

    def ref_copy(step):
        return send(
            ref_out.at[step], ref_in.at[step], ref_send.at[step], ref_recv.at[step],
            ref_peers[step], mode if step < 4 else 1 - mode,
        )

    ref_copies = [ref_copy(step) for step in range(5)]

    def ref_next(step):
        ref_copies[step].wait_recv()
        ref_out[step + 1] = ref_out[step] + ref_in[step]
        ref_copies[step + 1].start()

    contract = (((1,), (1,)), ((), ()))

    def turned(block):
        return jnp.concatenate([block[:, pixel_rows:], -block[:, :pixel_rows]], axis=1)

    def multiply(k):
        zc = chunk_z(k)
        field_copies[k].wait_recv()

        def one(t, carry):
            yy = jnp.where(t % 2 == 0, 1 - y, y)
            xx = jnp.where(t < 2, 1 - x, x)
            owner = zc * 4 + yy * 2 + xx
            at = pl.multiple_of(owner * GROUP, GROUP)
            own_cols = own[pl.ds(at, GROUP), :]
            other_cols = other[pl.ds(at, GROUP), :]
            cols = jnp.concatenate(
                [own_cols, turned(own_cols), other_cols, turned(other_cols)], axis=0
            )
            left = own[pl.ds(at, rows), :]
            out = lax.dot_general(left, cols, contract, preferred_element_type=jnp.float32)
            part[owner] = out.astype(jnp.bfloat16)
            return carry

        lax.fori_loop(0, 4, one, 0)

    spans = [pl.ds(0, SIDE), pl.ds(SIDE, SIDE)]
    both = pl.ds(0, 2 * SIDE)
    last = pl.ds(2 * SIDE, LAST)
    last_spans = [pl.ds(2 * SIDE, LAST // 2), pl.ds(2 * SIDE + LAST // 2, LAST // 2)]

    def owner_of(k, yy, xx):
        return chunk_z(k) * 4 + yy * 2 + xx

    def first_copy(axis, k, j):
        if axis == 0:
            owner = owner_of(k, 1 - y if j == 0 else y, 1 - x)
        else:
            owner = owner_of(k, 1 - y, 1 - x if j == 0 else x)
        return send(
            part.at[owner, spans[axis]], first_in.at[axis, k, j],
            first_send.at[axis, k, j], first_recv.at[axis, k, j],
            x_peer if axis == 0 else y_peer, mode,
        )

    def second_owner(axis, k):
        return owner_of(k, 1 - y, x) if axis == 0 else owner_of(k, y, 1 - x)

    def second_copy(axis, k):
        return send(
            part.at[second_owner(axis, k), spans[axis]], second_in.at[axis, k],
            second_send.at[axis, k], second_recv.at[axis, k],
            y_peer if axis == 0 else x_peer, mode,
        )

    firsts = {(a, k, j): first_copy(a, k, j) for a in range(2) for k in range(4) for j in range(2)}
    seconds = {(a, k): second_copy(a, k) for a in range(2) for k in range(4)}

    def f32(value):
        return value.astype(jnp.float32)

    def start_first(k):
        for j in range(2):
            for a in range(2):
                firsts[a, k, j].start()

    def forward(k):
        for a in range(2):
            firsts[a, k, 0].wait_recv()
            owner = second_owner(a, k)
            part[owner, spans[a]] = (
                f32(part[owner, spans[a]]) + f32(first_in[a, k, 0])
            ).astype(jnp.bfloat16)
            seconds[a, k].start()

    def line_copy(k, to):
        owner = owner_of(k, y, x)
        if to == "outer":
            dst, sem = outer_in.at[k], outer_recv.at[k]
        elif to == "inner":
            dst, sem = inner_in.at[k], inner_recv.at[k]
        else:
            dst, sem = end_in, end_recv
        return send(
            part.at[owner, both], dst, line_send.at[k], sem,
            outer_peer if to == "end" else inner_peer, mode,
        )

    def keep(k):
        owner = owner_of(k, y, x)
        for a in range(2):
            firsts[a, k, 1].wait_recv()
            seconds[a, k].wait_recv()
            value = (
                f32(part[owner, spans[a]]) + f32(first_in[a, k, 1]) + f32(second_in[a, k])
            )
            if k >= 2:
                @pl.when(is_mid if k == 2 else is_end)
                def _():
                    total[spans[a], :] = value
            part[owner, spans[a]] = value.astype(jnp.bfloat16)
        if k < 3:
            @pl.when(is_end)
            def _():
                line_copy(k, "outer").start()

    def pass_on(k):
        owner = owner_of(k, y, x)

        @pl.when(is_mid)
        def _():
            if k < 2:
                line_copy(k, "outer").wait_recv()
                arrived = outer_in[k]
            else:
                line_copy(0, "inner").wait_recv()
                arrived = inner_in[0]
            part[owner, both] = (f32(part[owner, both]) + f32(arrived)).astype(jnp.bfloat16)
            line_copy(k, "inner" if k < 2 else "end").start()

    def last_copy(k, to):
        owners = pl.ds(chunk_z(k) * 4, 4)
        if to == "outer":
            dst, sem = last_outer_in.at[k], last_outer_recv.at[k]
        elif to == "inner":
            dst, sem = last_inner_in.at[k], last_inner_recv.at[k]
        else:
            dst, sem = last_end_in, last_end_recv
        return send(
            part.at[owners, last], dst, last_send.at[k], sem,
            outer_peer if to == "end" else inner_peer, mode,
        )

    def last_begin(k):
        @pl.when(is_end)
        def _():
            last_copy(k, "outer").start()

    def last_add(k, terms):
        first = chunk_z(k) * 4
        for i in range(4):
            value = f32(part[first + i, last])
            for term in terms:
                value = value + f32(term[i])
            part[first + i, last] = value.astype(jnp.bfloat16)

    def last_pass(k):
        @pl.when(is_mid)
        def _():
            if k < 2:
                last_copy(k, "outer").wait_recv()
                last_add(k, [last_outer_in.at[k]])
                last_copy(k, "inner").start()
            else:
                last_copy(0, "inner").wait_recv()
                last_add(k, [last_inner_in.at[0]])
                last_copy(k, "end").start()

    def last_first_copy(axis, j):
        if axis == 0:
            owner = z * 4 + (1 - y if j == 0 else y) * 2 + 1 - x
        else:
            owner = z * 4 + (1 - y) * 2 + (1 - x if j == 0 else x)
        return send(
            part.at[owner, last_spans[axis]], last_first_in.at[axis, j],
            last_first_send.at[axis, j], last_first_recv.at[axis, j],
            x_peer if axis == 0 else y_peer, mode,
        )

    def last_second_owner(axis):
        return z * 4 + (1 - y) * 2 + x if axis == 0 else z * 4 + y * 2 + 1 - x

    def last_second_copy(axis):
        return send(
            part.at[last_second_owner(axis), last_spans[axis]], last_second_in.at[axis],
            last_second_send.at[axis], last_second_recv.at[axis],
            y_peer if axis == 0 else x_peer, mode,
        )

    last_firsts = {(a, j): last_first_copy(a, j) for a in range(2) for j in range(2)}
    last_seconds = [last_second_copy(a) for a in range(2)]

    def last_spread():
        @pl.when(is_mid)
        def _():
            last_copy(2, "outer").wait_recv()
            last_copy(1, "inner").wait_recv()
            last_add(2, [last_outer_in.at[2], last_inner_in.at[1]])

        @pl.when(is_end)
        def _():
            last_copy(3, "end").wait_recv()
            last_add(3, [last_end_in])

        for j in range(2):
            for a in range(2):
                last_firsts[a, j].start()

    def last_forward():
        for a in range(2):
            last_firsts[a, 0].wait_recv()
            owner = last_second_owner(a)
            part[owner, last_spans[a]] = (
                f32(part[owner, last_spans[a]]) + f32(last_first_in[a, 0])
            ).astype(jnp.bfloat16)
            last_seconds[a].start()

    def last_keep():
        for a in range(2):
            last_firsts[a, 1].wait_recv()
            last_seconds[a].wait_recv()
            total[last_spans[a], :] = (
                f32(part[pix, last_spans[a]]) + f32(last_first_in[a, 1]) + f32(last_second_in[a])
            )

    for k in range(3):
        multiply(k)
        if k < 2:
            start_first(k)
        last_begin(k)
    positions = pix * pixel_rows + lax.broadcasted_iota(
        jnp.int32, (pixels_ref.shape[1], pixel_rows), 1
    )
    listed = jnp.broadcast_to(pixels_ref[...], (8, pixels_ref.shape[1])).T[:, 0:1]
    counts = jnp.sum(
        jnp.where(listed == positions, 1.0, 0.0), axis=0, keepdims=True
    )
    nothing = jnp.zeros_like(counts)
    row = lax.broadcasted_iota(jnp.int32, (16, 2 * pixel_rows), 0)
    real_weight = jnp.concatenate([counts, nothing], axis=1)
    imag_weight = jnp.concatenate([nothing, counts], axis=1)
    weight = jnp.where(row == 0, real_weight, jnp.where(row == 1, imag_weight, 0.0))
    ref_out[0] = lax.dot_general(
        weight.astype(jnp.bfloat16), own[pl.ds(0, width), :], contract, preferred_element_type=jnp.float32
    )[0:8]
    ref_copies[0].start()
    forward(0)
    start_first(2)
    multiply(3)
    ref_next(0)
    last_pass(0)
    forward(1)
    start_first(3)
    last_pass(1)
    ref_next(1)
    keep(0)
    forward(2)
    last_pass(3)
    ref_next(2)
    last_spread()
    keep(1)
    pass_on(0)
    ref_next(3)
    forward(3)
    last_forward()
    keep(2)
    pass_on(1)
    last_keep()
    keep(3)
    pass_on(3)

    @pl.when(is_mid)
    def _():
        line_copy(2, "outer").wait_recv()
        line_copy(1, "inner").wait_recv()
        total[both, :] = total[both, :] + f32(outer_in[2]) + f32(inner_in[1])

    @pl.when(is_end)
    def _():
        line_copy(3, "end").wait_recv()
        total[both, :] = total[both, :] + f32(end_in[...])

    cross_out[...] = total[GROUP:8 * GROUP, 128:256].astype(jnp.bfloat16)
    cross = send(cross_out, cross_in, cross_send, cross_recv, pix, 1 - mode)
    cross.start()

    lane = lax.broadcasted_iota(jnp.int32, (GROUP, 128), 1)
    low = lane < GROUP

    def group_rows(step):
        return pl.ds(pl.multiple_of(((pix + step) % 16) * GROUP, GROUP), GROUP)

    for d in range(NEAR):
        here = total[d * GROUP:(d + 1) * GROUP, 0:128]
        there = total[d * GROUP:(d + 1) * GROUP, 128:256]
        gram_ref[0, group_rows(d), :] = jnp.where(low, here, pltpu.roll(there, GROUP, 1))
        gram_ref[1, group_rows(d), :] = jnp.where(low, pltpu.roll(here, GROUP, 1), there)

    cross.wait_recv()
    turns = []
    for d in range(1, FAR + 1):
        stacked = jnp.concatenate(
            [
                total[d * GROUP:(d + 1) * GROUP, 0:128].astype(jnp.bfloat16),
                cross_in[(d - 1) * GROUP:d * GROUP, :],
            ],
            axis=0,
        )
        turn_out[d - 1] = stacked.T
        turn = send(
            turn_out.at[d - 1], turn_in.at[d - 1], turn_send.at[d - 1], turn_recv.at[d - 1],
            (pix + d) % 16, mode,
        )
        turn.start()
        turns.append(turn)
    ref_copies[4].wait_recv()
    sums_ref[0] = ref_out[4]
    sums_ref[1] = ref_in[4]
    for d in range(1, FAR + 1):
        turns[d - 1].wait_recv()
        arrived = f32(turn_in[d - 1])
        gram_ref[0, group_rows(16 - d), :] = arrived[0:GROUP]
        gram_ref[1, group_rows(16 - d), :] = -arrived[GROUP:]

    for copy in field_copies + ref_copies + list(firsts.values()) + list(seconds.values()):
        copy.wait_send()
    for copy in turns + [cross] + list(last_firsts.values()) + last_seconds:
        copy.wait_send()
    for k in range(3):
        @pl.when(is_end | (k < 2))
        def _():
            line_copy(k, "outer").wait_send()
            last_copy(k, "outer").wait_send()

    @pl.when(is_mid)
    def _():
        line_copy(3, "end").wait_send()
        last_copy(3, "end").wait_send()


def finish_kernel(pixel_scale, gram_ref, sums_ref, band_ref, diag_ref):
    pix = lax.axis_index("pix")
    odd = pix % 2 == 1
    at = pl.multiple_of((pix // 2) * 128, 128)
    own = sums_ref[0, :, pl.ds(at, 128)]
    other = sums_ref[1, :, pl.ds(at, 128)]
    low = lax.broadcasted_iota(jnp.int32, own.shape, 1) < GROUP
    own = jnp.where(odd, pltpu.roll(own, GROUP, 1), own)
    other = jnp.where(odd, other, pltpu.roll(other, GROUP, 1))
    cols = jnp.where(low, own, other).T

    def unit(real, imag):
        magnitude = jnp.maximum(jnp.sqrt(real * real + imag * imag), 1.0)
        return real / magnitude, imag / magnitude

    col_real, col_imag = unit(cols[:, 0:1], cols[:, 1:2])
    row_real, row_imag = unit(sums_ref[0, 0:1, :], sums_ref[0, 1:2, :])
    unit_real = row_real * col_real + row_imag * col_imag
    unit_imag = row_imag * col_real - row_real * col_imag
    gram_real = gram_ref[0].T
    gram_imag = gram_ref[1].T
    real = (unit_real * gram_real - unit_imag * gram_imag) * pixel_scale
    imag = (unit_real * gram_imag + unit_imag * gram_real) * pixel_scale
    diag_ref[0] = real[:GROUP]
    diag_ref[1] = imag[:GROUP]
    band_ref[0] = real[GROUP:]
    band_ref[1] = imag[GROUP:]


def paired_shards(frames, ref_pixels):
    pixel_rows = frames.shape[1]
    width = frames.shape[2]
    rows = NEAR * GROUP
    b16 = jnp.bfloat16
    dma = pltpu.SemaphoreType.DMA
    gram, sums = pl.pallas_call(
        gram_kernel,
        out_shape=(
            jax.ShapeDtypeStruct((2, width, 128), jnp.float32),
            jax.ShapeDtypeStruct((2, 8, width), jnp.float32),
        ),
        in_specs=[
            pl.BlockSpec(memory_space=pltpu.HBM),
            pl.BlockSpec(memory_space=pltpu.VMEM),
        ],
        out_specs=(pl.BlockSpec(memory_space=pltpu.VMEM),) * 2,
        scratch_shapes=[
            pltpu.VMEM((4, 4, pixel_rows, 4 * GROUP), b16),
            pltpu.VMEM((width + 8 * GROUP, 2 * pixel_rows), b16),
            pltpu.VMEM((width, 2 * pixel_rows), b16),
            pltpu.VMEM((16, rows, 256), b16),
            pltpu.VMEM((2, 4, 2, SIDE, 256), b16),
            pltpu.VMEM((2, 4, SIDE, 256), b16),
            pltpu.VMEM((3, 2 * SIDE, 256), b16),
            pltpu.VMEM((2, 2 * SIDE, 256), b16),
            pltpu.VMEM((2 * SIDE, 256), b16),
            pltpu.VMEM((3, 4, LAST, 256), b16),
            pltpu.VMEM((2, 4, LAST, 256), b16),
            pltpu.VMEM((4, LAST, 256), b16),
            pltpu.VMEM((2, 2, LAST // 2, 256), b16),
            pltpu.VMEM((2, LAST // 2, 256), b16),
            pltpu.VMEM((5, 8, width), jnp.float32),
            pltpu.VMEM((5, 8, width), jnp.float32),
            pltpu.VMEM((rows, 256), jnp.float32),
            pltpu.VMEM((FAR * GROUP, 128), b16),
            pltpu.VMEM((FAR * GROUP, 128), b16),
            pltpu.VMEM((FAR, 128, 128), b16),
            pltpu.VMEM((FAR, 128, 128), b16),
            dma((4,)), dma((4,)), dma((4,)),
            dma((2, 4, 2)), dma((2, 4, 2)),
            dma((2, 4)), dma((2, 4)),
            dma((4,)), dma((3,)), dma((2,)), dma,
            dma((4,)), dma((3,)), dma((2,)), dma,
            dma((2, 2)), dma((2, 2)), dma((2,)), dma((2,)),
            dma((5,)), dma((5,)),
            dma, dma,
            dma((FAR,)), dma((FAR,)),
        ],
        compiler_params=pltpu.CompilerParams(
            collective_id=0, has_side_effects=True, vmem_limit_bytes=55 * 1024 * 1024
        ),
    )(frames, ref_pixels.reshape(1, -1))
    pixel_scale = 1.0 / math.sqrt(lax.axis_size("pix") * pixel_rows)
    band, diag = pl.pallas_call(
        functools.partial(finish_kernel, pixel_scale),
        out_shape=(jax.ShapeDtypeStruct((2, GROUP, width), jnp.float32),) * 2,
        in_specs=[pl.BlockSpec(memory_space=pltpu.VMEM)] * 2,
        out_specs=(pl.BlockSpec(memory_space=pltpu.VMEM),) * 2,
    )(gram, sums)
    return (jnp.swapaxes(band, 1, 2), jnp.swapaxes(diag, 1, 2))


def solution(mesh):
    placed = (P(None, "pix", "mode"), P())
    paired = mesh.shape["pix"] == 16 and mesh.shape["mode"] == 2

    def body(frames, ref_pixels):
        if paired and frames.shape[2] == 16 * GROUP:
            return paired_shards(frames, ref_pixels)
        return shards(frames, ref_pixels)

    return jax.shard_map(
        body,
        mesh=mesh,
        in_specs=placed,
        out_specs=(P(None, "mode", "pix"), P(None, "mode", "pix")),
        check_vma=False,
    )
```

```python
import functools
import math

import jax
import jax.numpy as jnp
from jax import lax
from jax.experimental import pallas as pl
from jax.experimental.pallas import tpu as pltpu
from jax.sharding import PartitionSpec as P


def unit_phase(sums):
    magnitude = jnp.maximum(jnp.sqrt(sums[0] * sums[0] + sums[1] * sums[1]), 1.0)
    return sums / magnitude[None, :]


def rotate(gram_real, gram_imag, phase_rows, phase_cols, pixel_scale):
    row_real = phase_rows[0][:, None]
    row_imag = phase_rows[1][:, None]
    col_real = phase_cols[0][None, :]
    col_imag = phase_cols[1][None, :]
    unit_real = row_real * col_real + row_imag * col_imag
    unit_imag = row_imag * col_real - row_real * col_imag
    return jnp.stack(
        [
            (unit_real * gram_real - unit_imag * gram_imag) * pixel_scale,
            (unit_real * gram_imag + unit_imag * gram_real) * pixel_scale,
        ]
    )


def shards(frames, ref_pixels):
    pix_count = lax.axis_size("pix")
    mode_count = lax.axis_size("mode")
    pix_index = lax.axis_index("pix")
    mode_index = lax.axis_index("mode")
    pixel_rows = frames.shape[1]
    block_width = frames.shape[2]
    full_tiles = mode_count // 2 + 1
    full_width = full_tiles * block_width
    frame_float = frames.astype(jnp.float32)
    real_part = (frame_float[0] - frame_float[2]).astype(jnp.bfloat16)
    imag_part = (frame_float[3] - frame_float[1]).astype(jnp.bfloat16)
    fields = jnp.stack([real_part, imag_part])
    positions = pix_index * pixel_rows + lax.iota(jnp.int32, pixel_rows)
    counts = jnp.sum(
        (ref_pixels[:, None] == positions[None, :]).astype(jnp.float32), axis=0
    ).astype(jnp.bfloat16)
    local_ref = jnp.einsum("p,cpm->cm", counts, fields, preferred_element_type=jnp.float32)
    own_ref = lax.psum(local_ref, "pix")
    phase_all = lax.all_gather(unit_phase(own_ref), "mode", axis=1, tiled=True)
    phase_own = lax.dynamic_slice_in_dim(phase_all, mode_index * block_width, block_width, 1)
    phase_twice = jnp.concatenate([phase_all, phase_all], axis=1)
    phase_full = lax.dynamic_slice_in_dim(phase_twice, mode_index * block_width, full_width, 1)
    whole_fields = lax.all_gather(fields, "mode", axis=2, tiled=True)
    tiled = whole_fields.reshape(2, pixel_rows, mode_count, block_width)
    picked = (mode_index + lax.iota(jnp.int32, full_tiles)) % mode_count
    band_fields = jnp.take(tiled, picked, axis=2).reshape(2, pixel_rows, full_width)
    contract = (((0,), (0,)), ((), ()))
    own_real = fields[0]
    own_imag = fields[1]
    band_real = band_fields[0]
    band_imag = band_fields[1]
    gram_real = lax.dot_general(
        own_real, band_real, contract, preferred_element_type=jnp.float32
    ) + lax.dot_general(own_imag, band_imag, contract, preferred_element_type=jnp.float32)
    gram_imag = lax.dot_general(
        own_real, band_imag, contract, preferred_element_type=jnp.float32
    ) - lax.dot_general(own_imag, band_real, contract, preferred_element_type=jnp.float32)
    pixel_scale = 1.0 / math.sqrt(pix_count * pixel_rows)
    raw_terms = jnp.stack([gram_real, gram_imag])
    raw_diag, raw_band = (
        lax.psum_scatter(raw_terms[:, :, :block_width], "pix", scatter_dimension=2, tiled=True),
        lax.psum_scatter(raw_terms[:, :, block_width:], "pix", scatter_dimension=2, tiled=True),
    )
    diag_slice = block_width // pix_count
    band_slice = (full_width - block_width) // pix_count
    diag_cols = lax.dynamic_slice_in_dim(phase_full, pix_index * diag_slice, diag_slice, 1)
    band_cols = lax.dynamic_slice_in_dim(
        phase_full, block_width + pix_index * band_slice, band_slice, 1
    )
    diag_out = rotate(raw_diag[0], raw_diag[1], phase_own, diag_cols, pixel_scale)
    band_out = rotate(raw_band[0], raw_band[1], phase_own, band_cols, pixel_scale)
    return (band_out, diag_out)


MESH = pl.DeviceIdType.MESH
GROUP = 64
NEAR = 9
SIDE = 224
LAST = 128
FAR = 7


def gram_kernel(
    frames_hbm, pixels_ref, gram_ref, sums_ref,
    frames_ref, own, other, part, first_in, second_in, outer_in, inner_in, end_in,
    last_outer_in, last_inner_in, last_end_in, last_first_in, last_second_in,
    ref_out, ref_in, total, cross_out, cross_in, turn_out, turn_in,
    frame_sem, field_send, field_recv, first_send, first_recv, second_send, second_recv,
    line_send, outer_recv, inner_recv, end_recv,
    last_send, last_outer_recv, last_inner_recv, last_end_recv,
    last_first_send, last_first_recv, last_second_send, last_second_recv, ref_send, ref_recv,
    cross_send, cross_recv, turn_send, turn_recv,
):
    pix = lax.axis_index("pix")
    mode = lax.axis_index("mode")
    x, y, z = pix % 2, (pix // 2) % 2, pix // 4
    upper = z >= 2
    is_end = (z == 0) | (z == 3)
    is_mid = (z == 1) | (z == 2)
    x_peer = pix + 1 - 2 * x
    y_peer = pix + 2 - 4 * y
    inner_peer = jnp.where(upper, pix - 4, pix + 4)
    outer_peer = jnp.where(upper, pix + 4, pix - 4)
    z_even_peer = pix + 4 - 8 * (z % 2)
    z_far_peer = pix + 8 - 16 * (z // 2)
    pixel_rows = frames_hbm.shape[1]
    width = frames_hbm.shape[2]
    rows = NEAR * GROUP
    chunk = 4 * GROUP

    def chunk_z(k):
        return jnp.where(upper, k, 3 - k)

    def chunk_modes(k):
        return pl.ds(pl.multiple_of(chunk_z(k) * chunk, chunk), chunk)

    loads = [
        pltpu.make_async_copy(
            frames_hbm.at[:, :, chunk_modes(k)], frames_ref.at[k], frame_sem.at[k]
        )
        for k in range(4)
    ]
    for load in loads:
        load.start()
    barrier = pltpu.get_barrier_semaphore()
    for step in range(1, 16):
        pl.semaphore_signal(
            barrier, inc=1, device_id=((pix + step) % 16, mode), device_id_type=MESH
        )
    pl.semaphore_signal(barrier, inc=1, device_id=(pix, 1 - mode), device_id_type=MESH)

    def send(src, dst, send_sem, recv_sem, to_pix, to_mode):
        copy = pltpu.make_async_remote_copy(
            src_ref=src, dst_ref=dst, send_sem=send_sem, recv_sem=recv_sem,
            device_id=(to_pix, to_mode), device_id_type=MESH,
        )
        return copy

    def ring_rows(zz, column):
        return pl.ds(pl.multiple_of((column * 4 + zz) * GROUP, GROUP), GROUP)

    for k in range(4):
        loads[k].wait()
        frame = [frames_ref[k, step].astype(jnp.float32) for step in range(4)]
        real = (frame[0] - frame[2]).astype(jnp.bfloat16).T
        imag = (frame[3] - frame[1]).astype(jnp.bfloat16).T
        for i in range(4):
            to = ring_rows(chunk_z(k), i)
            own[to, 0:pixel_rows] = real[i * GROUP:(i + 1) * GROUP]
            own[to, pixel_rows:2 * pixel_rows] = imag[i * GROUP:(i + 1) * GROUP]
    own[pl.ds(width, 8 * GROUP), :] = own[pl.ds(0, 8 * GROUP), :]
    pl.semaphore_wait(barrier, 16)

    def field_copy(k, i):
        at = ring_rows(chunk_z(k), i)
        return send(
            own.at[at], other.at[at], field_send.at[k, i], field_recv.at[k, i], pix, 1 - mode
        )

    field_copies = [field_copy(k, i) for k in range(4) for i in range(4)]
    for copy in field_copies:
        copy.start()

    ref_peers = [x_peer, y_peer, z_even_peer, z_far_peer, pix]

    def ref_copy(step):
        return send(
            ref_out.at[step], ref_in.at[step], ref_send.at[step], ref_recv.at[step],
            ref_peers[step], mode if step < 4 else 1 - mode,
        )

    ref_copies = [ref_copy(step) for step in range(5)]

    def ref_next(step):
        ref_copies[step].wait_recv()
        ref_out[step + 1] = ref_out[step] + ref_in[step]
        ref_copies[step + 1].start()

    contract = (((1,), (1,)), ((), ()))

    def turned(block):
        return jnp.concatenate([block[:, pixel_rows:], -block[:, :pixel_rows]], axis=1)

    def multiply(k):
        zc = chunk_z(k)
        for i in range(4):
            field_copies[4 * k + i].wait_recv()
        for t in range(4):
            column = (1 - y if t % 2 == 0 else y) * 2 + (1 - x if t < 2 else x)
            start = pl.multiple_of((column * 4 + zc) * GROUP, GROUP)
            own_cols = own[pl.ds(start, GROUP), :]
            other_cols = other[pl.ds(start, GROUP), :]
            cols = jnp.concatenate(
                [own_cols, turned(own_cols), other_cols, turned(other_cols)], axis=0
            )
            left = own[pl.ds(start, rows), :]
            out = lax.dot_general(left, cols, contract, preferred_element_type=jnp.float32)
            part[zc * 4 + column] = out.astype(jnp.bfloat16)
            if k < 2:
                for a, j in (((0, 0), (1, 0)), ((0, 1),), ((1, 1),), ())[t]:
                    firsts[a, k, j].start()

    spans = [pl.ds(0, SIDE), pl.ds(SIDE, SIDE)]
    both = pl.ds(0, 2 * SIDE)
    last = pl.ds(2 * SIDE, LAST)
    last_spans = [pl.ds(2 * SIDE, LAST // 2), pl.ds(2 * SIDE + LAST // 2, LAST // 2)]

    def owner_of(k, yy, xx):
        return chunk_z(k) * 4 + yy * 2 + xx

    def first_copy(axis, k, j):
        if axis == 0:
            owner = owner_of(k, 1 - y if j == 0 else y, 1 - x)
        else:
            owner = owner_of(k, 1 - y, 1 - x if j == 0 else x)
        return send(
            part.at[owner, spans[axis]], first_in.at[axis, k, j],
            first_send.at[axis, k, j], first_recv.at[axis, k, j],
            x_peer if axis == 0 else y_peer, mode,
        )

    def second_owner(axis, k):
        return owner_of(k, 1 - y, x) if axis == 0 else owner_of(k, y, 1 - x)

    def second_copy(axis, k):
        return send(
            part.at[second_owner(axis, k), spans[axis]], second_in.at[axis, k],
            second_send.at[axis, k], second_recv.at[axis, k],
            y_peer if axis == 0 else x_peer, mode,
        )

    firsts = {(a, k, j): first_copy(a, k, j) for a in range(2) for k in range(4) for j in range(2)}
    seconds = {(a, k): second_copy(a, k) for a in range(2) for k in range(4)}

    def f32(value):
        return value.astype(jnp.float32)

    def start_first(k):
        for j in range(2):
            for a in range(2):
                firsts[a, k, j].start()

    def forward(k):
        for a in range(2):
            firsts[a, k, 0].wait_recv()
            owner = second_owner(a, k)
            part[owner, spans[a]] = (
                f32(part[owner, spans[a]]) + f32(first_in[a, k, 0])
            ).astype(jnp.bfloat16)
            seconds[a, k].start()

    def line_copy(k, to):
        owner = owner_of(k, y, x)
        if to == "outer":
            dst, sem = outer_in.at[k], outer_recv.at[k]
        elif to == "inner":
            dst, sem = inner_in.at[k], inner_recv.at[k]
        else:
            dst, sem = end_in, end_recv
        return send(
            part.at[owner, both], dst, line_send.at[k], sem,
            outer_peer if to == "end" else inner_peer, mode,
        )

    def keep(k):
        owner = owner_of(k, y, x)
        for a in range(2):
            firsts[a, k, 1].wait_recv()
            seconds[a, k].wait_recv()
            value = (
                f32(part[owner, spans[a]]) + f32(first_in[a, k, 1]) + f32(second_in[a, k])
            )
            if k >= 2:
                @pl.when(is_mid if k == 2 else is_end)
                def _():
                    total[spans[a], :] = value
            part[owner, spans[a]] = value.astype(jnp.bfloat16)
        if k < 3:
            @pl.when(is_end)
            def _():
                line_copy(k, "outer").start()

    def pass_on(k):
        owner = owner_of(k, y, x)

        @pl.when(is_mid)
        def _():
            if k < 2:
                line_copy(k, "outer").wait_recv()
                arrived = outer_in[k]
            else:
                line_copy(0, "inner").wait_recv()
                arrived = inner_in[0]
            part[owner, both] = (f32(part[owner, both]) + f32(arrived)).astype(jnp.bfloat16)
            line_copy(k, "inner" if k < 2 else "end").start()

    def last_copy(k, to):
        owners = pl.ds(chunk_z(k) * 4, 4)
        if to == "outer":
            dst, sem = last_outer_in.at[k], last_outer_recv.at[k]
        elif to == "inner":
            dst, sem = last_inner_in.at[k], last_inner_recv.at[k]
        else:
            dst, sem = last_end_in, last_end_recv
        return send(
            part.at[owners, last], dst, last_send.at[k], sem,
            outer_peer if to == "end" else inner_peer, mode,
        )

    def last_begin(k):
        @pl.when(is_end)
        def _():
            last_copy(k, "outer").start()

    def last_add(k, terms):
        first = chunk_z(k) * 4
        for i in range(4):
            value = f32(part[first + i, last])
            for term in terms:
                value = value + f32(term[i])
            part[first + i, last] = value.astype(jnp.bfloat16)

    def last_pass(k):
        @pl.when(is_mid)
        def _():
            if k < 2:
                last_copy(k, "outer").wait_recv()
                last_add(k, [last_outer_in.at[k]])
                last_copy(k, "inner").start()
            else:
                last_copy(0, "inner").wait_recv()
                last_add(k, [last_inner_in.at[0]])
                last_copy(k, "end").start()

    def last_first_copy(axis, j):
        if axis == 0:
            owner = z * 4 + (1 - y if j == 0 else y) * 2 + 1 - x
        else:
            owner = z * 4 + (1 - y) * 2 + (1 - x if j == 0 else x)
        return send(
            part.at[owner, last_spans[axis]], last_first_in.at[axis, j],
            last_first_send.at[axis, j], last_first_recv.at[axis, j],
            x_peer if axis == 0 else y_peer, mode,
        )

    def last_second_owner(axis):
        return z * 4 + (1 - y) * 2 + x if axis == 0 else z * 4 + y * 2 + 1 - x

    def last_second_copy(axis):
        return send(
            part.at[last_second_owner(axis), last_spans[axis]], last_second_in.at[axis],
            last_second_send.at[axis], last_second_recv.at[axis],
            y_peer if axis == 0 else x_peer, mode,
        )

    last_firsts = {(a, j): last_first_copy(a, j) for a in range(2) for j in range(2)}
    last_seconds = [last_second_copy(a) for a in range(2)]

    def last_spread():
        @pl.when(is_mid)
        def _():
            last_copy(2, "outer").wait_recv()
            last_copy(1, "inner").wait_recv()
            last_add(2, [last_outer_in.at[2], last_inner_in.at[1]])

        @pl.when(is_end)
        def _():
            last_copy(3, "end").wait_recv()
            last_add(3, [last_end_in])

        for j in range(2):
            for a in range(2):
                last_firsts[a, j].start()

    def last_forward():
        for a in range(2):
            last_firsts[a, 0].wait_recv()
            owner = last_second_owner(a)
            part[owner, last_spans[a]] = (
                f32(part[owner, last_spans[a]]) + f32(last_first_in[a, 0])
            ).astype(jnp.bfloat16)
            last_seconds[a].start()

    def last_keep():
        for a in range(2):
            last_firsts[a, 1].wait_recv()
            last_seconds[a].wait_recv()
            total[last_spans[a], :] = (
                f32(part[pix, last_spans[a]]) + f32(last_first_in[a, 1]) + f32(last_second_in[a])
            )

    rest = (FAR - 1) * GROUP
    ring = pix % 4 * 4 + z

    def chip_at(step):
        there = (ring + step) % 16
        return there % 4 * 4 + there // 4

    def cross_copy(at, size, index):
        rows_at = pl.ds(at, size)
        return send(
            cross_out.at[rows_at], cross_in.at[rows_at],
            cross_send.at[index], cross_recv.at[index], pix, 1 - mode,
        )

    cross_rest = cross_copy(0, rest, 0)
    cross_early = cross_copy(rest, GROUP, 1)
    turns = [
        send(
            turn_out.at[d - 1], turn_in.at[d - 1], turn_send.at[d - 1], turn_recv.at[d - 1],
            chip_at(d), mode,
        )
        for d in range(1, FAR + 1)
    ]

    def start_turn(d):
        stacked = jnp.concatenate(
            [
                total[d * GROUP:(d + 1) * GROUP, 0:128].astype(jnp.bfloat16),
                cross_in[(d - 1) * GROUP:d * GROUP, :],
            ],
            axis=0,
        )
        turn_out[d - 1] = stacked.T
        turns[d - 1].start()

    for k in range(3):
        multiply(k)
        last_begin(k)
    positions = pix * pixel_rows + lax.broadcasted_iota(
        jnp.int32, (pixels_ref.shape[1], pixel_rows), 1
    )
    listed = jnp.broadcast_to(pixels_ref[...], (8, pixels_ref.shape[1])).T[:, 0:1]
    counts = jnp.sum(
        jnp.where(listed == positions, 1.0, 0.0), axis=0, keepdims=True
    )
    nothing = jnp.zeros_like(counts)
    row = lax.broadcasted_iota(jnp.int32, (16, 2 * pixel_rows), 0)
    real_weight = jnp.concatenate([counts, nothing], axis=1)
    imag_weight = jnp.concatenate([nothing, counts], axis=1)
    weight = jnp.where(row == 0, real_weight, jnp.where(row == 1, imag_weight, 0.0))
    weight = weight.astype(jnp.bfloat16)
    for pair in range(8):
        places = [(p % 4 * 4 + p // 4) * GROUP for p in (2 * pair, 2 * pair + 1)]
        block = jnp.concatenate([own[pl.ds(at, GROUP), :] for at in places], axis=0)
        ref_out[0, :, pl.ds(pair * 128, 128)] = lax.dot_general(
            weight, block, contract, preferred_element_type=jnp.float32
        )[0:8]
    ref_copies[0].start()
    forward(0)
    start_first(2)
    multiply(3)
    ref_next(0)
    last_pass(0)
    forward(1)
    start_first(3)
    last_pass(1)
    ref_next(1)
    keep(0)
    forward(2)
    last_pass(3)
    ref_next(2)
    last_spread()
    keep(1)
    pass_on(0)
    ref_next(3)
    forward(3)
    last_forward()
    keep(2)
    pass_on(1)
    last_keep()
    cross_out[rest:] = total[FAR * GROUP:NEAR * GROUP - GROUP, 128:256].astype(jnp.bfloat16)
    cross_early.start()
    keep(3)
    pass_on(3)

    cross_early.wait_recv()
    start_turn(FAR)

    @pl.when(is_mid)
    def _():
        line_copy(2, "outer").wait_recv()
        line_copy(1, "inner").wait_recv()
        total[both, :] = total[both, :] + f32(outer_in[2]) + f32(inner_in[1])

    @pl.when(is_end)
    def _():
        line_copy(3, "end").wait_recv()
        total[both, :] = total[both, :] + f32(end_in[...])

    cross_out[0:rest] = total[GROUP:FAR * GROUP, 128:256].astype(jnp.bfloat16)
    cross_rest.start()

    lane = lax.broadcasted_iota(jnp.int32, (GROUP, 128), 1)
    low = lane < GROUP

    def group_rows(step):
        return pl.ds(pl.multiple_of(chip_at(step) * GROUP, GROUP), GROUP)

    for d in range(NEAR):
        here = total[d * GROUP:(d + 1) * GROUP, 0:128]
        there = total[d * GROUP:(d + 1) * GROUP, 128:256]
        gram_ref[0, group_rows(d), :] = jnp.where(low, here, pltpu.roll(there, GROUP, 1))
        gram_ref[1, group_rows(d), :] = jnp.where(low, pltpu.roll(here, GROUP, 1), there)

    cross_rest.wait_recv()
    for d in range(1, FAR):
        start_turn(d)
    ref_copies[4].wait_recv()
    sums_ref[0] = ref_out[4]
    sums_ref[1] = ref_in[4]
    for d in range(1, FAR + 1):
        turns[d - 1].wait_recv()
        arrived = f32(turn_in[d - 1])
        gram_ref[0, group_rows(16 - d), :] = arrived[0:GROUP]
        gram_ref[1, group_rows(16 - d), :] = -arrived[GROUP:]

    for copy in field_copies + ref_copies + list(firsts.values()) + list(seconds.values()):
        copy.wait_send()
    for copy in turns + [cross_rest, cross_early] + list(last_firsts.values()) + last_seconds:
        copy.wait_send()
    for k in range(3):
        @pl.when(is_end | (k < 2))
        def _():
            line_copy(k, "outer").wait_send()
            last_copy(k, "outer").wait_send()

    @pl.when(is_mid)
    def _():
        line_copy(3, "end").wait_send()
        last_copy(3, "end").wait_send()


def finish_kernel(pixel_scale, gram_ref, sums_ref, band_ref, diag_ref):
    pix = lax.axis_index("pix")
    odd = pix % 2 == 1
    at = pl.multiple_of((pix // 2) * 128, 128)
    own = sums_ref[0, :, pl.ds(at, 128)]
    other = sums_ref[1, :, pl.ds(at, 128)]
    low = lax.broadcasted_iota(jnp.int32, own.shape, 1) < GROUP
    own = jnp.where(odd, pltpu.roll(own, GROUP, 1), own)
    other = jnp.where(odd, other, pltpu.roll(other, GROUP, 1))
    cols = jnp.where(low, own, other).T

    def unit(real, imag):
        magnitude = jnp.maximum(jnp.sqrt(real * real + imag * imag), 1.0)
        return real / magnitude, imag / magnitude

    col_real, col_imag = unit(cols[:, 0:1], cols[:, 1:2])
    row_real, row_imag = unit(sums_ref[0, 0:1, :], sums_ref[0, 1:2, :])
    unit_real = row_real * col_real + row_imag * col_imag
    unit_imag = row_imag * col_real - row_real * col_imag
    gram_real = gram_ref[0].T
    gram_imag = gram_ref[1].T
    real = (unit_real * gram_real - unit_imag * gram_imag) * pixel_scale
    imag = (unit_real * gram_imag + unit_imag * gram_real) * pixel_scale
    diag_ref[0] = real[:GROUP]
    diag_ref[1] = imag[:GROUP]
    band_ref[0] = real[GROUP:]
    band_ref[1] = imag[GROUP:]


def paired_shards(frames, ref_pixels):
    pixel_rows = frames.shape[1]
    width = frames.shape[2]
    rows = NEAR * GROUP
    b16 = jnp.bfloat16
    dma = pltpu.SemaphoreType.DMA
    gram, sums = pl.pallas_call(
        gram_kernel,
        out_shape=(
            jax.ShapeDtypeStruct((2, width, 128), jnp.float32),
            jax.ShapeDtypeStruct((2, 8, width), jnp.float32),
        ),
        in_specs=[
            pl.BlockSpec(memory_space=pltpu.HBM),
            pl.BlockSpec(memory_space=pltpu.VMEM),
        ],
        out_specs=(pl.BlockSpec(memory_space=pltpu.VMEM),) * 2,
        scratch_shapes=[
            pltpu.VMEM((4, 4, pixel_rows, 4 * GROUP), b16),
            pltpu.VMEM((width + 8 * GROUP, 2 * pixel_rows), b16),
            pltpu.VMEM((width, 2 * pixel_rows), b16),
            pltpu.VMEM((16, rows, 256), b16),
            pltpu.VMEM((2, 4, 2, SIDE, 256), b16),
            pltpu.VMEM((2, 4, SIDE, 256), b16),
            pltpu.VMEM((3, 2 * SIDE, 256), b16),
            pltpu.VMEM((2, 2 * SIDE, 256), b16),
            pltpu.VMEM((2 * SIDE, 256), b16),
            pltpu.VMEM((3, 4, LAST, 256), b16),
            pltpu.VMEM((2, 4, LAST, 256), b16),
            pltpu.VMEM((4, LAST, 256), b16),
            pltpu.VMEM((2, 2, LAST // 2, 256), b16),
            pltpu.VMEM((2, LAST // 2, 256), b16),
            pltpu.VMEM((5, 8, width), jnp.float32),
            pltpu.VMEM((5, 8, width), jnp.float32),
            pltpu.VMEM((rows, 256), jnp.float32),
            pltpu.VMEM((FAR * GROUP, 128), b16),
            pltpu.VMEM((FAR * GROUP, 128), b16),
            pltpu.VMEM((FAR, 128, 128), b16),
            pltpu.VMEM((FAR, 128, 128), b16),
            dma((4,)), dma((4, 4)), dma((4, 4)),
            dma((2, 4, 2)), dma((2, 4, 2)),
            dma((2, 4)), dma((2, 4)),
            dma((4,)), dma((3,)), dma((2,)), dma,
            dma((4,)), dma((3,)), dma((2,)), dma,
            dma((2, 2)), dma((2, 2)), dma((2,)), dma((2,)),
            dma((5,)), dma((5,)),
            dma((2,)), dma((2,)),
            dma((FAR,)), dma((FAR,)),
        ],
        compiler_params=pltpu.CompilerParams(
            collective_id=0, has_side_effects=True, vmem_limit_bytes=52 * 1024 * 1024
        ),
    )(frames, ref_pixels.reshape(1, -1))
    pixel_scale = 1.0 / math.sqrt(lax.axis_size("pix") * pixel_rows)
    band, diag = pl.pallas_call(
        functools.partial(finish_kernel, pixel_scale),
        out_shape=(jax.ShapeDtypeStruct((2, GROUP, width), jnp.float32),) * 2,
        in_specs=[pl.BlockSpec(memory_space=pltpu.VMEM)] * 2,
        out_specs=(pl.BlockSpec(memory_space=pltpu.VMEM),) * 2,
    )(gram, sums)
    return (jnp.swapaxes(band, 1, 2), jnp.swapaxes(diag, 1, 2))


def solution(mesh):
    placed = (P(None, "pix", "mode"), P())
    paired = mesh.shape["pix"] == 16 and mesh.shape["mode"] == 2

    def body(frames, ref_pixels):
        if paired and frames.shape[2] == 16 * GROUP:
            return paired_shards(frames, ref_pixels)
        return shards(frames, ref_pixels)

    return jax.shard_map(
        body,
        mesh=mesh,
        in_specs=placed,
        out_specs=(P(None, "mode", "pix"), P(None, "mode", "pix")),
        check_vma=False,
    )
```

```python
import functools
import math

import jax
import jax.numpy as jnp
from jax import lax
from jax.experimental import pallas as pl
from jax.experimental.pallas import tpu as pltpu
from jax.sharding import PartitionSpec as P


def unit_phase(sums):
    magnitude = jnp.maximum(jnp.sqrt(sums[0] * sums[0] + sums[1] * sums[1]), 1.0)
    return sums / magnitude[None, :]


def rotate(gram_real, gram_imag, phase_rows, phase_cols, pixel_scale):
    row_real = phase_rows[0][:, None]
    row_imag = phase_rows[1][:, None]
    col_real = phase_cols[0][None, :]
    col_imag = phase_cols[1][None, :]
    unit_real = row_real * col_real + row_imag * col_imag
    unit_imag = row_imag * col_real - row_real * col_imag
    return jnp.stack(
        [
            (unit_real * gram_real - unit_imag * gram_imag) * pixel_scale,
            (unit_real * gram_imag + unit_imag * gram_real) * pixel_scale,
        ]
    )


def shards(frames, ref_pixels):
    pix_count = lax.axis_size("pix")
    mode_count = lax.axis_size("mode")
    pix_index = lax.axis_index("pix")
    mode_index = lax.axis_index("mode")
    pixel_rows = frames.shape[1]
    block_width = frames.shape[2]
    full_tiles = mode_count // 2 + 1
    full_width = full_tiles * block_width
    frame_float = frames.astype(jnp.float32)
    real_part = (frame_float[0] - frame_float[2]).astype(jnp.bfloat16)
    imag_part = (frame_float[3] - frame_float[1]).astype(jnp.bfloat16)
    fields = jnp.stack([real_part, imag_part])
    positions = pix_index * pixel_rows + lax.iota(jnp.int32, pixel_rows)
    counts = jnp.sum(
        (ref_pixels[:, None] == positions[None, :]).astype(jnp.float32), axis=0
    ).astype(jnp.bfloat16)
    local_ref = jnp.einsum("p,cpm->cm", counts, fields, preferred_element_type=jnp.float32)
    own_ref = lax.psum(local_ref, "pix")
    phase_all = lax.all_gather(unit_phase(own_ref), "mode", axis=1, tiled=True)
    phase_own = lax.dynamic_slice_in_dim(phase_all, mode_index * block_width, block_width, 1)
    phase_twice = jnp.concatenate([phase_all, phase_all], axis=1)
    phase_full = lax.dynamic_slice_in_dim(phase_twice, mode_index * block_width, full_width, 1)
    whole_fields = lax.all_gather(fields, "mode", axis=2, tiled=True)
    tiled = whole_fields.reshape(2, pixel_rows, mode_count, block_width)
    picked = (mode_index + lax.iota(jnp.int32, full_tiles)) % mode_count
    band_fields = jnp.take(tiled, picked, axis=2).reshape(2, pixel_rows, full_width)
    contract = (((0,), (0,)), ((), ()))
    own_real = fields[0]
    own_imag = fields[1]
    band_real = band_fields[0]
    band_imag = band_fields[1]
    gram_real = lax.dot_general(
        own_real, band_real, contract, preferred_element_type=jnp.float32
    ) + lax.dot_general(own_imag, band_imag, contract, preferred_element_type=jnp.float32)
    gram_imag = lax.dot_general(
        own_real, band_imag, contract, preferred_element_type=jnp.float32
    ) - lax.dot_general(own_imag, band_real, contract, preferred_element_type=jnp.float32)
    pixel_scale = 1.0 / math.sqrt(pix_count * pixel_rows)
    raw_terms = jnp.stack([gram_real, gram_imag])
    raw_diag, raw_band = (
        lax.psum_scatter(raw_terms[:, :, :block_width], "pix", scatter_dimension=2, tiled=True),
        lax.psum_scatter(raw_terms[:, :, block_width:], "pix", scatter_dimension=2, tiled=True),
    )
    diag_slice = block_width // pix_count
    band_slice = (full_width - block_width) // pix_count
    diag_cols = lax.dynamic_slice_in_dim(phase_full, pix_index * diag_slice, diag_slice, 1)
    band_cols = lax.dynamic_slice_in_dim(
        phase_full, block_width + pix_index * band_slice, band_slice, 1
    )
    diag_out = rotate(raw_diag[0], raw_diag[1], phase_own, diag_cols, pixel_scale)
    band_out = rotate(raw_band[0], raw_band[1], phase_own, band_cols, pixel_scale)
    return (band_out, diag_out)


MESH = pl.DeviceIdType.MESH
GROUP = 64
NEAR = 9
SIDE = 224
EARLY = 3
LAST = 128
FAR = 7


def gram_kernel(
    frames_hbm, pixels_ref, gram_ref, sums_ref,
    frames_ref, own, other, part, first_in, second_in, outer_in, inner_in, end_in,
    last_outer_in, last_inner_in, last_end_in, last_first_in, last_second_in,
    ref_out, ref_in, total, cross_out, cross_in, turn_out, turn_in,
    frame_sem, field_send, field_recv, first_send, first_recv, second_send, second_recv,
    line_send, outer_recv, inner_recv, end_recv,
    last_send, last_outer_recv, last_inner_recv, last_end_recv,
    last_first_send, last_first_recv, last_second_send, last_second_recv, ref_send, ref_recv,
    cross_send, cross_recv, turn_send, turn_recv,
):
    pix = lax.axis_index("pix")
    mode = lax.axis_index("mode")
    x, y, z = pix % 2, (pix // 2) % 2, pix // 4
    upper = z >= 2
    is_end = (z == 0) | (z == 3)
    is_mid = (z == 1) | (z == 2)
    x_peer = pix + 1 - 2 * x
    y_peer = pix + 2 - 4 * y
    inner_peer = jnp.where(upper, pix - 4, pix + 4)
    outer_peer = jnp.where(upper, pix + 4, pix - 4)
    z_even_peer = pix + 4 - 8 * (z % 2)
    z_far_peer = pix + 8 - 16 * (z // 2)
    pixel_rows = frames_hbm.shape[1]
    width = frames_hbm.shape[2]
    rows = NEAR * GROUP
    chunk = 4 * GROUP

    def chunk_z(k):
        return jnp.where(upper, k, 3 - k)

    def chunk_modes(k):
        return pl.ds(pl.multiple_of(chunk_z(k) * chunk, chunk), chunk)

    loads = [
        pltpu.make_async_copy(
            frames_hbm.at[:, :, chunk_modes(k)], frames_ref.at[k], frame_sem.at[k]
        )
        for k in range(4)
    ]
    for load in loads:
        load.start()
    barrier = pltpu.get_barrier_semaphore()
    for step in range(1, 16):
        pl.semaphore_signal(
            barrier, inc=1, device_id=((pix + step) % 16, mode), device_id_type=MESH
        )
    pl.semaphore_signal(barrier, inc=1, device_id=(pix, 1 - mode), device_id_type=MESH)

    def send(src, dst, send_sem, recv_sem, to_pix, to_mode):
        copy = pltpu.make_async_remote_copy(
            src_ref=src, dst_ref=dst, send_sem=send_sem, recv_sem=recv_sem,
            device_id=(to_pix, to_mode), device_id_type=MESH,
        )
        return copy

    def ring_rows(zz, column):
        return pl.ds(pl.multiple_of((column * 4 + zz) * GROUP, GROUP), GROUP)

    for k in range(4):
        loads[k].wait()
        frame = [frames_ref[k, step].astype(jnp.float32) for step in range(4)]
        real = (frame[0] - frame[2]).astype(jnp.bfloat16).T
        imag = (frame[3] - frame[1]).astype(jnp.bfloat16).T
        for i in range(4):
            to = ring_rows(chunk_z(k), i)
            own[to, 0:pixel_rows] = real[i * GROUP:(i + 1) * GROUP]
            own[to, pixel_rows:2 * pixel_rows] = imag[i * GROUP:(i + 1) * GROUP]
    own[pl.ds(width, 8 * GROUP), :] = own[pl.ds(0, 8 * GROUP), :]
    pl.semaphore_wait(barrier, 16)

    def field_copy(k, i):
        at = ring_rows(chunk_z(k), i)
        return send(
            own.at[at], other.at[at], field_send.at[k, i], field_recv.at[k, i], pix, 1 - mode
        )

    field_copies = [field_copy(k, i) for k in range(4) for i in range(4)]
    for copy in field_copies:
        copy.start()

    ref_peers = [x_peer, y_peer, z_even_peer, z_far_peer, pix]

    def ref_copy(step):
        return send(
            ref_out.at[step], ref_in.at[step], ref_send.at[step], ref_recv.at[step],
            ref_peers[step], mode if step < 4 else 1 - mode,
        )

    ref_copies = [ref_copy(step) for step in range(5)]

    def ref_next(step):
        ref_copies[step].wait_recv()
        ref_out[step + 1] = ref_out[step] + ref_in[step]
        ref_copies[step + 1].start()

    contract = (((1,), (1,)), ((), ()))

    def turned(block):
        return jnp.concatenate([block[:, pixel_rows:], -block[:, :pixel_rows]], axis=1)

    def multiply(k):
        zc = chunk_z(k)
        for i in range(4):
            field_copies[4 * k + i].wait_recv()
        for t in range(4):
            column = (1 - y if t % 2 == 0 else y) * 2 + (1 - x if t < 2 else x)
            start = pl.multiple_of((column * 4 + zc) * GROUP, GROUP)
            own_cols = own[pl.ds(start, GROUP), :]
            other_cols = other[pl.ds(start, GROUP), :]
            cols = jnp.concatenate(
                [own_cols, turned(own_cols), other_cols, turned(other_cols)], axis=0
            )
            left = own[pl.ds(start, rows), :]
            out = lax.dot_general(left, cols, contract, preferred_element_type=jnp.float32)
            part[zc * 4 + column] = out.astype(jnp.bfloat16)
            if k < 2:
                for a, j in (((0, 0), (1, 0)), ((0, 1),), ((1, 1),), ())[t]:
                    firsts[a, 0, k, j].start()

    late_rows = EARLY * GROUP
    wave_rows = [(late_rows, 2 * SIDE - late_rows), (0, late_rows)]
    spans = [
        [pl.ds(at, size // 2), pl.ds(at + size // 2, size // 2)] for at, size in wave_rows
    ]
    slots = [pl.ds(at // 2, size // 2) for at, size in wave_rows]
    boths = [pl.ds(at, size) for at, size in wave_rows]
    last = pl.ds(2 * SIDE, LAST)
    last_spans = [pl.ds(2 * SIDE, LAST // 2), pl.ds(2 * SIDE + LAST // 2, LAST // 2)]

    def owner_of(k, yy, xx):
        return chunk_z(k) * 4 + yy * 2 + xx

    def first_copy(axis, w, k, j):
        if axis == 0:
            owner = owner_of(k, 1 - y if j == 0 else y, 1 - x)
        else:
            owner = owner_of(k, 1 - y, 1 - x if j == 0 else x)
        return send(
            part.at[owner, spans[w][axis]], first_in.at[axis, k, j, slots[w]],
            first_send.at[axis, w, k, j], first_recv.at[axis, w, k, j],
            x_peer if axis == 0 else y_peer, mode,
        )

    def second_owner(axis, k):
        return owner_of(k, 1 - y, x) if axis == 0 else owner_of(k, y, 1 - x)

    def second_copy(axis, w, k):
        return send(
            part.at[second_owner(axis, k), spans[w][axis]], second_in.at[axis, k, slots[w]],
            second_send.at[axis, w, k], second_recv.at[axis, w, k],
            y_peer if axis == 0 else x_peer, mode,
        )

    steps = [(w, k) for w in range(2) for k in range(4)]
    firsts = {
        (a, w, k, j): first_copy(a, w, k, j) for a in range(2) for w, k in steps for j in range(2)
    }
    seconds = {(a, w, k): second_copy(a, w, k) for a in range(2) for w, k in steps}

    def f32(value):
        return value.astype(jnp.float32)

    def start_first(step):
        w, k = steps[step]
        for j in range(2):
            for a in range(2):
                firsts[a, w, k, j].start()

    def forward(step):
        w, k = steps[step]
        for a in range(2):
            firsts[a, w, k, 0].wait_recv()
            owner = second_owner(a, k)
            span = spans[w][a]
            part[owner, span] = (
                f32(part[owner, span]) + f32(first_in[a, k, 0, slots[w]])
            ).astype(jnp.bfloat16)
            seconds[a, w, k].start()

    def line_copy(w, k, to):
        owner = owner_of(k, y, x)
        both = boths[w]
        if to == "outer":
            dst, sem = outer_in.at[k, both], outer_recv.at[w, k]
        elif to == "inner":
            dst, sem = inner_in.at[k, both], inner_recv.at[w, k]
        else:
            dst, sem = end_in.at[both], end_recv.at[w]
        return send(
            part.at[owner, both], dst, line_send.at[w, k], sem,
            outer_peer if to == "end" else inner_peer, mode,
        )

    def keep(step):
        w, k = steps[step]
        owner = owner_of(k, y, x)
        for a in range(2):
            firsts[a, w, k, 1].wait_recv()
            seconds[a, w, k].wait_recv()
            span = spans[w][a]
            value = (
                f32(part[owner, span])
                + f32(first_in[a, k, 1, slots[w]])
                + f32(second_in[a, k, slots[w]])
            )
            if k >= 2:
                @pl.when(is_mid if k == 2 else is_end)
                def _():
                    total[span, :] = value
            part[owner, span] = value.astype(jnp.bfloat16)
        if k < 3:
            @pl.when(is_end)
            def _():
                line_copy(w, k, "outer").start()

    def pass_on(step):
        w, k = steps[step]
        owner = owner_of(k, y, x)
        both = boths[w]

        @pl.when(is_mid)
        def _():
            if k < 2:
                line_copy(w, k, "outer").wait_recv()
                arrived = outer_in[k, both]
            else:
                line_copy(w, 0, "inner").wait_recv()
                arrived = inner_in[0, both]
            part[owner, both] = (f32(part[owner, both]) + f32(arrived)).astype(jnp.bfloat16)
            line_copy(w, k, "inner" if k < 2 else "end").start()

    def line_end(w):
        both = boths[w]

        @pl.when(is_mid)
        def _():
            line_copy(w, 2, "outer").wait_recv()
            line_copy(w, 1, "inner").wait_recv()
            total[both, :] = total[both, :] + f32(outer_in[2, both]) + f32(inner_in[1, both])

        @pl.when(is_end)
        def _():
            line_copy(w, 3, "end").wait_recv()
            total[both, :] = total[both, :] + f32(end_in[both])

    def last_copy(k, to):
        owners = pl.ds(chunk_z(k) * 4, 4)
        if to == "outer":
            dst, sem = last_outer_in.at[k], last_outer_recv.at[k]
        elif to == "inner":
            dst, sem = last_inner_in.at[k], last_inner_recv.at[k]
        else:
            dst, sem = last_end_in, last_end_recv
        return send(
            part.at[owners, last], dst, last_send.at[k], sem,
            outer_peer if to == "end" else inner_peer, mode,
        )

    def last_begin(k):
        @pl.when(is_end)
        def _():
            last_copy(k, "outer").start()

    def last_add(k, terms):
        first = chunk_z(k) * 4
        for i in range(4):
            value = f32(part[first + i, last])
            for term in terms:
                value = value + f32(term[i])
            part[first + i, last] = value.astype(jnp.bfloat16)

    def last_pass(k):
        @pl.when(is_mid)
        def _():
            if k < 2:
                last_copy(k, "outer").wait_recv()
                last_add(k, [last_outer_in.at[k]])
                last_copy(k, "inner").start()
            else:
                last_copy(0, "inner").wait_recv()
                last_add(k, [last_inner_in.at[0]])
                last_copy(k, "end").start()

    def last_first_copy(axis, j):
        if axis == 0:
            owner = z * 4 + (1 - y if j == 0 else y) * 2 + 1 - x
        else:
            owner = z * 4 + (1 - y) * 2 + (1 - x if j == 0 else x)
        return send(
            part.at[owner, last_spans[axis]], last_first_in.at[axis, j],
            last_first_send.at[axis, j], last_first_recv.at[axis, j],
            x_peer if axis == 0 else y_peer, mode,
        )

    def last_second_owner(axis):
        return z * 4 + (1 - y) * 2 + x if axis == 0 else z * 4 + y * 2 + 1 - x

    def last_second_copy(axis):
        return send(
            part.at[last_second_owner(axis), last_spans[axis]], last_second_in.at[axis],
            last_second_send.at[axis], last_second_recv.at[axis],
            y_peer if axis == 0 else x_peer, mode,
        )

    last_firsts = {(a, j): last_first_copy(a, j) for a in range(2) for j in range(2)}
    last_seconds = [last_second_copy(a) for a in range(2)]

    def last_spread():
        @pl.when(is_mid)
        def _():
            last_copy(2, "outer").wait_recv()
            last_copy(1, "inner").wait_recv()
            last_add(2, [last_outer_in.at[2], last_inner_in.at[1]])

        @pl.when(is_end)
        def _():
            last_copy(3, "end").wait_recv()
            last_add(3, [last_end_in])

        for j in range(2):
            for a in range(2):
                last_firsts[a, j].start()

    def last_forward():
        for a in range(2):
            last_firsts[a, 0].wait_recv()
            owner = last_second_owner(a)
            part[owner, last_spans[a]] = (
                f32(part[owner, last_spans[a]]) + f32(last_first_in[a, 0])
            ).astype(jnp.bfloat16)
            last_seconds[a].start()

    def last_keep():
        for a in range(2):
            last_firsts[a, 1].wait_recv()
            last_seconds[a].wait_recv()
            total[last_spans[a], :] = (
                f32(part[pix, last_spans[a]]) + f32(last_first_in[a, 1]) + f32(last_second_in[a])
            )

    ring = pix % 4 * 4 + z

    def chip_at(step):
        there = (ring + step) % 16
        return there % 4 * 4 + there // 4

    def cross_copy(at, size, index):
        rows_at = pl.ds(at, size)
        return send(
            cross_out.at[rows_at], cross_in.at[rows_at],
            cross_send.at[index], cross_recv.at[index], pix, 1 - mode,
        )

    cross_rows = [(FAR, FAR + 1), (EARLY, FAR), (1, EARLY)]
    crosses = [
        cross_copy((first - 1) * GROUP, (end - first) * GROUP, i)
        for i, (first, end) in enumerate(cross_rows)
    ]

    def start_cross(i):
        first, end = cross_rows[i]
        cross_out[(first - 1) * GROUP:(end - 1) * GROUP] = total[
            first * GROUP:end * GROUP, 128:256
        ].astype(jnp.bfloat16)
        crosses[i].start()

    def mirror(i):
        crosses[i].wait_recv()
        for d in range(*cross_rows[i]):
            start_turn(d)

    turns = [
        send(
            turn_out.at[d - 1], turn_in.at[d - 1], turn_send.at[d - 1], turn_recv.at[d - 1],
            chip_at(d), mode,
        )
        for d in range(1, FAR + 1)
    ]

    def start_turn(d):
        stacked = jnp.concatenate(
            [
                total[d * GROUP:(d + 1) * GROUP, 0:128].astype(jnp.bfloat16),
                cross_in[(d - 1) * GROUP:d * GROUP, :],
            ],
            axis=0,
        )
        turn_out[d - 1] = stacked.T
        turns[d - 1].start()

    for k in range(3):
        multiply(k)
        last_begin(k)
    positions = pix * pixel_rows + lax.broadcasted_iota(
        jnp.int32, (pixels_ref.shape[1], pixel_rows), 1
    )
    listed = jnp.broadcast_to(pixels_ref[...], (8, pixels_ref.shape[1])).T[:, 0:1]
    counts = jnp.sum(
        jnp.where(listed == positions, 1.0, 0.0), axis=0, keepdims=True
    )
    nothing = jnp.zeros_like(counts)
    row = lax.broadcasted_iota(jnp.int32, (16, 2 * pixel_rows), 0)
    real_weight = jnp.concatenate([counts, nothing], axis=1)
    imag_weight = jnp.concatenate([nothing, counts], axis=1)
    weight = jnp.where(row == 0, real_weight, jnp.where(row == 1, imag_weight, 0.0))
    weight = weight.astype(jnp.bfloat16)
    for pair in range(8):
        places = [(p % 4 * 4 + p // 4) * GROUP for p in (2 * pair, 2 * pair + 1)]
        block = jnp.concatenate([own[pl.ds(at, GROUP), :] for at in places], axis=0)
        ref_out[0, :, pl.ds(pair * 128, 128)] = lax.dot_general(
            weight, block, contract, preferred_element_type=jnp.float32
        )[0:8]
    ref_copies[0].start()
    forward(0)
    start_first(2)
    multiply(3)
    ref_next(0)
    last_pass(0)
    forward(1)
    start_first(3)
    last_pass(1)
    ref_next(1)
    keep(0)
    forward(2)
    start_first(4)
    last_pass(3)
    ref_next(2)
    last_spread()
    keep(1)
    pass_on(0)
    ref_next(3)
    forward(3)
    start_first(5)
    last_forward()
    keep(2)
    pass_on(1)
    forward(4)
    start_first(6)
    last_keep()
    start_cross(0)
    keep(3)
    pass_on(3)
    forward(5)
    start_first(7)
    mirror(0)
    keep(4)
    forward(6)
    line_end(0)
    start_cross(1)
    keep(5)
    pass_on(4)
    forward(7)
    keep(6)
    pass_on(5)
    mirror(1)
    keep(7)
    pass_on(7)
    line_end(1)
    start_cross(2)

    lane = lax.broadcasted_iota(jnp.int32, (GROUP, 128), 1)
    low = lane < GROUP

    def group_rows(step):
        return pl.ds(pl.multiple_of(chip_at(step) * GROUP, GROUP), GROUP)

    for d in range(NEAR):
        here = total[d * GROUP:(d + 1) * GROUP, 0:128]
        there = total[d * GROUP:(d + 1) * GROUP, 128:256]
        gram_ref[0, group_rows(d), :] = jnp.where(low, here, pltpu.roll(there, GROUP, 1))
        gram_ref[1, group_rows(d), :] = jnp.where(low, pltpu.roll(here, GROUP, 1), there)

    mirror(2)
    ref_copies[4].wait_recv()
    sums_ref[0] = ref_out[4]
    sums_ref[1] = ref_in[4]
    for d in range(1, FAR + 1):
        turns[d - 1].wait_recv()
        arrived = f32(turn_in[d - 1])
        gram_ref[0, group_rows(16 - d), :] = arrived[0:GROUP]
        gram_ref[1, group_rows(16 - d), :] = -arrived[GROUP:]

    for copy in field_copies + ref_copies + list(firsts.values()) + list(seconds.values()):
        copy.wait_send()
    for copy in turns + crosses + list(last_firsts.values()) + last_seconds:
        copy.wait_send()
    for k in range(3):
        @pl.when(is_end | (k < 2))
        def _():
            line_copy(0, k, "outer").wait_send()
            line_copy(1, k, "outer").wait_send()
            last_copy(k, "outer").wait_send()

    @pl.when(is_mid)
    def _():
        line_copy(0, 3, "end").wait_send()
        line_copy(1, 3, "end").wait_send()
        last_copy(3, "end").wait_send()


def finish_kernel(pixel_scale, gram_ref, sums_ref, band_ref, diag_ref):
    pix = lax.axis_index("pix")
    odd = pix % 2 == 1
    at = pl.multiple_of((pix // 2) * 128, 128)
    own = sums_ref[0, :, pl.ds(at, 128)]
    other = sums_ref[1, :, pl.ds(at, 128)]
    low = lax.broadcasted_iota(jnp.int32, own.shape, 1) < GROUP
    own = jnp.where(odd, pltpu.roll(own, GROUP, 1), own)
    other = jnp.where(odd, other, pltpu.roll(other, GROUP, 1))
    cols = jnp.where(low, own, other).T

    def unit(real, imag):
        magnitude = jnp.maximum(jnp.sqrt(real * real + imag * imag), 1.0)
        return real / magnitude, imag / magnitude

    col_real, col_imag = unit(cols[:, 0:1], cols[:, 1:2])
    row_real, row_imag = unit(sums_ref[0, 0:1, :], sums_ref[0, 1:2, :])
    unit_real = row_real * col_real + row_imag * col_imag
    unit_imag = row_imag * col_real - row_real * col_imag
    gram_real = gram_ref[0].T
    gram_imag = gram_ref[1].T
    real = (unit_real * gram_real - unit_imag * gram_imag) * pixel_scale
    imag = (unit_real * gram_imag + unit_imag * gram_real) * pixel_scale
    diag_ref[0] = real[:GROUP]
    diag_ref[1] = imag[:GROUP]
    band_ref[0] = real[GROUP:]
    band_ref[1] = imag[GROUP:]


def paired_shards(frames, ref_pixels):
    pixel_rows = frames.shape[1]
    width = frames.shape[2]
    rows = NEAR * GROUP
    b16 = jnp.bfloat16
    dma = pltpu.SemaphoreType.DMA
    gram, sums = pl.pallas_call(
        gram_kernel,
        out_shape=(
            jax.ShapeDtypeStruct((2, width, 128), jnp.float32),
            jax.ShapeDtypeStruct((2, 8, width), jnp.float32),
        ),
        in_specs=[
            pl.BlockSpec(memory_space=pltpu.HBM),
            pl.BlockSpec(memory_space=pltpu.VMEM),
        ],
        out_specs=(pl.BlockSpec(memory_space=pltpu.VMEM),) * 2,
        scratch_shapes=[
            pltpu.VMEM((4, 4, pixel_rows, 4 * GROUP), b16),
            pltpu.VMEM((width + 8 * GROUP, 2 * pixel_rows), b16),
            pltpu.VMEM((width, 2 * pixel_rows), b16),
            pltpu.VMEM((16, rows, 256), b16),
            pltpu.VMEM((2, 4, 2, SIDE, 256), b16),
            pltpu.VMEM((2, 4, SIDE, 256), b16),
            pltpu.VMEM((3, 2 * SIDE, 256), b16),
            pltpu.VMEM((2, 2 * SIDE, 256), b16),
            pltpu.VMEM((2 * SIDE, 256), b16),
            pltpu.VMEM((3, 4, LAST, 256), b16),
            pltpu.VMEM((2, 4, LAST, 256), b16),
            pltpu.VMEM((4, LAST, 256), b16),
            pltpu.VMEM((2, 2, LAST // 2, 256), b16),
            pltpu.VMEM((2, LAST // 2, 256), b16),
            pltpu.VMEM((5, 8, width), jnp.float32),
            pltpu.VMEM((5, 8, width), jnp.float32),
            pltpu.VMEM((rows, 256), jnp.float32),
            pltpu.VMEM((FAR * GROUP, 128), b16),
            pltpu.VMEM((FAR * GROUP, 128), b16),
            pltpu.VMEM((FAR, 128, 128), b16),
            pltpu.VMEM((FAR, 128, 128), b16),
            dma((4,)), dma((4, 4)), dma((4, 4)),
            dma((2, 2, 4, 2)), dma((2, 2, 4, 2)),
            dma((2, 2, 4)), dma((2, 2, 4)),
            dma((2, 4)), dma((2, 3)), dma((2, 2)), dma((2,)),
            dma((4,)), dma((3,)), dma((2,)), dma,
            dma((2, 2)), dma((2, 2)), dma((2,)), dma((2,)),
            dma((5,)), dma((5,)),
            dma((3,)), dma((3,)),
            dma((FAR,)), dma((FAR,)),
        ],
        compiler_params=pltpu.CompilerParams(
            collective_id=0, has_side_effects=True, vmem_limit_bytes=52 * 1024 * 1024
        ),
    )(frames, ref_pixels.reshape(1, -1))
    pixel_scale = 1.0 / math.sqrt(lax.axis_size("pix") * pixel_rows)
    band, diag = pl.pallas_call(
        functools.partial(finish_kernel, pixel_scale),
        out_shape=(jax.ShapeDtypeStruct((2, GROUP, width), jnp.float32),) * 2,
        in_specs=[pl.BlockSpec(memory_space=pltpu.VMEM)] * 2,
        out_specs=(pl.BlockSpec(memory_space=pltpu.VMEM),) * 2,
        compiler_params=pltpu.CompilerParams(vmem_limit_bytes=16 * 1024 * 1024),
    )(gram, sums)
    return (jnp.swapaxes(band, 1, 2), jnp.swapaxes(diag, 1, 2))


def solution(mesh):
    placed = (P(None, "pix", "mode"), P())
    paired = mesh.shape["pix"] == 16 and mesh.shape["mode"] == 2

    def body(frames, ref_pixels):
        if paired and frames.shape[2] == 16 * GROUP:
            return paired_shards(frames, ref_pixels)
        return shards(frames, ref_pixels)

    return jax.shard_map(
        body,
        mesh=mesh,
        in_specs=placed,
        out_specs=(P(None, "mode", "pix"), P(None, "mode", "pix")),
        check_vma=False,
    )
```

```python
import functools
import math

import jax
import jax.numpy as jnp
from jax import lax
from jax.experimental import pallas as pl
from jax.experimental.pallas import tpu as pltpu
from jax.sharding import PartitionSpec as P


def unit_phase(sums):
    magnitude = jnp.maximum(jnp.sqrt(sums[0] * sums[0] + sums[1] * sums[1]), 1.0)
    return sums / magnitude[None, :]


def rotate(gram_real, gram_imag, phase_rows, phase_cols, pixel_scale):
    row_real = phase_rows[0][:, None]
    row_imag = phase_rows[1][:, None]
    col_real = phase_cols[0][None, :]
    col_imag = phase_cols[1][None, :]
    unit_real = row_real * col_real + row_imag * col_imag
    unit_imag = row_imag * col_real - row_real * col_imag
    return jnp.stack(
        [
            (unit_real * gram_real - unit_imag * gram_imag) * pixel_scale,
            (unit_real * gram_imag + unit_imag * gram_real) * pixel_scale,
        ]
    )


def shards(frames, ref_pixels):
    pix_count = lax.axis_size("pix")
    mode_count = lax.axis_size("mode")
    pix_index = lax.axis_index("pix")
    mode_index = lax.axis_index("mode")
    pixel_rows = frames.shape[1]
    block_width = frames.shape[2]
    full_tiles = mode_count // 2 + 1
    full_width = full_tiles * block_width
    frame_float = frames.astype(jnp.float32)
    real_part = (frame_float[0] - frame_float[2]).astype(jnp.bfloat16)
    imag_part = (frame_float[3] - frame_float[1]).astype(jnp.bfloat16)
    fields = jnp.stack([real_part, imag_part])
    positions = pix_index * pixel_rows + lax.iota(jnp.int32, pixel_rows)
    counts = jnp.sum(
        (ref_pixels[:, None] == positions[None, :]).astype(jnp.float32), axis=0
    ).astype(jnp.bfloat16)
    local_ref = jnp.einsum("p,cpm->cm", counts, fields, preferred_element_type=jnp.float32)
    own_ref = lax.psum(local_ref, "pix")
    phase_all = lax.all_gather(unit_phase(own_ref), "mode", axis=1, tiled=True)
    phase_own = lax.dynamic_slice_in_dim(phase_all, mode_index * block_width, block_width, 1)
    phase_twice = jnp.concatenate([phase_all, phase_all], axis=1)
    phase_full = lax.dynamic_slice_in_dim(phase_twice, mode_index * block_width, full_width, 1)
    whole_fields = lax.all_gather(fields, "mode", axis=2, tiled=True)
    tiled = whole_fields.reshape(2, pixel_rows, mode_count, block_width)
    picked = (mode_index + lax.iota(jnp.int32, full_tiles)) % mode_count
    band_fields = jnp.take(tiled, picked, axis=2).reshape(2, pixel_rows, full_width)
    contract = (((0,), (0,)), ((), ()))
    own_real = fields[0]
    own_imag = fields[1]
    band_real = band_fields[0]
    band_imag = band_fields[1]
    gram_real = lax.dot_general(
        own_real, band_real, contract, preferred_element_type=jnp.float32
    ) + lax.dot_general(own_imag, band_imag, contract, preferred_element_type=jnp.float32)
    gram_imag = lax.dot_general(
        own_real, band_imag, contract, preferred_element_type=jnp.float32
    ) - lax.dot_general(own_imag, band_real, contract, preferred_element_type=jnp.float32)
    pixel_scale = 1.0 / math.sqrt(pix_count * pixel_rows)
    raw_terms = jnp.stack([gram_real, gram_imag])
    raw_diag, raw_band = (
        lax.psum_scatter(raw_terms[:, :, :block_width], "pix", scatter_dimension=2, tiled=True),
        lax.psum_scatter(raw_terms[:, :, block_width:], "pix", scatter_dimension=2, tiled=True),
    )
    diag_slice = block_width // pix_count
    band_slice = (full_width - block_width) // pix_count
    diag_cols = lax.dynamic_slice_in_dim(phase_full, pix_index * diag_slice, diag_slice, 1)
    band_cols = lax.dynamic_slice_in_dim(
        phase_full, block_width + pix_index * band_slice, band_slice, 1
    )
    diag_out = rotate(raw_diag[0], raw_diag[1], phase_own, diag_cols, pixel_scale)
    band_out = rotate(raw_band[0], raw_band[1], phase_own, band_cols, pixel_scale)
    return (band_out, diag_out)


MESH = pl.DeviceIdType.MESH
GROUP = 64
NEAR = 9
SIDE = 224
LAST = 96
PACK = GROUP // 2
FAR = 7


def gram_kernel(
    frames_hbm, pixels_ref, gram_ref, sums_ref,
    frames_ref, own, other, part, first_in, second_in, outer_in, inner_in, end_in,
    last_outer_in, last_inner_in, last_end_in, last_first_in, last_second_in,
    ref_out, ref_in, total, cross_out, cross_in, turn_out, turn_in, shared_out, shared_in,
    frame_sem, field_send, field_recv, first_send, first_recv, second_send, second_recv,
    line_send, outer_recv, inner_recv, end_recv,
    last_send, last_outer_recv, last_inner_recv, last_end_recv,
    last_first_send, last_first_recv, last_second_send, last_second_recv, ref_send, ref_recv,
    cross_send, cross_recv, turn_send, turn_recv, shared_send, shared_recv,
):
    pix = lax.axis_index("pix")
    mode = lax.axis_index("mode")
    x, y, z = pix % 2, (pix // 2) % 2, pix // 4
    upper = z >= 2
    is_end = (z == 0) | (z == 3)
    is_mid = (z == 1) | (z == 2)
    x_peer = pix + 1 - 2 * x
    y_peer = pix + 2 - 4 * y
    inner_peer = jnp.where(upper, pix - 4, pix + 4)
    outer_peer = jnp.where(upper, pix + 4, pix - 4)
    z_even_peer = pix + 4 - 8 * (z % 2)
    z_far_peer = pix + 8 - 16 * (z // 2)
    pixel_rows = frames_hbm.shape[1]
    width = frames_hbm.shape[2]
    rows = NEAR * GROUP
    top = rows - GROUP
    chunk = 4 * GROUP

    def chunk_z(k):
        return jnp.where(upper, k, 3 - k)

    def chunk_modes(k):
        return pl.ds(pl.multiple_of(chunk_z(k) * chunk, chunk), chunk)

    loads = [
        pltpu.make_async_copy(
            frames_hbm.at[:, :, chunk_modes(k)], frames_ref.at[k], frame_sem.at[k]
        )
        for k in range(4)
    ]
    for load in loads:
        load.start()
    barrier = pltpu.get_barrier_semaphore()
    for step in range(1, 16):
        pl.semaphore_signal(
            barrier, inc=1, device_id=((pix + step) % 16, mode), device_id_type=MESH
        )
    pl.semaphore_signal(barrier, inc=1, device_id=(pix, 1 - mode), device_id_type=MESH)
    pl.semaphore_signal(barrier, inc=1, device_id=(y_peer, 1 - mode), device_id_type=MESH)

    def send(src, dst, send_sem, recv_sem, to_pix, to_mode):
        copy = pltpu.make_async_remote_copy(
            src_ref=src, dst_ref=dst, send_sem=send_sem, recv_sem=recv_sem,
            device_id=(to_pix, to_mode), device_id_type=MESH,
        )
        return copy

    def ring_rows(zz, column):
        return pl.ds(pl.multiple_of((column * 4 + zz) * GROUP, GROUP), GROUP)

    for k in range(4):
        loads[k].wait()
        frame = [frames_ref[k, step].astype(jnp.float32) for step in range(4)]
        real = (frame[0] - frame[2]).astype(jnp.bfloat16).T
        imag = (frame[3] - frame[1]).astype(jnp.bfloat16).T
        for i in range(4):
            to = ring_rows(chunk_z(k), i)
            own[to, 0:pixel_rows] = real[i * GROUP:(i + 1) * GROUP]
            own[to, pixel_rows:2 * pixel_rows] = imag[i * GROUP:(i + 1) * GROUP]
    own[pl.ds(width, 8 * GROUP), :] = own[pl.ds(0, 8 * GROUP), :]
    pl.semaphore_wait(barrier, 17)

    def field_copy(k, i):
        at = ring_rows(chunk_z(k), i)
        return send(
            own.at[at], other.at[at], field_send.at[k, i], field_recv.at[k, i], pix, 1 - mode
        )

    field_copies = [field_copy(k, i) for k in range(4) for i in range(4)]
    for copy in field_copies:
        copy.start()

    ref_peers = [x_peer, y_peer, z_even_peer, z_far_peer, pix]

    def ref_copy(step):
        return send(
            ref_out.at[step], ref_in.at[step], ref_send.at[step], ref_recv.at[step],
            ref_peers[step], mode if step < 4 else 1 - mode,
        )

    ref_copies = [ref_copy(step) for step in range(5)]

    def ref_next(step):
        ref_copies[step].wait_recv()
        ref_out[step + 1] = ref_out[step] + ref_in[step]
        ref_copies[step + 1].start()

    contract = (((1,), (1,)), ((), ()))

    def turned(block):
        return jnp.concatenate([block[:, pixel_rows:], -block[:, :pixel_rows]], axis=1)

    def multiply(k):
        zc = chunk_z(k)
        for i in range(4):
            field_copies[4 * k + i].wait_recv()
        for t in range(4):
            column = (1 - y if t % 2 == 0 else y) * 2 + (1 - x if t < 2 else x)
            start = pl.multiple_of((column * 4 + zc) * GROUP, GROUP)
            own_cols = own[pl.ds(start, GROUP), :]
            other_cols = other[pl.ds(start, GROUP), :]
            cols = jnp.concatenate(
                [own_cols, turned(own_cols), other_cols, turned(other_cols)], axis=0
            )
            left = own[pl.ds(start, rows), :]
            out = lax.dot_general(left, cols, contract, preferred_element_type=jnp.float32)
            part[zc * 4 + column, pl.ds(0, top)] = out[:top].astype(jnp.bfloat16)
            owner_y = 1 - y if t % 2 == 0 else y
            shared = jnp.where(owner_y == 0, out[top:, 0:128], out[top:, 128:256])
            part[zc * 4 + column, pl.ds(top, PACK)] = jnp.concatenate(
                [shared[:PACK], shared[PACK:]], axis=1
            ).astype(jnp.bfloat16)
            if k < 2:
                for a, j in (((0, 0), (1, 0)), ((0, 1),), ((1, 1),), ())[t]:
                    firsts[a, k, j].start()

    spans = [pl.ds(0, SIDE), pl.ds(SIDE, SIDE)]
    both = pl.ds(0, 2 * SIDE)
    last = pl.ds(2 * SIDE, LAST)
    last_spans = [pl.ds(2 * SIDE, LAST // 2), pl.ds(2 * SIDE + LAST // 2, LAST // 2)]

    def owner_of(k, yy, xx):
        return chunk_z(k) * 4 + yy * 2 + xx

    def first_copy(axis, k, j):
        if axis == 0:
            owner = owner_of(k, 1 - y if j == 0 else y, 1 - x)
        else:
            owner = owner_of(k, 1 - y, 1 - x if j == 0 else x)
        return send(
            part.at[owner, spans[axis]], first_in.at[axis, k, j],
            first_send.at[axis, k, j], first_recv.at[axis, k, j],
            x_peer if axis == 0 else y_peer, mode,
        )

    def second_owner(axis, k):
        return owner_of(k, 1 - y, x) if axis == 0 else owner_of(k, y, 1 - x)

    def second_copy(axis, k):
        return send(
            part.at[second_owner(axis, k), spans[axis]], second_in.at[axis, k],
            second_send.at[axis, k], second_recv.at[axis, k],
            y_peer if axis == 0 else x_peer, mode,
        )

    firsts = {(a, k, j): first_copy(a, k, j) for a in range(2) for k in range(4) for j in range(2)}
    seconds = {(a, k): second_copy(a, k) for a in range(2) for k in range(4)}

    def f32(value):
        return value.astype(jnp.float32)

    def start_first(k):
        for j in range(2):
            for a in range(2):
                firsts[a, k, j].start()

    def forward(k):
        for a in range(2):
            firsts[a, k, 0].wait_recv()
            owner = second_owner(a, k)
            part[owner, spans[a]] = (
                f32(part[owner, spans[a]]) + f32(first_in[a, k, 0])
            ).astype(jnp.bfloat16)
            seconds[a, k].start()

    def line_copy(k, to):
        owner = owner_of(k, y, x)
        if to == "outer":
            dst, sem = outer_in.at[k], outer_recv.at[k]
        elif to == "inner":
            dst, sem = inner_in.at[k], inner_recv.at[k]
        else:
            dst, sem = end_in, end_recv
        return send(
            part.at[owner, both], dst, line_send.at[k], sem,
            outer_peer if to == "end" else inner_peer, mode,
        )

    def keep(k):
        owner = owner_of(k, y, x)
        for a in range(2):
            firsts[a, k, 1].wait_recv()
            seconds[a, k].wait_recv()
            value = (
                f32(part[owner, spans[a]]) + f32(first_in[a, k, 1]) + f32(second_in[a, k])
            )
            if k >= 2:
                @pl.when(is_mid if k == 2 else is_end)
                def _():
                    total[spans[a], :] = value
            part[owner, spans[a]] = value.astype(jnp.bfloat16)
        if k < 3:
            @pl.when(is_end)
            def _():
                line_copy(k, "outer").start()

    def pass_on(k):
        owner = owner_of(k, y, x)

        @pl.when(is_mid)
        def _():
            if k < 2:
                line_copy(k, "outer").wait_recv()
                arrived = outer_in[k]
            else:
                line_copy(0, "inner").wait_recv()
                arrived = inner_in[0]
            part[owner, both] = (f32(part[owner, both]) + f32(arrived)).astype(jnp.bfloat16)
            line_copy(k, "inner" if k < 2 else "end").start()

    def last_copy(k, to):
        owners = pl.ds(chunk_z(k) * 4, 4)
        if to == "outer":
            dst, sem = last_outer_in.at[k], last_outer_recv.at[k]
        elif to == "inner":
            dst, sem = last_inner_in.at[k], last_inner_recv.at[k]
        else:
            dst, sem = last_end_in, last_end_recv
        return send(
            part.at[owners, last], dst, last_send.at[k], sem,
            outer_peer if to == "end" else inner_peer, mode,
        )

    def last_begin(k):
        @pl.when(is_end)
        def _():
            last_copy(k, "outer").start()

    def last_add(k, terms):
        first = chunk_z(k) * 4
        for i in range(4):
            value = f32(part[first + i, last])
            for term in terms:
                value = value + f32(term[i])
            part[first + i, last] = value.astype(jnp.bfloat16)

    def last_pass(k):
        @pl.when(is_mid)
        def _():
            if k < 2:
                last_copy(k, "outer").wait_recv()
                last_add(k, [last_outer_in.at[k]])
                last_copy(k, "inner").start()
            else:
                last_copy(0, "inner").wait_recv()
                last_add(k, [last_inner_in.at[0]])
                last_copy(k, "end").start()

    def last_first_copy(axis, j):
        if axis == 0:
            owner = z * 4 + (1 - y if j == 0 else y) * 2 + 1 - x
        else:
            owner = z * 4 + (1 - y) * 2 + (1 - x if j == 0 else x)
        return send(
            part.at[owner, last_spans[axis]], last_first_in.at[axis, j],
            last_first_send.at[axis, j], last_first_recv.at[axis, j],
            x_peer if axis == 0 else y_peer, mode,
        )

    def last_second_owner(axis):
        return z * 4 + (1 - y) * 2 + x if axis == 0 else z * 4 + y * 2 + 1 - x

    def last_second_copy(axis):
        return send(
            part.at[last_second_owner(axis), last_spans[axis]], last_second_in.at[axis],
            last_second_send.at[axis], last_second_recv.at[axis],
            y_peer if axis == 0 else x_peer, mode,
        )

    last_firsts = {(a, j): last_first_copy(a, j) for a in range(2) for j in range(2)}
    last_seconds = [last_second_copy(a) for a in range(2)]

    def last_spread():
        @pl.when(is_mid)
        def _():
            last_copy(2, "outer").wait_recv()
            last_copy(1, "inner").wait_recv()
            last_add(2, [last_outer_in.at[2], last_inner_in.at[1]])

        @pl.when(is_end)
        def _():
            last_copy(3, "end").wait_recv()
            last_add(3, [last_end_in])

        for j in range(2):
            for a in range(2):
                last_firsts[a, j].start()

    def last_forward():
        for a in range(2):
            last_firsts[a, 0].wait_recv()
            owner = last_second_owner(a)
            part[owner, last_spans[a]] = (
                f32(part[owner, last_spans[a]]) + f32(last_first_in[a, 0])
            ).astype(jnp.bfloat16)
            last_seconds[a].start()

    def last_keep():
        for a in range(2):
            last_firsts[a, 1].wait_recv()
            last_seconds[a].wait_recv()
            total[last_spans[a], :] = (
                f32(part[pix, last_spans[a]]) + f32(last_first_in[a, 1]) + f32(last_second_in[a])
            )

    rest = (FAR - 1) * GROUP
    ring = pix % 4 * 4 + z

    def chip_at(step):
        there = (ring + step) % 16
        return there % 4 * 4 + there // 4

    def cross_copy(at, size, index):
        rows_at = pl.ds(at, size)
        return send(
            cross_out.at[rows_at], cross_in.at[rows_at],
            cross_send.at[index], cross_recv.at[index], pix, 1 - mode,
        )

    cross_rest = cross_copy(0, rest, 0)
    cross_early = cross_copy(rest, GROUP, 1)
    shared_copy = send(
        shared_out, shared_in, shared_send, shared_recv,
        y_peer, jnp.where(y == 0, mode, 1 - mode),
    )
    turns = [
        send(
            turn_out.at[d - 1], turn_in.at[d - 1], turn_send.at[d - 1], turn_recv.at[d - 1],
            chip_at(d), mode,
        )
        for d in range(1, FAR + 1)
    ]

    def start_turn(d):
        stacked = jnp.concatenate(
            [
                total[d * GROUP:(d + 1) * GROUP, 0:128].astype(jnp.bfloat16),
                cross_in[(d - 1) * GROUP:d * GROUP, :],
            ],
            axis=0,
        )
        turn_out[d - 1] = stacked.T
        turns[d - 1].start()

    for k in range(3):
        multiply(k)
        last_begin(k)
    positions = pix * pixel_rows + lax.broadcasted_iota(
        jnp.int32, (pixels_ref.shape[1], pixel_rows), 1
    )
    listed = jnp.broadcast_to(pixels_ref[...], (8, pixels_ref.shape[1])).T[:, 0:1]
    counts = jnp.sum(
        jnp.where(listed == positions, 1.0, 0.0), axis=0, keepdims=True
    )
    nothing = jnp.zeros_like(counts)
    row = lax.broadcasted_iota(jnp.int32, (16, 2 * pixel_rows), 0)
    real_weight = jnp.concatenate([counts, nothing], axis=1)
    imag_weight = jnp.concatenate([nothing, counts], axis=1)
    weight = jnp.where(row == 0, real_weight, jnp.where(row == 1, imag_weight, 0.0))
    weight = weight.astype(jnp.bfloat16)
    for pair in range(8):
        places = [(p % 4 * 4 + p // 4) * GROUP for p in (2 * pair, 2 * pair + 1)]
        block = jnp.concatenate([own[pl.ds(at, GROUP), :] for at in places], axis=0)
        ref_out[0, :, pl.ds(pair * 128, 128)] = lax.dot_general(
            weight, block, contract, preferred_element_type=jnp.float32
        )[0:8]
    ref_copies[0].start()
    forward(0)
    start_first(2)
    multiply(3)
    ref_next(0)
    last_pass(0)
    forward(1)
    start_first(3)
    last_pass(1)
    ref_next(1)
    keep(0)
    forward(2)
    last_pass(3)
    ref_next(2)
    last_spread()
    keep(1)
    pass_on(0)
    ref_next(3)
    forward(3)
    last_forward()
    keep(2)
    pass_on(1)
    last_keep()
    cross_out[rest:] = total[FAR * GROUP:NEAR * GROUP - GROUP, 128:256].astype(jnp.bfloat16)
    cross_early.start()
    shared = jnp.concatenate(
        [total[top:top + PACK, 0:128], total[top:top + PACK, 128:256]], axis=0
    )
    shared_out[...] = jnp.concatenate([shared, shared], axis=0).astype(jnp.bfloat16).T
    shared_copy.start()
    keep(3)
    pass_on(3)

    cross_early.wait_recv()
    start_turn(FAR)

    @pl.when(is_mid)
    def _():
        line_copy(2, "outer").wait_recv()
        line_copy(1, "inner").wait_recv()
        total[both, :] = total[both, :] + f32(outer_in[2]) + f32(inner_in[1])

    @pl.when(is_end)
    def _():
        line_copy(3, "end").wait_recv()
        total[both, :] = total[both, :] + f32(end_in[...])

    cross_out[0:rest] = total[GROUP:FAR * GROUP, 128:256].astype(jnp.bfloat16)
    cross_rest.start()

    lane = lax.broadcasted_iota(jnp.int32, (GROUP, 128), 1)
    low = lane < GROUP

    def group_rows(step):
        return pl.ds(pl.multiple_of(chip_at(step) * GROUP, GROUP), GROUP)

    for d in range(NEAR - 1):
        here = total[d * GROUP:(d + 1) * GROUP, 0:128]
        there = total[d * GROUP:(d + 1) * GROUP, 128:256]
        gram_ref[0, group_rows(d), :] = jnp.where(low, here, pltpu.roll(there, GROUP, 1))
        gram_ref[1, group_rows(d), :] = jnp.where(low, pltpu.roll(here, GROUP, 1), there)

    cross_rest.wait_recv()
    for d in range(1, FAR):
        start_turn(d)
    shared_copy.wait_recv()
    arrived = f32(shared_in[...])
    mine = low == (y == 0)
    shared = jnp.concatenate(
        [total[top:top + PACK, 0:128], total[top:top + PACK, 128:256]], axis=0
    )
    rolled = pltpu.roll(shared, GROUP, 1)
    gram_ref[0, group_rows(8), :] = jnp.where(
        mine, jnp.where(low, shared, rolled), arrived[0:GROUP]
    )
    gram_ref[1, group_rows(8), :] = jnp.where(
        mine, jnp.where(low, rolled, shared), -arrived[GROUP:]
    )
    ref_copies[4].wait_recv()
    sums_ref[0] = ref_out[4]
    sums_ref[1] = ref_in[4]
    for d in range(1, FAR + 1):
        turns[d - 1].wait_recv()
        arrived = f32(turn_in[d - 1])
        gram_ref[0, group_rows(16 - d), :] = arrived[0:GROUP]
        gram_ref[1, group_rows(16 - d), :] = -arrived[GROUP:]

    for copy in field_copies + ref_copies + list(firsts.values()) + list(seconds.values()):
        copy.wait_send()
    for copy in turns + [cross_rest, cross_early, shared_copy] + list(last_firsts.values()) + last_seconds:
        copy.wait_send()
    for k in range(3):
        @pl.when(is_end | (k < 2))
        def _():
            line_copy(k, "outer").wait_send()
            last_copy(k, "outer").wait_send()

    @pl.when(is_mid)
    def _():
        line_copy(3, "end").wait_send()
        last_copy(3, "end").wait_send()


def finish_kernel(pixel_scale, gram_ref, sums_ref, band_ref, diag_ref):
    pix = lax.axis_index("pix")
    odd = pix % 2 == 1
    at = pl.multiple_of((pix // 2) * 128, 128)
    own = sums_ref[0, :, pl.ds(at, 128)]
    other = sums_ref[1, :, pl.ds(at, 128)]
    low = lax.broadcasted_iota(jnp.int32, own.shape, 1) < GROUP
    own = jnp.where(odd, pltpu.roll(own, GROUP, 1), own)
    other = jnp.where(odd, other, pltpu.roll(other, GROUP, 1))
    cols = jnp.where(low, own, other).T

    def unit(real, imag):
        magnitude = jnp.maximum(jnp.sqrt(real * real + imag * imag), 1.0)
        return real / magnitude, imag / magnitude

    col_real, col_imag = unit(cols[:, 0:1], cols[:, 1:2])
    row_real, row_imag = unit(sums_ref[0, 0:1, :], sums_ref[0, 1:2, :])
    unit_real = row_real * col_real + row_imag * col_imag
    unit_imag = row_imag * col_real - row_real * col_imag
    gram_real = gram_ref[0].T
    gram_imag = gram_ref[1].T
    real = (unit_real * gram_real - unit_imag * gram_imag) * pixel_scale
    imag = (unit_real * gram_imag + unit_imag * gram_real) * pixel_scale
    diag_ref[0] = real[:GROUP]
    diag_ref[1] = imag[:GROUP]
    band_ref[0] = real[GROUP:]
    band_ref[1] = imag[GROUP:]


def paired_shards(frames, ref_pixels):
    pixel_rows = frames.shape[1]
    width = frames.shape[2]
    rows = 2 * SIDE + LAST
    b16 = jnp.bfloat16
    dma = pltpu.SemaphoreType.DMA
    gram, sums = pl.pallas_call(
        gram_kernel,
        out_shape=(
            jax.ShapeDtypeStruct((2, width, 128), jnp.float32),
            jax.ShapeDtypeStruct((2, 8, width), jnp.float32),
        ),
        in_specs=[
            pl.BlockSpec(memory_space=pltpu.HBM),
            pl.BlockSpec(memory_space=pltpu.VMEM),
        ],
        out_specs=(pl.BlockSpec(memory_space=pltpu.VMEM),) * 2,
        scratch_shapes=[
            pltpu.VMEM((4, 4, pixel_rows, 4 * GROUP), b16),
            pltpu.VMEM((width + 8 * GROUP, 2 * pixel_rows), b16),
            pltpu.VMEM((width, 2 * pixel_rows), b16),
            pltpu.VMEM((16, rows, 256), b16),
            pltpu.VMEM((2, 4, 2, SIDE, 256), b16),
            pltpu.VMEM((2, 4, SIDE, 256), b16),
            pltpu.VMEM((3, 2 * SIDE, 256), b16),
            pltpu.VMEM((2, 2 * SIDE, 256), b16),
            pltpu.VMEM((2 * SIDE, 256), b16),
            pltpu.VMEM((3, 4, LAST, 256), b16),
            pltpu.VMEM((2, 4, LAST, 256), b16),
            pltpu.VMEM((4, LAST, 256), b16),
            pltpu.VMEM((2, 2, LAST // 2, 256), b16),
            pltpu.VMEM((2, LAST // 2, 256), b16),
            pltpu.VMEM((5, 8, width), jnp.float32),
            pltpu.VMEM((5, 8, width), jnp.float32),
            pltpu.VMEM((rows, 256), jnp.float32),
            pltpu.VMEM((FAR * GROUP, 128), b16),
            pltpu.VMEM((FAR * GROUP, 128), b16),
            pltpu.VMEM((FAR, 128, 128), b16),
            pltpu.VMEM((FAR, 128, 128), b16),
            pltpu.VMEM((128, 128), b16),
            pltpu.VMEM((128, 128), b16),
            dma((4,)), dma((4, 4)), dma((4, 4)),
            dma((2, 4, 2)), dma((2, 4, 2)),
            dma((2, 4)), dma((2, 4)),
            dma((4,)), dma((3,)), dma((2,)), dma,
            dma((4,)), dma((3,)), dma((2,)), dma,
            dma((2, 2)), dma((2, 2)), dma((2,)), dma((2,)),
            dma((5,)), dma((5,)),
            dma((2,)), dma((2,)),
            dma((FAR,)), dma((FAR,)),
            dma, dma,
        ],
        compiler_params=pltpu.CompilerParams(
            collective_id=0, has_side_effects=True, vmem_limit_bytes=52 * 1024 * 1024
        ),
    )(frames, ref_pixels.reshape(1, -1))
    pixel_scale = 1.0 / math.sqrt(lax.axis_size("pix") * pixel_rows)
    band, diag = pl.pallas_call(
        functools.partial(finish_kernel, pixel_scale),
        out_shape=(jax.ShapeDtypeStruct((2, GROUP, width), jnp.float32),) * 2,
        in_specs=[pl.BlockSpec(memory_space=pltpu.VMEM)] * 2,
        out_specs=(pl.BlockSpec(memory_space=pltpu.VMEM),) * 2,
        compiler_params=pltpu.CompilerParams(vmem_limit_bytes=16 * 1024 * 1024),
    )(gram, sums)
    return (jnp.swapaxes(band, 1, 2), jnp.swapaxes(diag, 1, 2))


def solution(mesh):
    placed = (P(None, "pix", "mode"), P())
    paired = mesh.shape["pix"] == 16 and mesh.shape["mode"] == 2

    def body(frames, ref_pixels):
        if paired and frames.shape[2] == 16 * GROUP:
            return paired_shards(frames, ref_pixels)
        return shards(frames, ref_pixels)

    return jax.shard_map(
        body,
        mesh=mesh,
        in_specs=placed,
        out_specs=(P(None, "mode", "pix"), P(None, "mode", "pix")),
        check_vma=False,
    )
```

```python
import functools
import math

import jax
import jax.numpy as jnp
from jax import lax
from jax.experimental import pallas as pl
from jax.experimental.pallas import tpu as pltpu
from jax.sharding import PartitionSpec as P


def unit_phase(sums):
    magnitude = jnp.maximum(jnp.sqrt(sums[0] * sums[0] + sums[1] * sums[1]), 1.0)
    return sums / magnitude[None, :]


def rotate(gram_real, gram_imag, phase_rows, phase_cols, pixel_scale):
    row_real = phase_rows[0][:, None]
    row_imag = phase_rows[1][:, None]
    col_real = phase_cols[0][None, :]
    col_imag = phase_cols[1][None, :]
    unit_real = row_real * col_real + row_imag * col_imag
    unit_imag = row_imag * col_real - row_real * col_imag
    return jnp.stack(
        [
            (unit_real * gram_real - unit_imag * gram_imag) * pixel_scale,
            (unit_real * gram_imag + unit_imag * gram_real) * pixel_scale,
        ]
    )


def shards(frames, ref_pixels):
    pix_count = lax.axis_size("pix")
    mode_count = lax.axis_size("mode")
    pix_index = lax.axis_index("pix")
    mode_index = lax.axis_index("mode")
    pixel_rows = frames.shape[1]
    block_width = frames.shape[2]
    full_tiles = mode_count // 2 + 1
    full_width = full_tiles * block_width
    frame_float = frames.astype(jnp.float32)
    real_part = (frame_float[0] - frame_float[2]).astype(jnp.bfloat16)
    imag_part = (frame_float[3] - frame_float[1]).astype(jnp.bfloat16)
    fields = jnp.stack([real_part, imag_part])
    positions = pix_index * pixel_rows + lax.iota(jnp.int32, pixel_rows)
    counts = jnp.sum(
        (ref_pixels[:, None] == positions[None, :]).astype(jnp.float32), axis=0
    ).astype(jnp.bfloat16)
    local_ref = jnp.einsum("p,cpm->cm", counts, fields, preferred_element_type=jnp.float32)
    own_ref = lax.psum(local_ref, "pix")
    phase_all = lax.all_gather(unit_phase(own_ref), "mode", axis=1, tiled=True)
    phase_own = lax.dynamic_slice_in_dim(phase_all, mode_index * block_width, block_width, 1)
    phase_twice = jnp.concatenate([phase_all, phase_all], axis=1)
    phase_full = lax.dynamic_slice_in_dim(phase_twice, mode_index * block_width, full_width, 1)
    whole_fields = lax.all_gather(fields, "mode", axis=2, tiled=True)
    tiled = whole_fields.reshape(2, pixel_rows, mode_count, block_width)
    picked = (mode_index + lax.iota(jnp.int32, full_tiles)) % mode_count
    band_fields = jnp.take(tiled, picked, axis=2).reshape(2, pixel_rows, full_width)
    contract = (((0,), (0,)), ((), ()))
    own_real = fields[0]
    own_imag = fields[1]
    band_real = band_fields[0]
    band_imag = band_fields[1]
    gram_real = lax.dot_general(
        own_real, band_real, contract, preferred_element_type=jnp.float32
    ) + lax.dot_general(own_imag, band_imag, contract, preferred_element_type=jnp.float32)
    gram_imag = lax.dot_general(
        own_real, band_imag, contract, preferred_element_type=jnp.float32
    ) - lax.dot_general(own_imag, band_real, contract, preferred_element_type=jnp.float32)
    pixel_scale = 1.0 / math.sqrt(pix_count * pixel_rows)
    raw_terms = jnp.stack([gram_real, gram_imag])
    raw_diag, raw_band = (
        lax.psum_scatter(raw_terms[:, :, :block_width], "pix", scatter_dimension=2, tiled=True),
        lax.psum_scatter(raw_terms[:, :, block_width:], "pix", scatter_dimension=2, tiled=True),
    )
    diag_slice = block_width // pix_count
    band_slice = (full_width - block_width) // pix_count
    diag_cols = lax.dynamic_slice_in_dim(phase_full, pix_index * diag_slice, diag_slice, 1)
    band_cols = lax.dynamic_slice_in_dim(
        phase_full, block_width + pix_index * band_slice, band_slice, 1
    )
    diag_out = rotate(raw_diag[0], raw_diag[1], phase_own, diag_cols, pixel_scale)
    band_out = rotate(raw_band[0], raw_band[1], phase_own, band_cols, pixel_scale)
    return (band_out, diag_out)


MESH = pl.DeviceIdType.MESH
GROUP = 64
NEAR = 9
SIDE = 224
LAST = 96
PACK = GROUP // 2
FAR = 7


def gram_kernel(
    frames_hbm, pixels_hbm, gram_ref, sums_ref,
    pixels_ref, frames_ref, own, other, part, first_in, second_in, outer_in, inner_in, end_in,
    last_outer_in, last_inner_in, last_end_in, last_first_in, last_second_in,
    ref_out, ref_in, total, cross_out, cross_in, turn_out, turn_in, shared_out, shared_in,
    pixel_sem, frame_sem, field_send, field_recv, first_send, first_recv, second_send, second_recv,
    line_send, outer_recv, inner_recv, end_recv,
    last_send, last_outer_recv, last_inner_recv, last_end_recv,
    last_first_send, last_first_recv, last_second_send, last_second_recv, ref_send, ref_recv,
    cross_send, cross_recv, turn_send, turn_recv, shared_send, shared_recv,
):
    pix = lax.axis_index("pix")
    mode = lax.axis_index("mode")
    x, y, z = pix % 2, (pix // 2) % 2, pix // 4
    upper = z >= 2
    is_end = (z == 0) | (z == 3)
    is_mid = (z == 1) | (z == 2)
    x_peer = pix + 1 - 2 * x
    y_peer = pix + 2 - 4 * y
    inner_peer = jnp.where(upper, pix - 4, pix + 4)
    outer_peer = jnp.where(upper, pix + 4, pix - 4)
    z_even_peer = pix + 4 - 8 * (z % 2)
    z_far_peer = pix + 8 - 16 * (z // 2)
    pixel_rows = frames_hbm.shape[1]
    width = frames_hbm.shape[2]
    rows = NEAR * GROUP
    top = rows - GROUP
    chunk = 4 * GROUP

    def chunk_z(k):
        return jnp.where(upper, k, 3 - k)

    def chunk_modes(k):
        return pl.ds(pl.multiple_of(chunk_z(k) * chunk, chunk), chunk)

    loads = [
        pltpu.make_async_copy(
            frames_hbm.at[:, :, chunk_modes(k)], frames_ref.at[k], frame_sem.at[k]
        )
        for k in range(4)
    ]
    for load in loads:
        load.start()
    listing = pltpu.make_async_copy(pixels_hbm, pixels_ref, pixel_sem)
    listing.start()
    barrier = pltpu.get_barrier_semaphore()
    for step in range(1, 16):
        pl.semaphore_signal(
            barrier, inc=1, device_id=((pix + step) % 16, mode), device_id_type=MESH
        )
    pl.semaphore_signal(barrier, inc=1, device_id=(pix, 1 - mode), device_id_type=MESH)
    pl.semaphore_signal(barrier, inc=1, device_id=(y_peer, 1 - mode), device_id_type=MESH)

    def send(src, dst, send_sem, recv_sem, to_pix, to_mode):
        copy = pltpu.make_async_remote_copy(
            src_ref=src, dst_ref=dst, send_sem=send_sem, recv_sem=recv_sem,
            device_id=(to_pix, to_mode), device_id_type=MESH,
        )
        return copy

    def ring_rows(zz, column):
        return pl.ds(pl.multiple_of((column * 4 + zz) * GROUP, GROUP), GROUP)

    for k in range(4):
        loads[k].wait()
        frame = [frames_ref[k, step].astype(jnp.float32) for step in range(4)]
        real = (frame[0] - frame[2]).astype(jnp.bfloat16).T
        imag = (frame[3] - frame[1]).astype(jnp.bfloat16).T
        for i in range(4):
            to = ring_rows(chunk_z(k), i)
            own[to, 0:pixel_rows] = real[i * GROUP:(i + 1) * GROUP]
            own[to, pixel_rows:2 * pixel_rows] = imag[i * GROUP:(i + 1) * GROUP]
    own[pl.ds(width, 8 * GROUP), :] = own[pl.ds(0, 8 * GROUP), :]
    pl.semaphore_wait(barrier, 17)

    def field_copy(k, i):
        at = ring_rows(chunk_z(k), i)
        return send(
            own.at[at], other.at[at], field_send.at[k, i], field_recv.at[k, i], pix, 1 - mode
        )

    field_copies = [field_copy(k, i) for k in range(4) for i in range(4)]
    for copy in field_copies:
        copy.start()

    ref_peers = [x_peer, y_peer, z_even_peer, z_far_peer, pix]

    def ref_copy(step):
        return send(
            ref_out.at[step], ref_in.at[step], ref_send.at[step], ref_recv.at[step],
            ref_peers[step], mode if step < 4 else 1 - mode,
        )

    ref_copies = [ref_copy(step) for step in range(5)]

    def ref_next(step):
        ref_copies[step].wait_recv()
        ref_out[step + 1] = ref_out[step] + ref_in[step]
        ref_copies[step + 1].start()

    contract = (((1,), (1,)), ((), ()))

    def turned(block):
        return jnp.concatenate([block[:, pixel_rows:], -block[:, :pixel_rows]], axis=1)

    def multiply(k):
        zc = chunk_z(k)
        for i in range(4):
            field_copies[4 * k + i].wait_recv()
        for t in range(4):
            column = (1 - y if t % 2 == 0 else y) * 2 + (1 - x if t < 2 else x)
            start = pl.multiple_of((column * 4 + zc) * GROUP, GROUP)
            own_cols = own[pl.ds(start, GROUP), :]
            other_cols = other[pl.ds(start, GROUP), :]
            cols = jnp.concatenate(
                [own_cols, turned(own_cols), other_cols, turned(other_cols)], axis=0
            )
            left = own[pl.ds(start, rows), :]
            out = lax.dot_general(left, cols, contract, preferred_element_type=jnp.float32)
            part[zc * 4 + column, pl.ds(0, top)] = out[:top].astype(jnp.bfloat16)
            owner_y = 1 - y if t % 2 == 0 else y
            shared = jnp.where(owner_y == 0, out[top:, 0:128], out[top:, 128:256])
            part[zc * 4 + column, pl.ds(top, PACK)] = jnp.concatenate(
                [shared[:PACK], shared[PACK:]], axis=1
            ).astype(jnp.bfloat16)
            if k < 2:
                for a, j in (((0, 0), (1, 0)), ((0, 1),), ((1, 1),), ())[t]:
                    firsts[a, k, j].start()

    spans = [pl.ds(0, SIDE), pl.ds(SIDE, SIDE)]
    last = pl.ds(2 * SIDE, LAST)
    last_spans = [pl.ds(2 * SIDE, LAST // 2), pl.ds(2 * SIDE + LAST // 2, LAST // 2)]

    def owner_of(k, yy, xx):
        return chunk_z(k) * 4 + yy * 2 + xx

    def first_copy(axis, k, j):
        if axis == 0:
            owner = owner_of(k, 1 - y if j == 0 else y, 1 - x)
        else:
            owner = owner_of(k, 1 - y, 1 - x if j == 0 else x)
        return send(
            part.at[owner, spans[axis]], first_in.at[axis, k, j],
            first_send.at[axis, k, j], first_recv.at[axis, k, j],
            x_peer if axis == 0 else y_peer, mode,
        )

    def second_owner(axis, k):
        return owner_of(k, 1 - y, x) if axis == 0 else owner_of(k, y, 1 - x)

    def second_copy(axis, k):
        return send(
            part.at[second_owner(axis, k), spans[axis]], second_in.at[axis, k],
            second_send.at[axis, k], second_recv.at[axis, k],
            y_peer if axis == 0 else x_peer, mode,
        )

    firsts = {(a, k, j): first_copy(a, k, j) for a in range(2) for k in range(4) for j in range(2)}
    seconds = {(a, k): second_copy(a, k) for a in range(2) for k in range(4)}

    def f32(value):
        return value.astype(jnp.float32)

    def start_first(k):
        for j in range(2):
            for a in range(2):
                firsts[a, k, j].start()

    def forward(k):
        for a in range(2):
            firsts[a, k, 0].wait_recv()
            owner = second_owner(a, k)
            part[owner, spans[a]] = (
                f32(part[owner, spans[a]]) + f32(first_in[a, k, 0])
            ).astype(jnp.bfloat16)
            seconds[a, k].start()

    def line_copy(k, a, to):
        owner = owner_of(k, y, x)
        span = spans[a]
        if to == "outer":
            dst, sem = outer_in.at[k, span], outer_recv.at[k, a]
        elif to == "inner":
            dst, sem = inner_in.at[k, span], inner_recv.at[k, a]
        else:
            dst, sem = end_in.at[span], end_recv.at[a]
        return send(
            part.at[owner, span], dst, line_send.at[k, a], sem,
            outer_peer if to == "end" else inner_peer, mode,
        )

    def keep(k):
        owner = owner_of(k, y, x)
        for a in (1, 0):
            firsts[a, k, 1].wait_recv()
            seconds[a, k].wait_recv()
            span = spans[a]
            value = f32(part[owner, span]) + f32(first_in[a, k, 1]) + f32(second_in[a, k])
            if k >= 2:
                @pl.when(is_mid if k == 2 else is_end)
                def _():
                    total[span, :] = value
            part[owner, span] = value.astype(jnp.bfloat16)
            if k < 3:
                @pl.when(is_end)
                def _():
                    line_copy(k, a, "outer").start()
            else:
                pass_on(k, a)

    def pass_on(k, a):
        owner = owner_of(k, y, x)
        span = spans[a]

        @pl.when(is_mid)
        def _():
            if k < 2:
                line_copy(k, a, "outer").wait_recv()
                arrived = outer_in[k, span]
            else:
                line_copy(0, a, "inner").wait_recv()
                arrived = inner_in[0, span]
            part[owner, span] = (f32(part[owner, span]) + f32(arrived)).astype(jnp.bfloat16)
            line_copy(k, a, "inner" if k < 2 else "end").start()

    def line_end(a):
        span = spans[a]

        @pl.when(is_mid)
        def _():
            line_copy(2, a, "outer").wait_recv()
            line_copy(1, a, "inner").wait_recv()
            total[span, :] = total[span, :] + f32(outer_in[2, span]) + f32(inner_in[1, span])

        @pl.when(is_end)
        def _():
            line_copy(3, a, "end").wait_recv()
            total[span, :] = total[span, :] + f32(end_in[span])

    def last_copy(k, to):
        owners = pl.ds(chunk_z(k) * 4, 4)
        if to == "outer":
            dst, sem = last_outer_in.at[k], last_outer_recv.at[k]
        elif to == "inner":
            dst, sem = last_inner_in.at[k], last_inner_recv.at[k]
        else:
            dst, sem = last_end_in, last_end_recv
        return send(
            part.at[owners, last], dst, last_send.at[k], sem,
            outer_peer if to == "end" else inner_peer, mode,
        )

    def last_begin(k):
        @pl.when(is_end)
        def _():
            last_copy(k, "outer").start()

    def last_add(k, terms):
        first = chunk_z(k) * 4
        for i in range(4):
            value = f32(part[first + i, last])
            for term in terms:
                value = value + f32(term[i])
            part[first + i, last] = value.astype(jnp.bfloat16)

    def last_pass(k):
        @pl.when(is_mid)
        def _():
            if k < 2:
                last_copy(k, "outer").wait_recv()
                last_add(k, [last_outer_in.at[k]])
                last_copy(k, "inner").start()
            else:
                last_copy(0, "inner").wait_recv()
                last_add(k, [last_inner_in.at[0]])
                last_copy(k, "end").start()

    def last_first_copy(axis, j):
        if axis == 0:
            owner = z * 4 + (1 - y if j == 0 else y) * 2 + 1 - x
        else:
            owner = z * 4 + (1 - y) * 2 + (1 - x if j == 0 else x)
        return send(
            part.at[owner, last_spans[axis]], last_first_in.at[axis, j],
            last_first_send.at[axis, j], last_first_recv.at[axis, j],
            x_peer if axis == 0 else y_peer, mode,
        )

    def last_second_owner(axis):
        return z * 4 + (1 - y) * 2 + x if axis == 0 else z * 4 + y * 2 + 1 - x

    def last_second_copy(axis):
        return send(
            part.at[last_second_owner(axis), last_spans[axis]], last_second_in.at[axis],
            last_second_send.at[axis], last_second_recv.at[axis],
            y_peer if axis == 0 else x_peer, mode,
        )

    last_firsts = {(a, j): last_first_copy(a, j) for a in range(2) for j in range(2)}
    last_seconds = [last_second_copy(a) for a in range(2)]

    def last_spread():
        @pl.when(is_mid)
        def _():
            last_copy(2, "outer").wait_recv()
            last_copy(1, "inner").wait_recv()
            last_add(2, [last_outer_in.at[2], last_inner_in.at[1]])

        @pl.when(is_end)
        def _():
            last_copy(3, "end").wait_recv()
            last_add(3, [last_end_in])

        for j in range(2):
            for a in range(2):
                last_firsts[a, j].start()

    def last_forward():
        for a in range(2):
            last_firsts[a, 0].wait_recv()
            owner = last_second_owner(a)
            part[owner, last_spans[a]] = (
                f32(part[owner, last_spans[a]]) + f32(last_first_in[a, 0])
            ).astype(jnp.bfloat16)
            last_seconds[a].start()

    def last_keep():
        for a in range(2):
            last_firsts[a, 1].wait_recv()
            last_seconds[a].wait_recv()
            total[last_spans[a], :] = (
                f32(part[pix, last_spans[a]]) + f32(last_first_in[a, 1]) + f32(last_second_in[a])
            )

    ring = pix % 4 * 4 + z

    def chip_at(step):
        there = (ring + step) % 16
        return there % 4 * 4 + there // 4

    def cross_copy(at, size, index):
        rows_at = pl.ds(at, size)
        return send(
            cross_out.at[rows_at], cross_in.at[rows_at],
            cross_send.at[index], cross_recv.at[index], pix, 1 - mode,
        )

    cross_rows = [(FAR, FAR + 1), (4, FAR), (1, 4)]
    crosses = [
        cross_copy((first - 1) * GROUP, (end - first) * GROUP, i)
        for i, (first, end) in enumerate(cross_rows)
    ]

    def start_cross(i):
        first, end = cross_rows[i]
        cross_out[(first - 1) * GROUP:(end - 1) * GROUP] = total[
            first * GROUP:end * GROUP, 128:256
        ].astype(jnp.bfloat16)
        crosses[i].start()

    def mirror(i):
        crosses[i].wait_recv()
        for d in range(*cross_rows[i]):
            start_turn(d)

    shared_copy = send(
        shared_out, shared_in, shared_send, shared_recv,
        y_peer, jnp.where(y == 0, mode, 1 - mode),
    )
    turns = [
        send(
            turn_out.at[d - 1], turn_in.at[d - 1], turn_send.at[d - 1], turn_recv.at[d - 1],
            chip_at(d), mode,
        )
        for d in range(1, FAR + 1)
    ]

    def start_turn(d):
        stacked = jnp.concatenate(
            [
                total[d * GROUP:(d + 1) * GROUP, 0:128].astype(jnp.bfloat16),
                cross_in[(d - 1) * GROUP:d * GROUP, :],
            ],
            axis=0,
        )
        turn_out[d - 1] = stacked.T
        turns[d - 1].start()

    for k in range(3):
        multiply(k)
        last_begin(k)
    positions = pix * pixel_rows + lax.broadcasted_iota(
        jnp.int32, (pixels_ref.shape[1], pixel_rows), 1
    )
    listing.wait()
    listed = jnp.broadcast_to(pixels_ref[...], (8, pixels_ref.shape[1])).T[:, 0:1]
    counts = jnp.sum(
        jnp.where(listed == positions, 1.0, 0.0), axis=0, keepdims=True
    )
    nothing = jnp.zeros_like(counts)
    row = lax.broadcasted_iota(jnp.int32, (16, 2 * pixel_rows), 0)
    real_weight = jnp.concatenate([counts, nothing], axis=1)
    imag_weight = jnp.concatenate([nothing, counts], axis=1)
    weight = jnp.where(row == 0, real_weight, jnp.where(row == 1, imag_weight, 0.0))
    weight = weight.astype(jnp.bfloat16)
    for pair in range(8):
        places = [(p % 4 * 4 + p // 4) * GROUP for p in (2 * pair, 2 * pair + 1)]
        block = jnp.concatenate([own[pl.ds(at, GROUP), :] for at in places], axis=0)
        ref_out[0, :, pl.ds(pair * 128, 128)] = lax.dot_general(
            weight, block, contract, preferred_element_type=jnp.float32
        )[0:8]
    ref_copies[0].start()
    forward(0)
    start_first(2)
    multiply(3)
    ref_next(0)
    last_pass(0)
    forward(1)
    start_first(3)
    last_pass(1)
    ref_next(1)
    keep(0)
    forward(2)
    last_pass(3)
    ref_next(2)
    last_spread()
    keep(1)
    pass_on(0, 1)
    pass_on(0, 0)
    ref_next(3)
    forward(3)
    last_forward()
    keep(2)
    pass_on(1, 1)
    pass_on(1, 0)
    last_keep()
    start_cross(0)
    shared = jnp.concatenate(
        [total[top:top + PACK, 0:128], total[top:top + PACK, 128:256]], axis=0
    )
    shared_out[...] = jnp.concatenate([shared, shared], axis=0).astype(jnp.bfloat16).T
    shared_copy.start()
    keep(3)
    mirror(0)
    line_end(1)
    start_cross(1)

    lane = lax.broadcasted_iota(jnp.int32, (GROUP, 128), 1)
    low = lane < GROUP

    def group_rows(step):
        return pl.ds(pl.multiple_of(chip_at(step) * GROUP, GROUP), GROUP)

    def place(d):
        here = total[d * GROUP:(d + 1) * GROUP, 0:128]
        there = total[d * GROUP:(d + 1) * GROUP, 128:256]
        gram_ref[0, group_rows(d), :] = jnp.where(low, here, pltpu.roll(there, GROUP, 1))
        gram_ref[1, group_rows(d), :] = jnp.where(low, pltpu.roll(here, GROUP, 1), there)

    mirror(1)
    line_end(0)
    start_cross(2)
    for d in range(NEAR - 1):
        place(d)
    mirror(2)
    shared_copy.wait_recv()
    arrived = f32(shared_in[...])
    mine = low == (y == 0)
    shared = jnp.concatenate(
        [total[top:top + PACK, 0:128], total[top:top + PACK, 128:256]], axis=0
    )
    rolled = pltpu.roll(shared, GROUP, 1)
    gram_ref[0, group_rows(8), :] = jnp.where(
        mine, jnp.where(low, shared, rolled), arrived[0:GROUP]
    )
    gram_ref[1, group_rows(8), :] = jnp.where(
        mine, jnp.where(low, rolled, shared), -arrived[GROUP:]
    )
    ref_copies[4].wait_recv()
    sums_ref[0] = ref_out[4]
    sums_ref[1] = ref_in[4]
    for d in range(1, FAR + 1):
        turns[d - 1].wait_recv()
        arrived = f32(turn_in[d - 1])
        gram_ref[0, group_rows(16 - d), :] = arrived[0:GROUP]
        gram_ref[1, group_rows(16 - d), :] = -arrived[GROUP:]

    for copy in field_copies + ref_copies + list(firsts.values()) + list(seconds.values()):
        copy.wait_send()
    for copy in turns + crosses + [shared_copy] + list(last_firsts.values()) + last_seconds:
        copy.wait_send()
    for k in range(3):
        @pl.when(is_end | (k < 2))
        def _():
            line_copy(k, 0, "outer").wait_send()
            line_copy(k, 1, "outer").wait_send()
            last_copy(k, "outer").wait_send()

    @pl.when(is_mid)
    def _():
        line_copy(3, 0, "end").wait_send()
        line_copy(3, 1, "end").wait_send()
        last_copy(3, "end").wait_send()


def finish_kernel(pixel_scale, gram_ref, sums_ref, band_ref, diag_ref):
    pix = lax.axis_index("pix")
    odd = pix % 2 == 1
    at = pl.multiple_of((pix // 2) * 128, 128)
    own = sums_ref[0, :, pl.ds(at, 128)]
    other = sums_ref[1, :, pl.ds(at, 128)]
    low = lax.broadcasted_iota(jnp.int32, own.shape, 1) < GROUP
    own = jnp.where(odd, pltpu.roll(own, GROUP, 1), own)
    other = jnp.where(odd, other, pltpu.roll(other, GROUP, 1))
    cols = jnp.where(low, own, other).T

    def unit(real, imag):
        magnitude = jnp.maximum(jnp.sqrt(real * real + imag * imag), 1.0)
        return real / magnitude, imag / magnitude

    col_real, col_imag = unit(cols[:, 0:1], cols[:, 1:2])
    row_real, row_imag = unit(sums_ref[0, 0:1, :], sums_ref[0, 1:2, :])
    unit_real = row_real * col_real + row_imag * col_imag
    unit_imag = row_imag * col_real - row_real * col_imag
    gram_real = gram_ref[0].T
    gram_imag = gram_ref[1].T
    real = (unit_real * gram_real - unit_imag * gram_imag) * pixel_scale
    imag = (unit_real * gram_imag + unit_imag * gram_real) * pixel_scale
    diag_ref[0] = real[:GROUP]
    diag_ref[1] = imag[:GROUP]
    band_ref[0] = real[GROUP:]
    band_ref[1] = imag[GROUP:]


def paired_shards(frames, ref_pixels):
    pixel_rows = frames.shape[1]
    width = frames.shape[2]
    rows = 2 * SIDE + LAST
    b16 = jnp.bfloat16
    dma = pltpu.SemaphoreType.DMA
    gram, sums = pl.pallas_call(
        gram_kernel,
        out_shape=(
            jax.ShapeDtypeStruct((2, width, 128), jnp.float32),
            jax.ShapeDtypeStruct((2, 8, width), jnp.float32),
        ),
        in_specs=[
            pl.BlockSpec(memory_space=pltpu.HBM),
            pl.BlockSpec(memory_space=pltpu.HBM),
        ],
        out_specs=(pl.BlockSpec(memory_space=pltpu.VMEM),) * 2,
        scratch_shapes=[
            pltpu.VMEM((1, ref_pixels.shape[0]), jnp.int32),
            pltpu.VMEM((4, 4, pixel_rows, 4 * GROUP), b16),
            pltpu.VMEM((width + 8 * GROUP, 2 * pixel_rows), b16),
            pltpu.VMEM((width, 2 * pixel_rows), b16),
            pltpu.VMEM((16, rows, 256), b16),
            pltpu.VMEM((2, 4, 2, SIDE, 256), b16),
            pltpu.VMEM((2, 4, SIDE, 256), b16),
            pltpu.VMEM((3, 2 * SIDE, 256), b16),
            pltpu.VMEM((2, 2 * SIDE, 256), b16),
            pltpu.VMEM((2 * SIDE, 256), b16),
            pltpu.VMEM((3, 4, LAST, 256), b16),
            pltpu.VMEM((2, 4, LAST, 256), b16),
            pltpu.VMEM((4, LAST, 256), b16),
            pltpu.VMEM((2, 2, LAST // 2, 256), b16),
            pltpu.VMEM((2, LAST // 2, 256), b16),
            pltpu.VMEM((5, 8, width), jnp.float32),
            pltpu.VMEM((5, 8, width), jnp.float32),
            pltpu.VMEM((rows, 256), jnp.float32),
            pltpu.VMEM((FAR * GROUP, 128), b16),
            pltpu.VMEM((FAR * GROUP, 128), b16),
            pltpu.VMEM((FAR, 128, 128), b16),
            pltpu.VMEM((FAR, 128, 128), b16),
            pltpu.VMEM((128, 128), b16),
            pltpu.VMEM((128, 128), b16),
            dma, dma((4,)), dma((4, 4)), dma((4, 4)),
            dma((2, 4, 2)), dma((2, 4, 2)),
            dma((2, 4)), dma((2, 4)),
            dma((4, 2)), dma((3, 2)), dma((2, 2)), dma((2,)),
            dma((4,)), dma((3,)), dma((2,)), dma,
            dma((2, 2)), dma((2, 2)), dma((2,)), dma((2,)),
            dma((5,)), dma((5,)),
            dma((3,)), dma((3,)),
            dma((FAR,)), dma((FAR,)),
            dma, dma,
        ],
        compiler_params=pltpu.CompilerParams(
            collective_id=0, has_side_effects=True, vmem_limit_bytes=52 * 1024 * 1024
        ),
    )(frames, ref_pixels.reshape(1, -1))
    pixel_scale = 1.0 / math.sqrt(lax.axis_size("pix") * pixel_rows)
    band, diag = pl.pallas_call(
        functools.partial(finish_kernel, pixel_scale),
        out_shape=(jax.ShapeDtypeStruct((2, GROUP, width), jnp.float32),) * 2,
        in_specs=[pl.BlockSpec(memory_space=pltpu.VMEM)] * 2,
        out_specs=(pl.BlockSpec(memory_space=pltpu.VMEM),) * 2,
        compiler_params=pltpu.CompilerParams(vmem_limit_bytes=16 * 1024 * 1024),
    )(gram, sums)
    return (jnp.swapaxes(band, 1, 2), jnp.swapaxes(diag, 1, 2))


def solution(mesh):
    placed = (P(None, "pix", "mode"), P())
    paired = mesh.shape["pix"] == 16 and mesh.shape["mode"] == 2

    def body(frames, ref_pixels):
        if paired and frames.shape[2] == 16 * GROUP:
            return paired_shards(frames, ref_pixels)
        return shards(frames, ref_pixels)

    return jax.shard_map(
        body,
        mesh=mesh,
        in_specs=placed,
        out_specs=(P(None, "mode", "pix"), P(None, "mode", "pix")),
        check_vma=False,
    )
```

```python
import functools
import math

import jax
import jax.numpy as jnp
from jax import lax
from jax.experimental import pallas as pl
from jax.experimental.pallas import tpu as pltpu
from jax.sharding import PartitionSpec as P


def unit_phase(sums):
    magnitude = jnp.maximum(jnp.sqrt(sums[0] * sums[0] + sums[1] * sums[1]), 1.0)
    return sums / magnitude[None, :]


def rotate(gram_real, gram_imag, phase_rows, phase_cols, pixel_scale):
    row_real = phase_rows[0][:, None]
    row_imag = phase_rows[1][:, None]
    col_real = phase_cols[0][None, :]
    col_imag = phase_cols[1][None, :]
    unit_real = row_real * col_real + row_imag * col_imag
    unit_imag = row_imag * col_real - row_real * col_imag
    return jnp.stack(
        [
            (unit_real * gram_real - unit_imag * gram_imag) * pixel_scale,
            (unit_real * gram_imag + unit_imag * gram_real) * pixel_scale,
        ]
    )


def shards(frames, ref_pixels):
    pix_count = lax.axis_size("pix")
    mode_count = lax.axis_size("mode")
    pix_index = lax.axis_index("pix")
    mode_index = lax.axis_index("mode")
    pixel_rows = frames.shape[1]
    block_width = frames.shape[2]
    full_tiles = mode_count // 2 + 1
    full_width = full_tiles * block_width
    frame_float = frames.astype(jnp.float32)
    real_part = (frame_float[0] - frame_float[2]).astype(jnp.bfloat16)
    imag_part = (frame_float[3] - frame_float[1]).astype(jnp.bfloat16)
    fields = jnp.stack([real_part, imag_part])
    positions = pix_index * pixel_rows + lax.iota(jnp.int32, pixel_rows)
    counts = jnp.sum(
        (ref_pixels[:, None] == positions[None, :]).astype(jnp.float32), axis=0
    ).astype(jnp.bfloat16)
    local_ref = jnp.einsum("p,cpm->cm", counts, fields, preferred_element_type=jnp.float32)
    own_ref = lax.psum(local_ref, "pix")
    phase_all = lax.all_gather(unit_phase(own_ref), "mode", axis=1, tiled=True)
    phase_own = lax.dynamic_slice_in_dim(phase_all, mode_index * block_width, block_width, 1)
    phase_twice = jnp.concatenate([phase_all, phase_all], axis=1)
    phase_full = lax.dynamic_slice_in_dim(phase_twice, mode_index * block_width, full_width, 1)
    whole_fields = lax.all_gather(fields, "mode", axis=2, tiled=True)
    tiled = whole_fields.reshape(2, pixel_rows, mode_count, block_width)
    picked = (mode_index + lax.iota(jnp.int32, full_tiles)) % mode_count
    band_fields = jnp.take(tiled, picked, axis=2).reshape(2, pixel_rows, full_width)
    contract = (((0,), (0,)), ((), ()))
    own_real = fields[0]
    own_imag = fields[1]
    band_real = band_fields[0]
    band_imag = band_fields[1]
    gram_real = lax.dot_general(
        own_real, band_real, contract, preferred_element_type=jnp.float32
    ) + lax.dot_general(own_imag, band_imag, contract, preferred_element_type=jnp.float32)
    gram_imag = lax.dot_general(
        own_real, band_imag, contract, preferred_element_type=jnp.float32
    ) - lax.dot_general(own_imag, band_real, contract, preferred_element_type=jnp.float32)
    pixel_scale = 1.0 / math.sqrt(pix_count * pixel_rows)
    raw_terms = jnp.stack([gram_real, gram_imag])
    raw_diag, raw_band = (
        lax.psum_scatter(raw_terms[:, :, :block_width], "pix", scatter_dimension=2, tiled=True),
        lax.psum_scatter(raw_terms[:, :, block_width:], "pix", scatter_dimension=2, tiled=True),
    )
    diag_slice = block_width // pix_count
    band_slice = (full_width - block_width) // pix_count
    diag_cols = lax.dynamic_slice_in_dim(phase_full, pix_index * diag_slice, diag_slice, 1)
    band_cols = lax.dynamic_slice_in_dim(
        phase_full, block_width + pix_index * band_slice, band_slice, 1
    )
    diag_out = rotate(raw_diag[0], raw_diag[1], phase_own, diag_cols, pixel_scale)
    band_out = rotate(raw_band[0], raw_band[1], phase_own, band_cols, pixel_scale)
    return (band_out, diag_out)


MESH = pl.DeviceIdType.MESH
GROUP = 64
NEAR = 9
SIDE = 224
LAST = 96
PACK = GROUP // 2
FAR = 7


def gram_kernel(
    frames_hbm, pixels_hbm, gram_ref, sums_ref,
    pixels_ref, frames_ref, own, other, part, first_in, second_in, outer_in, inner_in, end_in,
    last_outer_in, last_inner_in, last_end_in, last_first_in, last_second_in,
    ref_out, ref_in, total, turn_out, turn_in, shared_out, shared_in,
    pixel_sem, frame_sem, field_send, field_recv, first_send, first_recv, second_send, second_recv,
    line_send, outer_recv, inner_recv, end_recv,
    last_send, last_outer_recv, last_inner_recv, last_end_recv,
    last_first_send, last_first_recv, last_second_send, last_second_recv, ref_send, ref_recv,
    turn_send, turn_recv, shared_send, shared_recv,
):
    pix = lax.axis_index("pix")
    mode = lax.axis_index("mode")
    x, y, z = pix % 2, (pix // 2) % 2, pix // 4
    upper = z >= 2
    is_end = (z == 0) | (z == 3)
    is_mid = (z == 1) | (z == 2)
    x_peer = pix + 1 - 2 * x
    y_peer = pix + 2 - 4 * y
    inner_peer = jnp.where(upper, pix - 4, pix + 4)
    outer_peer = jnp.where(upper, pix + 4, pix - 4)
    z_even_peer = pix + 4 - 8 * (z % 2)
    z_far_peer = pix + 8 - 16 * (z // 2)
    pixel_rows = frames_hbm.shape[1]
    width = frames_hbm.shape[2]
    rows = NEAR * GROUP
    top = rows - GROUP
    chunk = 4 * GROUP

    def chunk_z(k):
        return jnp.where(upper, k, 3 - k)

    def chunk_modes(k):
        return pl.ds(pl.multiple_of(chunk_z(k) * chunk, chunk), chunk)

    loads = [
        pltpu.make_async_copy(
            frames_hbm.at[:, :, chunk_modes(k)], frames_ref.at[k], frame_sem.at[k]
        )
        for k in range(4)
    ]
    for load in loads:
        load.start()
    listing = pltpu.make_async_copy(pixels_hbm, pixels_ref, pixel_sem)
    listing.start()
    barrier = pltpu.get_barrier_semaphore()
    for step in range(1, 16):
        for to_mode in (mode, 1 - mode):
            pl.semaphore_signal(
                barrier, inc=1, device_id=((pix + step) % 16, to_mode), device_id_type=MESH
            )
    pl.semaphore_signal(barrier, inc=1, device_id=(pix, 1 - mode), device_id_type=MESH)

    def send(src, dst, send_sem, recv_sem, to_pix, to_mode):
        copy = pltpu.make_async_remote_copy(
            src_ref=src, dst_ref=dst, send_sem=send_sem, recv_sem=recv_sem,
            device_id=(to_pix, to_mode), device_id_type=MESH,
        )
        return copy

    def ring_rows(zz, column):
        return pl.ds(pl.multiple_of((column * 4 + zz) * GROUP, GROUP), GROUP)

    for k in range(4):
        loads[k].wait()
        frame = [frames_ref[k, step].astype(jnp.float32) for step in range(4)]
        real = (frame[0] - frame[2]).astype(jnp.bfloat16).T
        imag = (frame[3] - frame[1]).astype(jnp.bfloat16).T
        for i in range(4):
            to = ring_rows(chunk_z(k), i)
            own[to, 0:pixel_rows] = real[i * GROUP:(i + 1) * GROUP]
            own[to, pixel_rows:2 * pixel_rows] = imag[i * GROUP:(i + 1) * GROUP]
    own[pl.ds(width, 8 * GROUP), :] = own[pl.ds(0, 8 * GROUP), :]
    pl.semaphore_wait(barrier, 31)

    def field_copy(k, i):
        at = ring_rows(chunk_z(k), i)
        return send(
            own.at[at], other.at[at], field_send.at[k, i], field_recv.at[k, i], pix, 1 - mode
        )

    field_copies = [field_copy(k, i) for k in range(4) for i in range(4)]
    for copy in field_copies:
        copy.start()

    ref_peers = [x_peer, y_peer, z_even_peer, z_far_peer, pix]

    def ref_copy(step):
        return send(
            ref_out.at[step], ref_in.at[step], ref_send.at[step], ref_recv.at[step],
            ref_peers[step], mode if step < 4 else 1 - mode,
        )

    ref_copies = [ref_copy(step) for step in range(5)]

    def ref_next(step):
        ref_copies[step].wait_recv()
        ref_out[step + 1] = ref_out[step] + ref_in[step]
        ref_copies[step + 1].start()

    contract = (((1,), (1,)), ((), ()))

    def turned(block):
        return jnp.concatenate([block[:, pixel_rows:], -block[:, :pixel_rows]], axis=1)

    def multiply(k):
        zc = chunk_z(k)
        for i in range(4):
            field_copies[4 * k + i].wait_recv()
        for t in range(4):
            column = (1 - y if t % 2 == 0 else y) * 2 + (1 - x if t < 2 else x)
            start = pl.multiple_of((column * 4 + zc) * GROUP, GROUP)
            own_cols = own[pl.ds(start, GROUP), :]
            other_cols = other[pl.ds(start, GROUP), :]
            cols = jnp.concatenate(
                [own_cols, turned(own_cols), other_cols, turned(other_cols)], axis=0
            )
            left = own[pl.ds(start, rows), :]
            out = lax.dot_general(left, cols, contract, preferred_element_type=jnp.float32)
            part[zc * 4 + column, pl.ds(0, top)] = out[:top].astype(jnp.bfloat16)
            owner_y = 1 - y if t % 2 == 0 else y
            shared = jnp.where(owner_y == 0, out[top:, 0:128], out[top:, 128:256])
            part[zc * 4 + column, pl.ds(top, PACK)] = jnp.concatenate(
                [shared[:PACK], shared[PACK:]], axis=1
            ).astype(jnp.bfloat16)
            if k < 2:
                for a, j in (((0, 0), (1, 0)), ((0, 1),), ((1, 1),), ())[t]:
                    firsts[a, k, j].start()

    spans = [pl.ds(0, SIDE), pl.ds(SIDE, SIDE)]
    last = pl.ds(2 * SIDE, LAST)
    last_spans = [pl.ds(2 * SIDE, LAST // 2), pl.ds(2 * SIDE + LAST // 2, LAST // 2)]

    def owner_of(k, yy, xx):
        return chunk_z(k) * 4 + yy * 2 + xx

    def first_copy(axis, k, j):
        if axis == 0:
            owner = owner_of(k, 1 - y if j == 0 else y, 1 - x)
        else:
            owner = owner_of(k, 1 - y, 1 - x if j == 0 else x)
        return send(
            part.at[owner, spans[axis]], first_in.at[axis, k, j],
            first_send.at[axis, k, j], first_recv.at[axis, k, j],
            x_peer if axis == 0 else y_peer, mode,
        )

    def second_owner(axis, k):
        return owner_of(k, 1 - y, x) if axis == 0 else owner_of(k, y, 1 - x)

    def second_copy(axis, k):
        return send(
            part.at[second_owner(axis, k), spans[axis]], second_in.at[axis, k],
            second_send.at[axis, k], second_recv.at[axis, k],
            y_peer if axis == 0 else x_peer, mode,
        )

    firsts = {(a, k, j): first_copy(a, k, j) for a in range(2) for k in range(4) for j in range(2)}
    seconds = {(a, k): second_copy(a, k) for a in range(2) for k in range(4)}

    def f32(value):
        return value.astype(jnp.float32)

    def start_first(k):
        for j in range(2):
            for a in range(2):
                firsts[a, k, j].start()

    def forward(k):
        for a in range(2):
            firsts[a, k, 0].wait_recv()
            owner = second_owner(a, k)
            part[owner, spans[a]] = (
                f32(part[owner, spans[a]]) + f32(first_in[a, k, 0])
            ).astype(jnp.bfloat16)
            seconds[a, k].start()

    def line_copy(k, a, to):
        owner = owner_of(k, y, x)
        span = spans[a]
        if to == "outer":
            dst, sem = outer_in.at[k, span], outer_recv.at[k, a]
        elif to == "inner":
            dst, sem = inner_in.at[k, span], inner_recv.at[k, a]
        else:
            dst, sem = end_in.at[span], end_recv.at[a]
        return send(
            part.at[owner, span], dst, line_send.at[k, a], sem,
            outer_peer if to == "end" else inner_peer, mode,
        )

    def keep(k):
        owner = owner_of(k, y, x)
        for a in (1, 0):
            firsts[a, k, 1].wait_recv()
            seconds[a, k].wait_recv()
            span = spans[a]
            value = f32(part[owner, span]) + f32(first_in[a, k, 1]) + f32(second_in[a, k])
            if k >= 2:
                @pl.when(is_mid if k == 2 else is_end)
                def _():
                    total[span, :] = value
            part[owner, span] = value.astype(jnp.bfloat16)
            if k < 3:
                @pl.when(is_end)
                def _():
                    line_copy(k, a, "outer").start()
            else:
                pass_on(k, a)

    def pass_on(k, a):
        owner = owner_of(k, y, x)
        span = spans[a]

        @pl.when(is_mid)
        def _():
            if k < 2:
                line_copy(k, a, "outer").wait_recv()
                arrived = outer_in[k, span]
            else:
                line_copy(0, a, "inner").wait_recv()
                arrived = inner_in[0, span]
            part[owner, span] = (f32(part[owner, span]) + f32(arrived)).astype(jnp.bfloat16)
            line_copy(k, a, "inner" if k < 2 else "end").start()

    def line_end(a):
        span = spans[a]

        @pl.when(is_mid)
        def _():
            line_copy(2, a, "outer").wait_recv()
            line_copy(1, a, "inner").wait_recv()
            total[span, :] = total[span, :] + f32(outer_in[2, span]) + f32(inner_in[1, span])

        @pl.when(is_end)
        def _():
            line_copy(3, a, "end").wait_recv()
            total[span, :] = total[span, :] + f32(end_in[span])

    def last_copy(k, to):
        owners = pl.ds(chunk_z(k) * 4, 4)
        if to == "outer":
            dst, sem = last_outer_in.at[k], last_outer_recv.at[k]
        elif to == "inner":
            dst, sem = last_inner_in.at[k], last_inner_recv.at[k]
        else:
            dst, sem = last_end_in, last_end_recv
        return send(
            part.at[owners, last], dst, last_send.at[k], sem,
            outer_peer if to == "end" else inner_peer, mode,
        )

    def last_begin(k):
        @pl.when(is_end)
        def _():
            last_copy(k, "outer").start()

    def last_add(k, terms):
        first = chunk_z(k) * 4
        for i in range(4):
            value = f32(part[first + i, last])
            for term in terms:
                value = value + f32(term[i])
            part[first + i, last] = value.astype(jnp.bfloat16)

    def last_pass(k):
        @pl.when(is_mid)
        def _():
            if k < 2:
                last_copy(k, "outer").wait_recv()
                last_add(k, [last_outer_in.at[k]])
                last_copy(k, "inner").start()
            else:
                last_copy(0, "inner").wait_recv()
                last_add(k, [last_inner_in.at[0]])
                last_copy(k, "end").start()

    def last_first_copy(axis, j):
        if axis == 0:
            owner = z * 4 + (1 - y if j == 0 else y) * 2 + 1 - x
        else:
            owner = z * 4 + (1 - y) * 2 + (1 - x if j == 0 else x)
        return send(
            part.at[owner, last_spans[axis]], last_first_in.at[axis, j],
            last_first_send.at[axis, j], last_first_recv.at[axis, j],
            x_peer if axis == 0 else y_peer, mode,
        )

    def last_second_owner(axis):
        return z * 4 + (1 - y) * 2 + x if axis == 0 else z * 4 + y * 2 + 1 - x

    def last_second_copy(axis):
        return send(
            part.at[last_second_owner(axis), last_spans[axis]], last_second_in.at[axis],
            last_second_send.at[axis], last_second_recv.at[axis],
            y_peer if axis == 0 else x_peer, mode,
        )

    last_firsts = {(a, j): last_first_copy(a, j) for a in range(2) for j in range(2)}
    last_seconds = [last_second_copy(a) for a in range(2)]

    def last_spread():
        @pl.when(is_mid)
        def _():
            last_copy(2, "outer").wait_recv()
            last_copy(1, "inner").wait_recv()
            last_add(2, [last_outer_in.at[2], last_inner_in.at[1]])

        @pl.when(is_end)
        def _():
            last_copy(3, "end").wait_recv()
            last_add(3, [last_end_in])

        for j in range(2):
            for a in range(2):
                last_firsts[a, j].start()

    def last_forward():
        for a in range(2):
            last_firsts[a, 0].wait_recv()
            owner = last_second_owner(a)
            part[owner, last_spans[a]] = (
                f32(part[owner, last_spans[a]]) + f32(last_first_in[a, 0])
            ).astype(jnp.bfloat16)
            last_seconds[a].start()

    def last_keep():
        for a in range(2):
            last_firsts[a, 1].wait_recv()
            last_seconds[a].wait_recv()
            total[last_spans[a], :] = (
                f32(part[pix, last_spans[a]]) + f32(last_first_in[a, 1]) + f32(last_second_in[a])
            )

    ring = pix % 4 * 4 + z

    def chip_at(step):
        there = (ring + step) % 16
        return there % 4 * 4 + there // 4

    mirror_rows = [(FAR, FAR + 1), (4, FAR), (1, 4)]

    def mirror(i):
        for d in range(*mirror_rows[i]):
            for rel in range(2):
                block = total[
                    d * GROUP:(d + 1) * GROUP, rel * 128:(rel + 1) * 128
                ].astype(jnp.bfloat16)
                stacked = jnp.concatenate([block[:, :GROUP], block[:, GROUP:]], axis=0)
                turn_out[d - 1, rel] = stacked.T
                turns[d - 1][rel].start()

    shared_copy = send(
        shared_out, shared_in, shared_send, shared_recv,
        y_peer, jnp.where(y == 0, mode, 1 - mode),
    )
    turns = [
        [
            send(
                turn_out.at[d - 1, rel], turn_in.at[d - 1, rel],
                turn_send.at[d - 1, rel], turn_recv.at[d - 1, rel],
                chip_at(d), mode if rel == 0 else 1 - mode,
            )
            for rel in range(2)
        ]
        for d in range(1, FAR + 1)
    ]

    for k in range(3):
        multiply(k)
        last_begin(k)
    positions = pix * pixel_rows + lax.broadcasted_iota(
        jnp.int32, (pixels_ref.shape[1], pixel_rows), 1
    )
    listing.wait()
    listed = jnp.broadcast_to(pixels_ref[...], (8, pixels_ref.shape[1])).T[:, 0:1]
    counts = jnp.sum(
        jnp.where(listed == positions, 1.0, 0.0), axis=0, keepdims=True
    )
    nothing = jnp.zeros_like(counts)
    row = lax.broadcasted_iota(jnp.int32, (16, 2 * pixel_rows), 0)
    real_weight = jnp.concatenate([counts, nothing], axis=1)
    imag_weight = jnp.concatenate([nothing, counts], axis=1)
    weight = jnp.where(row == 0, real_weight, jnp.where(row == 1, imag_weight, 0.0))
    weight = weight.astype(jnp.bfloat16)
    for pair in range(8):
        places = [(p % 4 * 4 + p // 4) * GROUP for p in (2 * pair, 2 * pair + 1)]
        block = jnp.concatenate([own[pl.ds(at, GROUP), :] for at in places], axis=0)
        ref_out[0, :, pl.ds(pair * 128, 128)] = lax.dot_general(
            weight, block, contract, preferred_element_type=jnp.float32
        )[0:8]
    ref_copies[0].start()
    forward(0)
    start_first(2)
    multiply(3)
    ref_next(0)
    last_pass(0)
    forward(1)
    start_first(3)
    last_pass(1)
    ref_next(1)
    keep(0)
    forward(2)
    last_pass(3)
    ref_next(2)
    last_spread()
    keep(1)
    pass_on(0, 1)
    pass_on(0, 0)
    ref_next(3)
    forward(3)
    last_forward()
    keep(2)
    pass_on(1, 1)
    pass_on(1, 0)
    last_keep()
    mirror(0)
    shared = jnp.concatenate(
        [total[top:top + PACK, 0:128], total[top:top + PACK, 128:256]], axis=0
    )
    shared_out[...] = jnp.concatenate([shared, shared], axis=0).astype(jnp.bfloat16).T
    shared_copy.start()
    keep(3)
    line_end(1)
    mirror(1)

    lane = lax.broadcasted_iota(jnp.int32, (GROUP, 128), 1)
    low = lane < GROUP

    def group_rows(step):
        return pl.ds(pl.multiple_of(chip_at(step) * GROUP, GROUP), GROUP)

    def place(d):
        here = total[d * GROUP:(d + 1) * GROUP, 0:128]
        there = total[d * GROUP:(d + 1) * GROUP, 128:256]
        gram_ref[0, group_rows(d), :] = jnp.where(low, here, pltpu.roll(there, GROUP, 1))
        gram_ref[1, group_rows(d), :] = jnp.where(low, pltpu.roll(here, GROUP, 1), there)

    line_end(0)
    mirror(2)
    for d in range(NEAR - 1):
        place(d)
    shared_copy.wait_recv()
    arrived = f32(shared_in[...])
    mine = low == (y == 0)
    shared = jnp.concatenate(
        [total[top:top + PACK, 0:128], total[top:top + PACK, 128:256]], axis=0
    )
    rolled = pltpu.roll(shared, GROUP, 1)
    gram_ref[0, group_rows(8), :] = jnp.where(
        mine, jnp.where(low, shared, rolled), arrived[0:GROUP]
    )
    gram_ref[1, group_rows(8), :] = jnp.where(
        mine, jnp.where(low, rolled, shared), -arrived[GROUP:]
    )
    ref_copies[4].wait_recv()
    sums_ref[0] = ref_out[4]
    sums_ref[1] = ref_in[4]
    for d in range(1, FAR + 1):
        for rel in range(2):
            turns[d - 1][rel].wait_recv()
        here = f32(turn_in[d - 1, 0])
        there = f32(turn_in[d - 1, 1])
        gram_ref[0, group_rows(16 - d), :] = jnp.where(low, here, pltpu.roll(there, GROUP, 1))
        gram_ref[1, group_rows(16 - d), :] = -jnp.where(low, pltpu.roll(here, GROUP, 1), there)

    for copy in field_copies + ref_copies + list(firsts.values()) + list(seconds.values()):
        copy.wait_send()
    for copy in sum(turns, []) + [shared_copy] + list(last_firsts.values()) + last_seconds:
        copy.wait_send()
    for k in range(3):
        @pl.when(is_end | (k < 2))
        def _():
            line_copy(k, 0, "outer").wait_send()
            line_copy(k, 1, "outer").wait_send()
            last_copy(k, "outer").wait_send()

    @pl.when(is_mid)
    def _():
        line_copy(3, 0, "end").wait_send()
        line_copy(3, 1, "end").wait_send()
        last_copy(3, "end").wait_send()


def finish_kernel(pixel_scale, gram_ref, sums_ref, band_ref, diag_ref):
    pix = lax.axis_index("pix")
    odd = pix % 2 == 1
    at = pl.multiple_of((pix // 2) * 128, 128)
    own = sums_ref[0, :, pl.ds(at, 128)]
    other = sums_ref[1, :, pl.ds(at, 128)]
    low = lax.broadcasted_iota(jnp.int32, own.shape, 1) < GROUP
    own = jnp.where(odd, pltpu.roll(own, GROUP, 1), own)
    other = jnp.where(odd, other, pltpu.roll(other, GROUP, 1))
    cols = jnp.where(low, own, other).T

    def unit(real, imag):
        magnitude = jnp.maximum(jnp.sqrt(real * real + imag * imag), 1.0)
        return real / magnitude, imag / magnitude

    col_real, col_imag = unit(cols[:, 0:1], cols[:, 1:2])
    row_real, row_imag = unit(sums_ref[0, 0:1, :], sums_ref[0, 1:2, :])
    unit_real = row_real * col_real + row_imag * col_imag
    unit_imag = row_imag * col_real - row_real * col_imag
    gram_real = gram_ref[0].T
    gram_imag = gram_ref[1].T
    real = (unit_real * gram_real - unit_imag * gram_imag) * pixel_scale
    imag = (unit_real * gram_imag + unit_imag * gram_real) * pixel_scale
    diag_ref[0] = real[:GROUP]
    diag_ref[1] = imag[:GROUP]
    band_ref[0] = real[GROUP:]
    band_ref[1] = imag[GROUP:]


def paired_shards(frames, ref_pixels):
    pixel_rows = frames.shape[1]
    width = frames.shape[2]
    rows = 2 * SIDE + LAST
    b16 = jnp.bfloat16
    dma = pltpu.SemaphoreType.DMA
    gram, sums = pl.pallas_call(
        gram_kernel,
        out_shape=(
            jax.ShapeDtypeStruct((2, width, 128), jnp.float32),
            jax.ShapeDtypeStruct((2, 8, width), jnp.float32),
        ),
        in_specs=[
            pl.BlockSpec(memory_space=pltpu.HBM),
            pl.BlockSpec(memory_space=pltpu.HBM),
        ],
        out_specs=(pl.BlockSpec(memory_space=pltpu.VMEM),) * 2,
        scratch_shapes=[
            pltpu.VMEM((1, ref_pixels.shape[0]), jnp.int32),
            pltpu.VMEM((4, 4, pixel_rows, 4 * GROUP), b16),
            pltpu.VMEM((width + 8 * GROUP, 2 * pixel_rows), b16),
            pltpu.VMEM((width, 2 * pixel_rows), b16),
            pltpu.VMEM((16, rows, 256), b16),
            pltpu.VMEM((2, 4, 2, SIDE, 256), b16),
            pltpu.VMEM((2, 4, SIDE, 256), b16),
            pltpu.VMEM((3, 2 * SIDE, 256), b16),
            pltpu.VMEM((2, 2 * SIDE, 256), b16),
            pltpu.VMEM((2 * SIDE, 256), b16),
            pltpu.VMEM((3, 4, LAST, 256), b16),
            pltpu.VMEM((2, 4, LAST, 256), b16),
            pltpu.VMEM((4, LAST, 256), b16),
            pltpu.VMEM((2, 2, LAST // 2, 256), b16),
            pltpu.VMEM((2, LAST // 2, 256), b16),
            pltpu.VMEM((5, 8, width), jnp.float32),
            pltpu.VMEM((5, 8, width), jnp.float32),
            pltpu.VMEM((rows, 256), jnp.float32),
            pltpu.VMEM((FAR, 2, GROUP, 128), b16),
            pltpu.VMEM((FAR, 2, GROUP, 128), b16),
            pltpu.VMEM((128, 128), b16),
            pltpu.VMEM((128, 128), b16),
            dma, dma((4,)), dma((4, 4)), dma((4, 4)),
            dma((2, 4, 2)), dma((2, 4, 2)),
            dma((2, 4)), dma((2, 4)),
            dma((4, 2)), dma((3, 2)), dma((2, 2)), dma((2,)),
            dma((4,)), dma((3,)), dma((2,)), dma,
            dma((2, 2)), dma((2, 2)), dma((2,)), dma((2,)),
            dma((5,)), dma((5,)),
            dma((FAR, 2)), dma((FAR, 2)),
            dma, dma,
        ],
        compiler_params=pltpu.CompilerParams(
            collective_id=0, has_side_effects=True, vmem_limit_bytes=52 * 1024 * 1024
        ),
    )(frames, ref_pixels.reshape(1, -1))
    pixel_scale = 1.0 / math.sqrt(lax.axis_size("pix") * pixel_rows)
    band, diag = pl.pallas_call(
        functools.partial(finish_kernel, pixel_scale),
        out_shape=(jax.ShapeDtypeStruct((2, GROUP, width), jnp.float32),) * 2,
        in_specs=[pl.BlockSpec(memory_space=pltpu.VMEM)] * 2,
        out_specs=(pl.BlockSpec(memory_space=pltpu.VMEM),) * 2,
        compiler_params=pltpu.CompilerParams(vmem_limit_bytes=16 * 1024 * 1024),
    )(gram, sums)
    return (jnp.swapaxes(band, 1, 2), jnp.swapaxes(diag, 1, 2))


def solution(mesh):
    placed = (P(None, "pix", "mode"), P())
    paired = mesh.shape["pix"] == 16 and mesh.shape["mode"] == 2

    def body(frames, ref_pixels):
        if paired and frames.shape[2] == 16 * GROUP:
            return paired_shards(frames, ref_pixels)
        return shards(frames, ref_pixels)

    return jax.shard_map(
        body,
        mesh=mesh,
        in_specs=placed,
        out_specs=(P(None, "mode", "pix"), P(None, "mode", "pix")),
        check_vma=False,
    )
```

```python
import functools
import math

import jax
import jax.numpy as jnp
from jax import lax
from jax.experimental import pallas as pl
from jax.experimental.pallas import tpu as pltpu
from jax.sharding import PartitionSpec as P


def unit_phase(sums):
    magnitude = jnp.maximum(jnp.sqrt(sums[0] * sums[0] + sums[1] * sums[1]), 1.0)
    return sums / magnitude[None, :]


def rotate(gram_real, gram_imag, phase_rows, phase_cols, pixel_scale):
    row_real = phase_rows[0][:, None]
    row_imag = phase_rows[1][:, None]
    col_real = phase_cols[0][None, :]
    col_imag = phase_cols[1][None, :]
    unit_real = row_real * col_real + row_imag * col_imag
    unit_imag = row_imag * col_real - row_real * col_imag
    return jnp.stack(
        [
            (unit_real * gram_real - unit_imag * gram_imag) * pixel_scale,
            (unit_real * gram_imag + unit_imag * gram_real) * pixel_scale,
        ]
    )


def shards(frames, ref_pixels):
    pix_count = lax.axis_size("pix")
    mode_count = lax.axis_size("mode")
    pix_index = lax.axis_index("pix")
    mode_index = lax.axis_index("mode")
    pixel_rows = frames.shape[1]
    block_width = frames.shape[2]
    full_tiles = mode_count // 2 + 1
    full_width = full_tiles * block_width
    frame_float = frames.astype(jnp.float32)
    real_part = (frame_float[0] - frame_float[2]).astype(jnp.bfloat16)
    imag_part = (frame_float[3] - frame_float[1]).astype(jnp.bfloat16)
    fields = jnp.stack([real_part, imag_part])
    positions = pix_index * pixel_rows + lax.iota(jnp.int32, pixel_rows)
    counts = jnp.sum(
        (ref_pixels[:, None] == positions[None, :]).astype(jnp.float32), axis=0
    ).astype(jnp.bfloat16)
    local_ref = jnp.einsum("p,cpm->cm", counts, fields, preferred_element_type=jnp.float32)
    own_ref = lax.psum(local_ref, "pix")
    phase_all = lax.all_gather(unit_phase(own_ref), "mode", axis=1, tiled=True)
    phase_own = lax.dynamic_slice_in_dim(phase_all, mode_index * block_width, block_width, 1)
    phase_twice = jnp.concatenate([phase_all, phase_all], axis=1)
    phase_full = lax.dynamic_slice_in_dim(phase_twice, mode_index * block_width, full_width, 1)
    whole_fields = lax.all_gather(fields, "mode", axis=2, tiled=True)
    tiled = whole_fields.reshape(2, pixel_rows, mode_count, block_width)
    picked = (mode_index + lax.iota(jnp.int32, full_tiles)) % mode_count
    band_fields = jnp.take(tiled, picked, axis=2).reshape(2, pixel_rows, full_width)
    contract = (((0,), (0,)), ((), ()))
    own_real = fields[0]
    own_imag = fields[1]
    band_real = band_fields[0]
    band_imag = band_fields[1]
    gram_real = lax.dot_general(
        own_real, band_real, contract, preferred_element_type=jnp.float32
    ) + lax.dot_general(own_imag, band_imag, contract, preferred_element_type=jnp.float32)
    gram_imag = lax.dot_general(
        own_real, band_imag, contract, preferred_element_type=jnp.float32
    ) - lax.dot_general(own_imag, band_real, contract, preferred_element_type=jnp.float32)
    pixel_scale = 1.0 / math.sqrt(pix_count * pixel_rows)
    raw_terms = jnp.stack([gram_real, gram_imag])
    raw_diag, raw_band = (
        lax.psum_scatter(raw_terms[:, :, :block_width], "pix", scatter_dimension=2, tiled=True),
        lax.psum_scatter(raw_terms[:, :, block_width:], "pix", scatter_dimension=2, tiled=True),
    )
    diag_slice = block_width // pix_count
    band_slice = (full_width - block_width) // pix_count
    diag_cols = lax.dynamic_slice_in_dim(phase_full, pix_index * diag_slice, diag_slice, 1)
    band_cols = lax.dynamic_slice_in_dim(
        phase_full, block_width + pix_index * band_slice, band_slice, 1
    )
    diag_out = rotate(raw_diag[0], raw_diag[1], phase_own, diag_cols, pixel_scale)
    band_out = rotate(raw_band[0], raw_band[1], phase_own, band_cols, pixel_scale)
    return (band_out, diag_out)


MESH = pl.DeviceIdType.MESH
GROUP = 64
NEAR = 9
SIDE = 224
LAST = 96
PACK = GROUP // 2
FAR = 7


def gram_kernel(
    frames_hbm, pixels_hbm, gram_ref, sums_ref,
    pixels_ref, frames_ref, own, other, part, first_in, second_in, outer_in, inner_in, end_in,
    last_outer_in, last_inner_in, last_end_in, last_first_in, last_second_in,
    ref_out, ref_in, total, cross_out, cross_in, turn_out, turn_in, shared_out, shared_in,
    pixel_sem, frame_sem, field_send, field_recv, first_send, first_recv, second_send, second_recv,
    line_send, outer_recv, inner_recv, end_recv,
    last_send, last_outer_recv, last_inner_recv, last_end_recv,
    last_first_send, last_first_recv, last_second_send, last_second_recv, ref_send, ref_recv,
    cross_send, cross_recv, turn_send, turn_recv, shared_send, shared_recv,
):
    pix = lax.axis_index("pix")
    mode = lax.axis_index("mode")
    x, y, z = pix % 2, (pix // 2) % 2, pix // 4
    upper = z >= 2
    is_end = (z == 0) | (z == 3)
    is_mid = (z == 1) | (z == 2)
    x_peer = pix + 1 - 2 * x
    y_peer = pix + 2 - 4 * y
    inner_peer = jnp.where(upper, pix - 4, pix + 4)
    outer_peer = jnp.where(upper, pix + 4, pix - 4)
    z_even_peer = pix + 4 - 8 * (z % 2)
    z_far_peer = pix + 8 - 16 * (z // 2)
    pixel_rows = frames_hbm.shape[1]
    width = frames_hbm.shape[2]
    rows = NEAR * GROUP
    top = rows - GROUP
    chunk = 4 * GROUP

    def chunk_z(k):
        return jnp.where(upper, k, 3 - k)

    def chunk_modes(k):
        return pl.ds(pl.multiple_of(chunk_z(k) * chunk, chunk), chunk)

    loads = [
        pltpu.make_async_copy(
            frames_hbm.at[:, :, chunk_modes(k)], frames_ref.at[k], frame_sem.at[k]
        )
        for k in range(4)
    ]
    for load in loads:
        load.start()
    listing = pltpu.make_async_copy(pixels_hbm, pixels_ref, pixel_sem)
    listing.start()
    barrier = pltpu.get_barrier_semaphore()
    for step in range(1, 16):
        pl.semaphore_signal(
            barrier, inc=1, device_id=((pix + step) % 16, mode), device_id_type=MESH
        )
    pl.semaphore_signal(barrier, inc=1, device_id=(pix, 1 - mode), device_id_type=MESH)
    pl.semaphore_signal(barrier, inc=1, device_id=(y_peer, 1 - mode), device_id_type=MESH)

    def send(src, dst, send_sem, recv_sem, to_pix, to_mode):
        copy = pltpu.make_async_remote_copy(
            src_ref=src, dst_ref=dst, send_sem=send_sem, recv_sem=recv_sem,
            device_id=(to_pix, to_mode), device_id_type=MESH,
        )
        return copy

    def ring_rows(zz, column):
        return pl.ds(pl.multiple_of((column * 4 + zz) * GROUP, GROUP), GROUP)

    for k in range(4):
        loads[k].wait()
        frame = [frames_ref[k, step].astype(jnp.float32) for step in range(4)]
        real = (frame[0] - frame[2]).astype(jnp.bfloat16).T
        imag = (frame[3] - frame[1]).astype(jnp.bfloat16).T
        for i in range(4):
            to = ring_rows(chunk_z(k), i)
            own[to, 0:pixel_rows] = real[i * GROUP:(i + 1) * GROUP]
            own[to, pixel_rows:2 * pixel_rows] = imag[i * GROUP:(i + 1) * GROUP]
    own[pl.ds(width, 8 * GROUP), :] = own[pl.ds(0, 8 * GROUP), :]
    pl.semaphore_wait(barrier, 17)

    def field_copy(k, i):
        at = ring_rows(chunk_z(k), i)
        return send(
            own.at[at], other.at[at], field_send.at[k, i], field_recv.at[k, i], pix, 1 - mode
        )

    field_copies = [field_copy(k, i) for k in range(4) for i in range(4)]
    for copy in field_copies:
        copy.start()

    ref_peers = [x_peer, y_peer, z_even_peer, z_far_peer, pix]

    def ref_copy(step):
        return send(
            ref_out.at[step], ref_in.at[step], ref_send.at[step], ref_recv.at[step],
            ref_peers[step], mode if step < 4 else 1 - mode,
        )

    ref_copies = [ref_copy(step) for step in range(5)]

    def ref_next(step):
        ref_copies[step].wait_recv()
        ref_out[step + 1] = ref_out[step] + ref_in[step]
        ref_copies[step + 1].start()

    contract = (((1,), (1,)), ((), ()))

    def turned(block):
        return jnp.concatenate([block[:, pixel_rows:], -block[:, :pixel_rows]], axis=1)

    def multiply(k):
        zc = chunk_z(k)
        for i in range(4):
            field_copies[4 * k + i].wait_recv()
        for t in range(4):
            column = (1 - y if t % 2 == 0 else y) * 2 + (1 - x if t < 2 else x)
            start = pl.multiple_of((column * 4 + zc) * GROUP, GROUP)
            own_cols = own[pl.ds(start, GROUP), :]
            other_cols = other[pl.ds(start, GROUP), :]
            cols = jnp.concatenate(
                [own_cols, turned(own_cols), other_cols, turned(other_cols)], axis=0
            )
            left = own[pl.ds(start, rows), :]
            out = lax.dot_general(left, cols, contract, preferred_element_type=jnp.float32)
            part[zc * 4 + column, pl.ds(0, top)] = out[:top].astype(jnp.bfloat16)
            owner_y = 1 - y if t % 2 == 0 else y
            shared = jnp.where(owner_y == 0, out[top:, 0:128], out[top:, 128:256])
            part[zc * 4 + column, pl.ds(top, PACK)] = jnp.concatenate(
                [shared[:PACK], shared[PACK:]], axis=1
            ).astype(jnp.bfloat16)
            if k < 3:
                for a, j in (((0, 0), (1, 0)), ((0, 1),), ((1, 1),), ())[t]:
                    firsts[a, k, j].start()

    spans = [pl.ds(0, SIDE), pl.ds(SIDE, SIDE)]
    last = pl.ds(2 * SIDE, LAST)
    last_spans = [pl.ds(2 * SIDE, LAST // 2), pl.ds(2 * SIDE + LAST // 2, LAST // 2)]

    def owner_of(k, yy, xx):
        return chunk_z(k) * 4 + yy * 2 + xx

    def first_copy(axis, k, j):
        if axis == 0:
            owner = owner_of(k, 1 - y if j == 0 else y, 1 - x)
        else:
            owner = owner_of(k, 1 - y, 1 - x if j == 0 else x)
        return send(
            part.at[owner, spans[axis]], first_in.at[axis, k, j],
            first_send.at[axis, k, j], first_recv.at[axis, k, j],
            x_peer if axis == 0 else y_peer, mode,
        )

    def second_owner(axis, k):
        return owner_of(k, 1 - y, x) if axis == 0 else owner_of(k, y, 1 - x)

    def second_copy(axis, k):
        return send(
            part.at[second_owner(axis, k), spans[axis]], second_in.at[axis, k],
            second_send.at[axis, k], second_recv.at[axis, k],
            y_peer if axis == 0 else x_peer, mode,
        )

    firsts = {(a, k, j): first_copy(a, k, j) for a in range(2) for k in range(4) for j in range(2)}
    seconds = {(a, k): second_copy(a, k) for a in range(2) for k in range(4)}

    def f32(value):
        return value.astype(jnp.float32)

    def start_first(k):
        for j in range(2):
            for a in range(2):
                firsts[a, k, j].start()

    def forward(k):
        for a in range(2):
            firsts[a, k, 0].wait_recv()
            owner = second_owner(a, k)
            part[owner, spans[a]] = (
                f32(part[owner, spans[a]]) + f32(first_in[a, k, 0])
            ).astype(jnp.bfloat16)
            seconds[a, k].start()

    def line_copy(k, a, to):
        owner = owner_of(k, y, x)
        span = spans[a]
        if to == "outer":
            dst, sem = outer_in.at[k, span], outer_recv.at[k, a]
        elif to == "inner":
            dst, sem = inner_in.at[k, span], inner_recv.at[k, a]
        else:
            dst, sem = end_in.at[span], end_recv.at[a]
        return send(
            part.at[owner, span], dst, line_send.at[k, a], sem,
            outer_peer if to == "end" else inner_peer, mode,
        )

    def keep(k):
        owner = owner_of(k, y, x)
        for a in (1, 0):
            firsts[a, k, 1].wait_recv()
            seconds[a, k].wait_recv()
            span = spans[a]
            value = f32(part[owner, span]) + f32(first_in[a, k, 1]) + f32(second_in[a, k])
            if k >= 2:
                @pl.when(is_mid if k == 2 else is_end)
                def _():
                    total[span, :] = value
            part[owner, span] = value.astype(jnp.bfloat16)
            if k < 3:
                @pl.when(is_end)
                def _():
                    line_copy(k, a, "outer").start()
            else:
                pass_on(k, a)

    def pass_on(k, a):
        owner = owner_of(k, y, x)
        span = spans[a]

        @pl.when(is_mid)
        def _():
            if k < 2:
                line_copy(k, a, "outer").wait_recv()
                arrived = outer_in[k, span]
            else:
                line_copy(0, a, "inner").wait_recv()
                arrived = inner_in[0, span]
            part[owner, span] = (f32(part[owner, span]) + f32(arrived)).astype(jnp.bfloat16)
            line_copy(k, a, "inner" if k < 2 else "end").start()

    def line_end(a):
        span = spans[a]

        @pl.when(is_mid)
        def _():
            line_copy(2, a, "outer").wait_recv()
            line_copy(1, a, "inner").wait_recv()
            total[span, :] = total[span, :] + f32(outer_in[2, span]) + f32(inner_in[1, span])

        @pl.when(is_end)
        def _():
            line_copy(3, a, "end").wait_recv()
            total[span, :] = total[span, :] + f32(end_in[span])

    def last_copy(k, to):
        owners = pl.ds(chunk_z(k) * 4, 4)
        if to == "outer":
            dst, sem = last_outer_in.at[k], last_outer_recv.at[k]
        elif to == "inner":
            dst, sem = last_inner_in.at[k], last_inner_recv.at[k]
        else:
            dst, sem = last_end_in, last_end_recv
        return send(
            part.at[owners, last], dst, last_send.at[k], sem,
            outer_peer if to == "end" else inner_peer, mode,
        )

    def last_begin(k):
        @pl.when(is_end)
        def _():
            last_copy(k, "outer").start()

    def last_add(k, terms):
        first = chunk_z(k) * 4
        for i in range(4):
            value = f32(part[first + i, last])
            for term in terms:
                value = value + f32(term[i])
            part[first + i, last] = value.astype(jnp.bfloat16)

    def last_pass(k):
        @pl.when(is_mid)
        def _():
            if k < 2:
                last_copy(k, "outer").wait_recv()
                last_add(k, [last_outer_in.at[k]])
                last_copy(k, "inner").start()
            else:
                last_copy(0, "inner").wait_recv()
                last_add(k, [last_inner_in.at[0]])
                last_copy(k, "end").start()

    def last_first_copy(axis, j):
        if axis == 0:
            owner = z * 4 + (1 - y if j == 0 else y) * 2 + 1 - x
        else:
            owner = z * 4 + (1 - y) * 2 + (1 - x if j == 0 else x)
        return send(
            part.at[owner, last_spans[axis]], last_first_in.at[axis, j],
            last_first_send.at[axis, j], last_first_recv.at[axis, j],
            x_peer if axis == 0 else y_peer, mode,
        )

    def last_second_owner(axis):
        return z * 4 + (1 - y) * 2 + x if axis == 0 else z * 4 + y * 2 + 1 - x

    def last_second_copy(axis):
        return send(
            part.at[last_second_owner(axis), last_spans[axis]], last_second_in.at[axis],
            last_second_send.at[axis], last_second_recv.at[axis],
            y_peer if axis == 0 else x_peer, mode,
        )

    last_firsts = {(a, j): last_first_copy(a, j) for a in range(2) for j in range(2)}
    last_seconds = [last_second_copy(a) for a in range(2)]

    def last_spread():
        @pl.when(is_mid)
        def _():
            last_copy(2, "outer").wait_recv()
            last_copy(1, "inner").wait_recv()
            last_add(2, [last_outer_in.at[2], last_inner_in.at[1]])

        @pl.when(is_end)
        def _():
            last_copy(3, "end").wait_recv()
            last_add(3, [last_end_in])

        for j in range(2):
            for a in range(2):
                last_firsts[a, j].start()

    def last_forward():
        for a in range(2):
            last_firsts[a, 0].wait_recv()
            owner = last_second_owner(a)
            part[owner, last_spans[a]] = (
                f32(part[owner, last_spans[a]]) + f32(last_first_in[a, 0])
            ).astype(jnp.bfloat16)
            last_seconds[a].start()

    def last_keep():
        for a in range(2):
            last_firsts[a, 1].wait_recv()
            last_seconds[a].wait_recv()
            total[last_spans[a], :] = (
                f32(part[pix, last_spans[a]]) + f32(last_first_in[a, 1]) + f32(last_second_in[a])
            )

    ring = pix % 4 * 4 + z

    def chip_at(step):
        there = (ring + step) % 16
        return there % 4 * 4 + there // 4

    def cross_copy(at, size, index):
        rows_at = pl.ds(at, size)
        return send(
            cross_out.at[rows_at], cross_in.at[rows_at],
            cross_send.at[index], cross_recv.at[index], pix, 1 - mode,
        )

    cross_rows = [(FAR, FAR + 1), (4, FAR), (1, 4)]
    crosses = [
        cross_copy((first - 1) * GROUP, (end - first) * GROUP, i)
        for i, (first, end) in enumerate(cross_rows)
    ]

    def start_cross(i):
        first, end = cross_rows[i]
        cross_out[(first - 1) * GROUP:(end - 1) * GROUP] = total[
            first * GROUP:end * GROUP, 128:256
        ].astype(jnp.bfloat16)
        crosses[i].start()

    def mirror(i):
        crosses[i].wait_recv()
        for d in range(*cross_rows[i]):
            start_turn(d)

    shared_copy = send(
        shared_out, shared_in, shared_send, shared_recv,
        y_peer, jnp.where(y == 0, mode, 1 - mode),
    )
    turns = [
        send(
            turn_out.at[d - 1], turn_in.at[d - 1], turn_send.at[d - 1], turn_recv.at[d - 1],
            chip_at(d), mode,
        )
        for d in range(1, FAR + 1)
    ]

    def start_turn(d):
        stacked = jnp.concatenate(
            [
                total[d * GROUP:(d + 1) * GROUP, 0:128].astype(jnp.bfloat16),
                cross_in[(d - 1) * GROUP:d * GROUP, :],
            ],
            axis=0,
        )
        turn_out[d - 1] = stacked.T
        turns[d - 1].start()

    for k in range(3):
        multiply(k)
        last_begin(k)
    positions = pix * pixel_rows + lax.broadcasted_iota(
        jnp.int32, (pixels_ref.shape[1], pixel_rows), 1
    )
    listing.wait()
    listed = jnp.broadcast_to(pixels_ref[...], (8, pixels_ref.shape[1])).T[:, 0:1]
    counts = jnp.sum(
        jnp.where(listed == positions, 1.0, 0.0), axis=0, keepdims=True
    )
    nothing = jnp.zeros_like(counts)
    row = lax.broadcasted_iota(jnp.int32, (16, 2 * pixel_rows), 0)
    real_weight = jnp.concatenate([counts, nothing], axis=1)
    imag_weight = jnp.concatenate([nothing, counts], axis=1)
    weight = jnp.where(row == 0, real_weight, jnp.where(row == 1, imag_weight, 0.0))
    weight = weight.astype(jnp.bfloat16)
    for pair in range(8):
        places = [(p % 4 * 4 + p // 4) * GROUP for p in (2 * pair, 2 * pair + 1)]
        block = jnp.concatenate([own[pl.ds(at, GROUP), :] for at in places], axis=0)
        ref_out[0, :, pl.ds(pair * 128, 128)] = lax.dot_general(
            weight, block, contract, preferred_element_type=jnp.float32
        )[0:8]
    ref_copies[0].start()
    forward(0)
    multiply(3)
    ref_next(0)
    last_pass(0)
    forward(1)
    start_first(3)
    last_pass(1)
    ref_next(1)
    keep(0)
    forward(2)
    last_pass(3)
    ref_next(2)
    last_spread()
    keep(1)
    pass_on(0, 1)
    pass_on(0, 0)
    ref_next(3)
    forward(3)
    last_forward()
    keep(2)
    pass_on(1, 1)
    pass_on(1, 0)
    last_keep()
    start_cross(0)
    shared = jnp.concatenate(
        [total[top:top + PACK, 0:128], total[top:top + PACK, 128:256]], axis=0
    )
    shared_out[...] = jnp.concatenate([shared, shared], axis=0).astype(jnp.bfloat16).T
    shared_copy.start()
    keep(3)
    mirror(0)
    line_end(1)
    start_cross(1)

    lane = lax.broadcasted_iota(jnp.int32, (GROUP, 128), 1)
    low = lane < GROUP

    def group_rows(step):
        return pl.ds(pl.multiple_of(chip_at(step) * GROUP, GROUP), GROUP)

    def place(d):
        here = total[d * GROUP:(d + 1) * GROUP, 0:128]
        there = total[d * GROUP:(d + 1) * GROUP, 128:256]
        gram_ref[0, group_rows(d), :] = jnp.where(low, here, pltpu.roll(there, GROUP, 1))
        gram_ref[1, group_rows(d), :] = jnp.where(low, pltpu.roll(here, GROUP, 1), there)

    mirror(1)
    line_end(0)
    start_cross(2)
    for d in range(NEAR - 1):
        place(d)
    mirror(2)
    shared_copy.wait_recv()
    arrived = f32(shared_in[...])
    mine = low == (y == 0)
    shared = jnp.concatenate(
        [total[top:top + PACK, 0:128], total[top:top + PACK, 128:256]], axis=0
    )
    rolled = pltpu.roll(shared, GROUP, 1)
    gram_ref[0, group_rows(8), :] = jnp.where(
        mine, jnp.where(low, shared, rolled), arrived[0:GROUP]
    )
    gram_ref[1, group_rows(8), :] = jnp.where(
        mine, jnp.where(low, rolled, shared), -arrived[GROUP:]
    )
    ref_copies[4].wait_recv()
    sums_ref[0] = ref_out[4]
    sums_ref[1] = ref_in[4]
    for d in range(1, FAR + 1):
        turns[d - 1].wait_recv()
        arrived = f32(turn_in[d - 1])
        gram_ref[0, group_rows(16 - d), :] = arrived[0:GROUP]
        gram_ref[1, group_rows(16 - d), :] = -arrived[GROUP:]

    for copy in field_copies + ref_copies + list(firsts.values()) + list(seconds.values()):
        copy.wait_send()
    for copy in turns + crosses + [shared_copy] + list(last_firsts.values()) + last_seconds:
        copy.wait_send()
    for k in range(3):
        @pl.when(is_end | (k < 2))
        def _():
            line_copy(k, 0, "outer").wait_send()
            line_copy(k, 1, "outer").wait_send()
            last_copy(k, "outer").wait_send()

    @pl.when(is_mid)
    def _():
        line_copy(3, 0, "end").wait_send()
        line_copy(3, 1, "end").wait_send()
        last_copy(3, "end").wait_send()


def finish_kernel(pixel_scale, gram_ref, sums_ref, band_ref, diag_ref):
    pix = lax.axis_index("pix")
    odd = pix % 2 == 1
    at = pl.multiple_of((pix // 2) * 128, 128)
    own = sums_ref[0, :, pl.ds(at, 128)]
    other = sums_ref[1, :, pl.ds(at, 128)]
    low = lax.broadcasted_iota(jnp.int32, own.shape, 1) < GROUP
    own = jnp.where(odd, pltpu.roll(own, GROUP, 1), own)
    other = jnp.where(odd, other, pltpu.roll(other, GROUP, 1))
    cols = jnp.where(low, own, other).T

    def unit(real, imag):
        magnitude = jnp.maximum(jnp.sqrt(real * real + imag * imag), 1.0)
        return real / magnitude, imag / magnitude

    col_real, col_imag = unit(cols[:, 0:1], cols[:, 1:2])
    row_real, row_imag = unit(sums_ref[0, 0:1, :], sums_ref[0, 1:2, :])
    unit_real = row_real * col_real + row_imag * col_imag
    unit_imag = row_imag * col_real - row_real * col_imag
    gram_real = gram_ref[0].T
    gram_imag = gram_ref[1].T
    real = (unit_real * gram_real - unit_imag * gram_imag) * pixel_scale
    imag = (unit_real * gram_imag + unit_imag * gram_real) * pixel_scale
    diag_ref[0] = real[:GROUP]
    diag_ref[1] = imag[:GROUP]
    band_ref[0] = real[GROUP:]
    band_ref[1] = imag[GROUP:]


def paired_shards(frames, ref_pixels):
    pixel_rows = frames.shape[1]
    width = frames.shape[2]
    rows = 2 * SIDE + LAST
    b16 = jnp.bfloat16
    dma = pltpu.SemaphoreType.DMA
    gram, sums = pl.pallas_call(
        gram_kernel,
        out_shape=(
            jax.ShapeDtypeStruct((2, width, 128), jnp.float32),
            jax.ShapeDtypeStruct((2, 8, width), jnp.float32),
        ),
        in_specs=[
            pl.BlockSpec(memory_space=pltpu.HBM),
            pl.BlockSpec(memory_space=pltpu.HBM),
        ],
        out_specs=(pl.BlockSpec(memory_space=pltpu.VMEM),) * 2,
        scratch_shapes=[
            pltpu.VMEM((1, ref_pixels.shape[0]), jnp.int32),
            pltpu.VMEM((4, 4, pixel_rows, 4 * GROUP), b16),
            pltpu.VMEM((width + 8 * GROUP, 2 * pixel_rows), b16),
            pltpu.VMEM((width, 2 * pixel_rows), b16),
            pltpu.VMEM((16, rows, 256), b16),
            pltpu.VMEM((2, 4, 2, SIDE, 256), b16),
            pltpu.VMEM((2, 4, SIDE, 256), b16),
            pltpu.VMEM((3, 2 * SIDE, 256), b16),
            pltpu.VMEM((2, 2 * SIDE, 256), b16),
            pltpu.VMEM((2 * SIDE, 256), b16),
            pltpu.VMEM((3, 4, LAST, 256), b16),
            pltpu.VMEM((2, 4, LAST, 256), b16),
            pltpu.VMEM((4, LAST, 256), b16),
            pltpu.VMEM((2, 2, LAST // 2, 256), b16),
            pltpu.VMEM((2, LAST // 2, 256), b16),
            pltpu.VMEM((5, 8, width), jnp.float32),
            pltpu.VMEM((5, 8, width), jnp.float32),
            pltpu.VMEM((rows, 256), jnp.float32),
            pltpu.VMEM((FAR * GROUP, 128), b16),
            pltpu.VMEM((FAR * GROUP, 128), b16),
            pltpu.VMEM((FAR, 128, 128), b16),
            pltpu.VMEM((FAR, 128, 128), b16),
            pltpu.VMEM((128, 128), b16),
            pltpu.VMEM((128, 128), b16),
            dma, dma((4,)), dma((4, 4)), dma((4, 4)),
            dma((2, 4, 2)), dma((2, 4, 2)),
            dma((2, 4)), dma((2, 4)),
            dma((4, 2)), dma((3, 2)), dma((2, 2)), dma((2,)),
            dma((4,)), dma((3,)), dma((2,)), dma,
            dma((2, 2)), dma((2, 2)), dma((2,)), dma((2,)),
            dma((5,)), dma((5,)),
            dma((3,)), dma((3,)),
            dma((FAR,)), dma((FAR,)),
            dma, dma,
        ],
        compiler_params=pltpu.CompilerParams(
            collective_id=0, has_side_effects=True, vmem_limit_bytes=52 * 1024 * 1024
        ),
    )(frames, ref_pixels.reshape(1, -1))
    pixel_scale = 1.0 / math.sqrt(lax.axis_size("pix") * pixel_rows)
    band, diag = pl.pallas_call(
        functools.partial(finish_kernel, pixel_scale),
        out_shape=(jax.ShapeDtypeStruct((2, GROUP, width), jnp.float32),) * 2,
        in_specs=[pl.BlockSpec(memory_space=pltpu.VMEM)] * 2,
        out_specs=(pl.BlockSpec(memory_space=pltpu.VMEM),) * 2,
        compiler_params=pltpu.CompilerParams(vmem_limit_bytes=16 * 1024 * 1024),
    )(gram, sums)
    return (jnp.swapaxes(band, 1, 2), jnp.swapaxes(diag, 1, 2))


def solution(mesh):
    placed = (P(None, "pix", "mode"), P())
    paired = mesh.shape["pix"] == 16 and mesh.shape["mode"] == 2

    def body(frames, ref_pixels):
        if paired and frames.shape[2] == 16 * GROUP:
            return paired_shards(frames, ref_pixels)
        return shards(frames, ref_pixels)

    return jax.shard_map(
        body,
        mesh=mesh,
        in_specs=placed,
        out_specs=(P(None, "mode", "pix"), P(None, "mode", "pix")),
        check_vma=False,
    )
```
